128 devices in a mesh: occ: 4 (over z_hi, core), vir: 32 (over x, z_lo, y).
Axes of the slice: x: 4, y: 4, z: 4 (z_hi: 2, z_lo: 2; z = z_hi * 2 + z_lo), core: 2. Of those that a mesh axis runs over, the one named last changes fastest.
Arguments:
- cholesky: bfloat16 [256, 256, 128], P(None, 'vir'), may hold values from -6 to 6
- amplitudes: bfloat16 [256, 8, 128, 128], P('occ'), may hold values from -0.0029296875 to 0.0029296875
- mirror: int32 [256], P('occ'), may hold values from 0 to 63, as said below
Outputs:
- residual: float32 [256, 256, 32], P('occ', 'vir')
The draws below stay inside these ranges and needn't reach their ends.
Inputs may be any that keep to these rules, and one draw needn't show every extreme that they name: Pair rows on each occ device are sorted by class, 8 of each class. mirror[r] on occ device p is a row of occ device p XOR 1 within the same class block, and the mirror of that row is r.
All inputs are finite; a program needn't handle non-finite values.
Results may differ from the reference program's by a relative error of at most 0.0029.
Values may be sent and summed in bfloat16 or wider, within the bound.
No kernel may reach another device: no remote copies, remote signals or barrier semaphores. Data moves between devices by JAX's collectives and lax.ppermute only.
A program may use at most 256 MiB of HBM per device.

```python
import jax
import jax.numpy as jnp
import numpy as np
from jax import lax

NB = 128
IRREPS = 8
NL = 256
A_DEV = 8
CLS = 8
NA = 256
IJ_DEV = 64
IJ = 256
N_VIR = 32


def draw_mirror(key, part):
    key = jax.random.fold_in(key, 11)
    pair_devices = IJ // IJ_DEV // 2
    sub_keys = jax.random.split(key, pair_devices * IRREPS)
    orders = jax.vmap(lambda one_key: jax.random.permutation(one_key, CLS))(sub_keys).reshape(pair_devices, IRREPS, CLS)
    inverse = jnp.argsort(orders, axis=-1)
    offsets = (jnp.arange(IRREPS) * CLS)[None, :, None]
    even_rows = (orders + offsets).reshape(pair_devices, IJ_DEV)
    odd_rows = (inverse + offsets).reshape(pair_devices, IJ_DEV)
    return jnp.stack([even_rows, odd_rows], axis=1).reshape(IJ).astype(jnp.int32)


def levels(own_key, extent, cuts, smallest, largest):
    factor_of, own = 1.0, jax.random.fold_in(own_key, 6)
    for dim, parts in cuts:
        steps = jnp.exp(jax.random.uniform(jax.random.fold_in(own, dim), (parts,), jnp.float32, smallest / len(cuts), largest / len(cuts)))
        factor_of = factor_of * jnp.repeat(steps, extent[dim] // parts).reshape([-1 if axis == dim else 1 for axis in range(len(extent))])
    return factor_of


def normal_values(stream_key, extent, deviation, reach, pieces=(), kind=jnp.bfloat16):
    drawn = jax.random.normal(stream_key, extent, jnp.float32) * deviation
    if len(pieces) > 0:
        drawn = levels(stream_key, extent, pieces, -0.22, 0.18) * drawn
    return jnp.clip(drawn, min=-reach, max=reach).astype(kind)


def setup_inputs(seed: int = 0) -> dict:
    streams_of = jax.random.split(jax.random.key(seed), 4)
    cholesky = normal_values(streams_of[0], (NL, NA, NB), 1.0, 6.0, ((1, 32),))
    amplitudes = normal_values(streams_of[1], (IJ, IRREPS, NB, NB), (NB * NB * NL) ** -0.5, 0.0029296875, ((0, 4),))
    mirror = draw_mirror(jax.random.fold_in(streams_of[3], 71), 0)
    return dict(cholesky=cholesky, amplitudes=amplitudes, mirror=mirror)


def class_rows(occ_count, per_occ, pair_class):
    starts = np.arange(occ_count)[:, None] * per_occ + pair_class * CLS
    return (starts + np.arange(CLS)[None, :]).reshape(-1)


def reference(cholesky, amplitudes, mirror):
    all_rows = amplitudes.shape[0]
    window = A_DEV * (N_VIR // IRREPS)
    per_occ = IRREPS * CLS
    occ_count = all_rows // per_occ
    device = np.arange(all_rows) // per_occ
    partner = jnp.asarray((device ^ 1) * per_occ).astype(jnp.int32) + mirror.astype(jnp.int32)
    chol_f32 = cholesky.astype(jnp.float32)
    result = jnp.zeros((all_rows, IRREPS * window, window), jnp.float32)
    for irrep_one in range(IRREPS):
        left_rows = chol_f32[:, irrep_one * window:(irrep_one + 1) * window, :]
        for irrep_two in range(IRREPS):
            chosen = class_rows(occ_count, per_occ, irrep_one ^ irrep_two)
            right_rows = chol_f32[:, irrep_two * window:(irrep_two + 1) * window, :]
            v_slab = jnp.einsum("lac,lbd->abcd", left_rows, right_rows).astype(jnp.bfloat16)
            v_slab = lax.optimization_barrier(v_slab).astype(jnp.float32)
            amp_tiles = amplitudes[chosen, irrep_one].astype(jnp.float32)
            contrib = jnp.einsum("abcd,kcd->kab", v_slab, amp_tiles)
            result = result.at[chosen, irrep_one * window:(irrep_one + 1) * window, :].set(contrib)
    mirrored = jnp.take(result, partner, axis=0)
    symmetric = result
    for irrep_one in range(IRREPS):
        for irrep_two in range(IRREPS):
            chosen = class_rows(occ_count, per_occ, irrep_one ^ irrep_two)
            other = mirrored[chosen, irrep_two * window:(irrep_two + 1) * window, :]
            symmetric = symmetric.at[chosen, irrep_one * window:(irrep_one + 1) * window, :].add(jnp.transpose(other, (0, 2, 1)))
    return symmetric
```

```python
import functools

import jax
import jax.numpy as jnp
from jax import lax
from jax.experimental import pallas as pl
from jax.experimental.pallas import tpu as pltpu
from jax.sharding import PartitionSpec as P

IRREPS = 8
CLS = 8
NT = (((1,), (1,)), ((), ()))
BF16 = jnp.bfloat16
F32 = jnp.float32


def permute(value, move):
    pairs = []
    for occ in range(4):
        for vir in range(32):
            to_occ, to_vir = move(occ, vir)
            pairs.append((occ * 32 + vir, to_occ * 32 + to_vir))
    return lax.ppermute(value, ("occ", "vir"), pairs)


def over_y(value, k):
    return permute(value, lambda occ, vir: (occ, vir ^ k))


def over_x(value, k):
    return permute(value, lambda occ, vir: (occ, vir ^ (8 * k)))


def over_z(value):
    return permute(value, lambda occ, vir: (occ ^ (2 if occ & 1 else 0), vir ^ 4))


def to_sibling(value):
    return permute(value, lambda occ, vir: (occ ^ 1, vir))


def fill_positions(odd, mirror_ref, rows_ref):
    def step(i, _):
        rows_ref[jnp.where(odd == 1, mirror_ref[i], i)] = i
        return 0

    lax.fori_loop(0, IRREPS * CLS, step, 0)


def spec(space):
    return pl.BlockSpec(memory_space=space)


def pack_kernel(place_ref, mirror_ref, amp_ref, out_ref, rows_ref, sem):
    h = place_ref[0]
    fill_positions(place_ref[2], mirror_ref, rows_ref)

    def step(i, _):
        pltpu.make_async_copy(amp_ref.at[rows_ref[i], h ^ (i // CLS)], out_ref.at[i], sem).start()
        return 0

    lax.fori_loop(0, IRREPS * CLS, step, 0)
    pltpu.make_async_copy(out_ref, out_ref, sem).wait()


def pack_tiles(place, mirror, amplitudes):
    return pl.pallas_call(
        pack_kernel,
        out_shape=jax.ShapeDtypeStruct((IRREPS * CLS, 128, 128), BF16),
        in_specs=[spec(pltpu.SMEM), spec(pltpu.SMEM), spec(pl.ANY)],
        out_specs=spec(pl.ANY),
        scratch_shapes=[pltpu.SMEM((IRREPS * CLS,), jnp.int32), pltpu.SemaphoreType.DMA],
        name="pack_tiles",
    )(place, mirror, amplitudes)


def rows_kernel(place_ref, r0_ref, r1_ref, r2_ref, r3_ref, mine_ref, other_ref, all_ref):
    y, core = place_ref[1], place_ref[2]
    for k, ref in enumerate((r0_ref, r1_ref, r2_ref, r3_ref)):
        all_ref[k] = ref[...]
    for half, out_ref in enumerate((mine_ref, other_ref)):
        base = (half ^ core) * 256

        def step(i, _):
            parts = []
            for q in range(4):
                start = pl.multiple_of(base + i * 16, 16)
                parts.append(all_ref[q ^ y, pl.ds(start, 16), :].astype(F32))
            both = [p[0:8] for p in parts] + [p[8:16] for p in parts]
            out_ref[pl.ds(pl.multiple_of(i * 64, 64), 64), :] = jnp.concatenate(both, axis=0).astype(BF16)
            return 0

        lax.fori_loop(0, 16, step, 0, unroll=4)


def order_rows(place, quarters):
    half = jax.ShapeDtypeStruct((1024, 128), BF16)
    return pl.pallas_call(
        rows_kernel,
        out_shape=(half, half),
        in_specs=[spec(pltpu.SMEM)] + [spec(pltpu.VMEM)] * 4,
        out_specs=(spec(pltpu.VMEM), spec(pltpu.VMEM)),
        scratch_shapes=[pltpu.VMEM((4, 512, 128), BF16)],
        name="order_rows",
    )(place, *quarters)


CHUNK = 16


def ladder_kernel(classes, carried, *refs):
    n = len(classes)
    place_ref, mirror_ref, amp_ref, tp_ref, mine_ref, other_ref = refs[:6]
    refs = refs[6:]
    peers, refs = refs[: 2 * n], refs[2 * n :]
    if carried:
        carry_ref, refs = refs[0], refs[1:]
    out_ref, rows_ref, own_s, b_s, t_s, tp_s, w_s, r_s, own_sem, b_sem, t_sem, tp_sem = refs
    h, y = place_ref[0], place_ref[1]
    fill_positions(place_ref[2], mirror_ref, rows_ref)

    own = [
        pltpu.make_async_copy(mine_ref, own_s.at[0], own_sem.at[0]),
        pltpu.make_async_copy(other_ref, own_s.at[1], own_sem.at[1]),
    ]
    for i, g in enumerate(classes):
        def tile(j, _):
            pltpu.make_async_copy(amp_ref.at[rows_ref[g * CLS + j], h], t_s.at[i, j], t_sem.at[i]).start()
            return 0

        lax.fori_loop(0, CLS, tile, 0)
        pltpu.make_async_copy(tp_ref.at[pl.ds(g * CLS, CLS)], tp_s.at[i], tp_sem.at[i]).start()
        if i == 0:
            for copy in own:
                copy.start()
        for half in range(2):
            pltpu.make_async_copy(peers[2 * i + half], b_s.at[i, half], b_sem.at[i, half]).start()
    for copy in own:
        copy.wait()

    rows = CHUNK * 32

    def one_class(i, _):
        pltpu.make_async_copy(t_s.at[i], t_s.at[i], t_sem.at[i]).wait()
        pltpu.make_async_copy(tp_s.at[i], tp_s.at[i], tp_sem.at[i]).wait()
        for half in range(2):
            pltpu.make_async_copy(b_s.at[i, half], b_s.at[i, half], b_sem.at[i, half]).wait()
        for j in range(CLS):
            w_s[0:128, j * 128 : (j + 1) * 128] = t_s[i, j]
            w_s[128:256, j * 128 : (j + 1) * 128] = tp_s[i, j].T
        r_s[i] = jnp.zeros((256, 32), F32)

        def chunk(n_chunk, _):
            half = n_chunk // (32 // CHUNK)
            start = pl.multiple_of((n_chunk % (32 // CHUNK)) * rows, rows)
            own_rows = own_s[half, pl.ds(start, rows), :]
            lhs = jnp.concatenate([own_rows, own_rows], axis=1)
            x = jnp.dot(lhs, w_s[...], preferred_element_type=F32).astype(BF16)
            b = b_s[i, half, pl.ds(start, rows), :]
            x2 = jnp.concatenate(
                [
                    jnp.concatenate(
                        [x[l * 32 : (l + 1) * 32, j * 128 : (j + 1) * 128] for l in range(CHUNK)], axis=1
                    )
                    for j in range(CLS)
                ],
                axis=0,
            )
            bt = jnp.concatenate([b[l * 32 : (l + 1) * 32] for l in range(CHUNK)], axis=1)
            r_s[i] += lax.dot_general(x2, bt, NT, preferred_element_type=F32)
            return 0

        lax.fori_loop(0, 64 // CHUNK, chunk, 0)
        return 0

    lax.fori_loop(0, n, one_class, 0)
    for q in range(4):
        blocks = []
        for i in range(n):
            r = r_s[i]
            blocks.append(
                jnp.concatenate([r[j * 32 + q * 8 : j * 32 + q * 8 + 8] for j in range(CLS)], axis=0)
            )
        if carried:
            blocks = [carry_ref[q ^ y]] + blocks
        out_ref[q ^ y] = jnp.concatenate(blocks, axis=1) if len(blocks) > 1 else blocks[0]


def ladder(classes, place, mirror, amplitudes, received, own, peers, carry=None):
    n = len(classes)
    lanes = 32 * (n + (carry is not None))
    operands = [place, mirror, amplitudes, received, *own, *[half for peer in peers for half in peer]]
    in_specs = [spec(pltpu.SMEM)] * 2 + [spec(pl.ANY)] * (len(operands) - 2)
    if carry is not None:
        operands.append(carry)
        in_specs.append(spec(pltpu.VMEM))
    return pl.pallas_call(
        functools.partial(ladder_kernel, classes, carry is not None),
        out_shape=jax.ShapeDtypeStruct((4, 64, lanes), F32),
        in_specs=in_specs,
        out_specs=spec(pltpu.VMEM),
        scratch_shapes=[
            pltpu.SMEM((IRREPS * CLS,), jnp.int32),
            pltpu.VMEM((2, 1024, 128), BF16),
            pltpu.VMEM((n, 2, 1024, 128), BF16),
            pltpu.VMEM((n, CLS, 128, 128), BF16),
            pltpu.VMEM((n, CLS, 128, 128), BF16),
            pltpu.VMEM((256, 1024), BF16),
            pltpu.VMEM((n, 256, 32), F32),
            pltpu.SemaphoreType.DMA((2,)),
            pltpu.SemaphoreType.DMA((n, 2)),
            pltpu.SemaphoreType.DMA((n,)),
            pltpu.SemaphoreType.DMA((n,)),
        ],
        compiler_params=pltpu.CompilerParams(vmem_limit_bytes=40 * 2**20),
        cost_estimate=pl.CostEstimate(
            flops=n * 2**31, transcendentals=0, bytes_accessed=n * 2**20
        ),
        name="ladder_" + "_".join(str(g) for g in classes),
    )(*operands)


def finish_kernel(orders, place_ref, mirror_ref, *refs):
    parts, out_ref, rows_ref = refs[:-2], refs[-2], refs[-1]
    fill_positions(place_ref[2], mirror_ref, rows_ref)
    for n, order in enumerate(orders):
        own, rest = parts[4 * n], parts[4 * n + 1 : 4 * n + 4]
        total = own[0]
        for ref in rest:
            total = total + ref[...]
        for lane, g in enumerate(order):
            for j in range(CLS):
                out_ref[rows_ref[g * CLS + j]] = total[j * 8 : (j + 1) * 8, lane * 32 : (lane + 1) * 32]


def finish(orders, place, mirror, parts):
    return pl.pallas_call(
        functools.partial(finish_kernel, orders),
        out_shape=jax.ShapeDtypeStruct((64, 8, 32), F32),
        in_specs=[spec(pltpu.SMEM)] * 2 + [spec(pltpu.VMEM)] * len(parts),
        out_specs=spec(pltpu.VMEM),
        scratch_shapes=[pltpu.SMEM((IRREPS * CLS,), jnp.int32)],
        name="finish",
    )(place, mirror, *parts)


def shards(cholesky, amplitudes, mirror):
    vir = lax.axis_index("vir")
    core = lax.axis_index("occ") % 2
    h, y = vir // 4, vir % 4
    place = jnp.stack([h, y, core]).astype(jnp.int32)

    by_chunk = cholesky.reshape(4, 512, 128)
    quarters = [lax.dynamic_index_in_dim(by_chunk, y, 0, keepdims=False)]
    for k in range(1, 4):
        quarters.append(over_y(lax.dynamic_index_in_dim(by_chunk, y ^ k, 0, keepdims=False), k))
    received = to_sibling(pack_tiles(place, mirror, amplitudes))
    mine, other = order_rows(place, quarters)

    halves = {0: (mine, other)}
    direct = {1: over_z(mine), 2: over_x(mine, 1), 4: over_x(mine, 2), 6: over_x(mine, 3)}
    for g in (2, 4, 6):
        direct[g + 1] = over_z(direct[g])
    for g in range(1, 8):
        halves[g] = (direct[g], to_sibling(direct[g]))

    def run(classes, carry=None):
        return ladder(
            classes, place, mirror, amplitudes, received, halves[0], [halves[g] for g in classes], carry
        )

    first = run((0,))
    near = run((1, 2, 4, 6))
    far = run((3, 5, 7), first)
    parts = []
    for block in (near, far):
        parts.append(block)
        for k in range(1, 4):
            parts.append(over_y(block[k], k))
    return finish(((1, 2, 4, 6), (0, 3, 5, 7)), place, mirror, parts)


def solution(mesh):
    placed = (P(None, "vir", None), P("occ", None, None, None), P("occ"))
    return jax.shard_map(
        shards, mesh=mesh, in_specs=placed, out_specs=P("occ", "vir", None), check_vma=False
    )
```

```python
import functools

import jax
import jax.numpy as jnp
from jax import lax
from jax.experimental import pallas as pl
from jax.experimental.pallas import tpu as pltpu
from jax.sharding import PartitionSpec as P

IRREPS = 8
CLS = 8
ROWS = IRREPS * CLS
NT = (((1,), (1,)), ((), ()))
TN = (((0,), (0,)), ((), ()))
BF16 = jnp.bfloat16
F32 = jnp.float32
MIB = 2**20


def permute(value, move):
    pairs = []
    for occ in range(4):
        for vir in range(32):
            to_occ, to_vir = move(occ, vir)
            pairs.append((occ * 32 + vir, to_occ * 32 + to_vir))
    return lax.ppermute(value, ("occ", "vir"), pairs)


def over_y(value, k):
    return permute(value, lambda occ, vir: (occ, vir ^ k))


def over_x(value, even, odd):
    return permute(value, lambda occ, vir: (occ, vir ^ (8 * (odd if occ & 1 else even))))


def over_z(value):
    return permute(value, lambda occ, vir: (occ ^ (2 if occ & 1 else 0), vir ^ 4))


def to_sibling(value):
    return permute(value, lambda occ, vir: (occ ^ 1, vir))


def spec(space):
    return pl.BlockSpec(memory_space=space)


def params(mib):
    return pltpu.CompilerParams(vmem_limit_bytes=mib * MIB)


def place():
    vir, core = lax.axis_index("vir"), lax.axis_index("occ") & 1
    return lax.shift_right_logical(vir, 2), vir & 3, core


def fill_positions(core, mirror_ref, rows_ref):
    def step(i, _):
        rows_ref[jnp.where(core == 1, mirror_ref[i], i)] = i
        return 0

    lax.fori_loop(0, ROWS, step, 0, unroll=8)


def pack_kernel(mirror_ref, amp_ref, out_ref, rows_ref, tiles, sems):
    h, _, core = place()
    fill_positions(core, mirror_ref, rows_ref)
    for g in range(IRREPS):
        for j in range(CLS):
            source = amp_ref.at[rows_ref[g * CLS + j], h ^ g]
            pltpu.make_async_copy(source, tiles.at[g, j], sems.at[g]).start()

    def one_class(g, _):
        pltpu.make_async_copy(tiles.at[g], tiles.at[g], sems.at[g]).wait()
        for j in range(CLS):
            out_ref[g, :, j * 128 : (j + 1) * 128] = tiles[g, j].T
        return 0

    lax.fori_loop(0, IRREPS, one_class, 0)


def pack_tiles(mirror, amplitudes):
    return pl.pallas_call(
        pack_kernel,
        out_shape=jax.ShapeDtypeStruct((IRREPS, 128, CLS * 128), BF16),
        in_specs=[spec(pltpu.SMEM), spec(pl.ANY)],
        out_specs=spec(pltpu.VMEM),
        scratch_shapes=[
            pltpu.SMEM((ROWS,), jnp.int32),
            pltpu.VMEM((IRREPS, CLS, 128, 128), BF16),
            pltpu.SemaphoreType.DMA((IRREPS,)),
        ],
        compiler_params=params(8),
        name="pack_tiles",
    )(mirror, amplitudes)


def rows_kernel(quarters_ref, all_ref, mine_ref):
    core = place()[2]

    def step(i, _):
        start = pl.multiple_of(i * 16, 16)
        parts = [quarters_ref[q, pl.ds(start, 16), :].astype(F32) for q in range(4)]
        both = [p[0:8] for p in parts] + [p[8:16] for p in parts]
        all_ref[pl.ds(pl.multiple_of(i * 64, 64), 64), :] = jnp.concatenate(both, axis=0).astype(BF16)
        return 0

    lax.fori_loop(0, 32, step, 0, unroll=8)
    mine_ref[...] = all_ref[pl.ds(pl.multiple_of(core * 1024, 1024), 1024), :]


def order_rows(quarters):
    return pl.pallas_call(
        rows_kernel,
        out_shape=(jax.ShapeDtypeStruct((2048, 128), BF16), jax.ShapeDtypeStruct((1024, 128), BF16)),
        in_specs=[spec(pltpu.VMEM)],
        out_specs=(spec(pltpu.VMEM), spec(pltpu.VMEM)),
        compiler_params=params(6),
        name="order_rows",
    )(quarters)


def ladder_kernel(classes, blocks, carried, *refs):
    n = len(classes)
    mirror_ref, amp_ref, tp_ref, own_ref = refs[:4]
    refs = refs[4:]
    peers, refs = refs[: 2 * len(blocks)], refs[2 * len(blocks) :]
    carry, refs = refs[:carried], refs[carried:]
    out_ref, rows_ref, own_s, b_s, w_s, x_s, r_s, own_sem, b_sem, t_sem, tp_sem = refs
    h, y, core = place()
    fill_positions(core, mirror_ref, rows_ref)

    own_copy = pltpu.make_async_copy(own_ref, own_s, own_sem)
    for i, g in enumerate(classes):
        for j in range(CLS):
            source = amp_ref.at[rows_ref[g * CLS + j], h]
            lanes = pl.ds(j * 128, 128)
            pltpu.make_async_copy(source, w_s.at[i, pl.ds(0, 128), lanes], t_sem.at[i]).start()
        pltpu.make_async_copy(tp_ref.at[g], w_s.at[i, pl.ds(128, 128)], tp_sem.at[i]).start()
        if i == 0:
            own_copy.start()
    copies = {}
    for k, block in enumerate(blocks):
        first, second = peers[2 * k], peers[2 * k + 1]
        if len(block) == 2:
            i = classes.index(block[0])
            pltpu.make_async_copy(first, b_s.at[i + core], b_sem.at[i, 0]).start()
            pltpu.make_async_copy(second, b_s.at[i + 1 - core], b_sem.at[i, 1]).start()
        else:
            i = classes.index(block[0])
            for half, ref in ((core, first), (1 - core, second)):
                target = b_s.at[i, pl.ds(pl.multiple_of(half * 1024, 1024), 1024)]
                pltpu.make_async_copy(ref, target, b_sem.at[i, 0 if ref is first else 1]).start()
        copies[i] = (first, second)

    def wait_weights(i):
        pltpu.make_async_copy(w_s.at[i, pl.ds(0, 128)], w_s.at[i, pl.ds(0, 128)], t_sem.at[i]).wait()
        pltpu.make_async_copy(tp_ref.at[classes[i]], w_s.at[i, pl.ds(128, 128)], tp_sem.at[i]).wait()

    def wait_peers(i):
        if i in copies:
            for k, ref in enumerate(copies[i]):
                rows = ref.shape[0]
                pltpu.make_async_copy(ref, b_s.at[i, pl.ds(0, rows)], b_sem.at[i, k]).wait()

    own_copy.wait()
    for i in range(n + 1):
        if i < n:
            wait_weights(i)
        if i > 0:
            wait_peers(i - 1)
        total = None
        for pair in range(4):
            for part in range(4):
                if i < n:
                    own = own_s[part * 512 : (part + 1) * 512, :]
                    lhs = jnp.concatenate([own, own], axis=1)
                    weights = w_s[i, :, pair * 256 : (pair + 1) * 256]
                    x = jnp.dot(lhs, weights, preferred_element_type=F32).astype(BF16)
                    for k in range(2):
                        j = pair * 2 + k
                        for l in range(16):
                            lane = (part * 16 + l) * 128
                            x_s[i % 2, j * 32 : (j + 1) * 32, lane : lane + 128] = x[
                                l * 32 : (l + 1) * 32, k * 128 : (k + 1) * 128
                            ]
                if i > 0:
                    step = pair * 4 + part
                    source = own_s if classes[i - 1] == 0 else b_s.at[i - 1]
                    b = source[step * 128 : (step + 1) * 128, :]
                    bt = jnp.concatenate([b[l * 32 : (l + 1) * 32] for l in range(4)], axis=1)
                    x2 = x_s[(i - 1) % 2, :, step * 512 : (step + 1) * 512]
                    term = lax.dot_general(x2, bt, NT, preferred_element_type=F32)
                    total = term if total is None else total + term
        if i > 0:
            r_s[i - 1] = total
    for q in range(4):
        columns = [ref[q ^ y] for ref in carry]
        for i in range(n):
            r = r_s[i]
            columns.append(
                jnp.concatenate([r[j * 32 + q * 8 : j * 32 + q * 8 + 8] for j in range(CLS)], axis=0)
            )
        out_ref[q ^ y] = jnp.concatenate(columns, axis=1) if len(columns) > 1 else columns[0]


def ladder(classes, mirror, amplitudes, received, own, blocks, peers, carry=()):
    n = len(classes)
    lanes = 32 * n + sum(c.shape[2] for c in carry)
    operands = [mirror, amplitudes, received, own, *peers, *carry]
    in_specs = [spec(pltpu.SMEM)] + [spec(pl.ANY)] * (3 + len(peers)) + [spec(pltpu.VMEM)] * len(carry)
    return pl.pallas_call(
        functools.partial(ladder_kernel, classes, blocks, len(carry)),
        out_shape=jax.ShapeDtypeStruct((4, 64, lanes), F32),
        in_specs=in_specs,
        out_specs=spec(pltpu.VMEM),
        scratch_shapes=[
            pltpu.SMEM((ROWS,), jnp.int32),
            pltpu.VMEM((2048, 128), BF16),
            pltpu.VMEM((n, 2048, 128), BF16),
            pltpu.VMEM((n, 256, 1024), BF16),
            pltpu.VMEM((2, 256, 8192), BF16),
            pltpu.VMEM((n, 256, 32), F32),
            pltpu.SemaphoreType.DMA,
            pltpu.SemaphoreType.DMA((n, 2)),
            pltpu.SemaphoreType.DMA((n,)),
            pltpu.SemaphoreType.DMA((n,)),
        ],
        compiler_params=params(36),
        cost_estimate=pl.CostEstimate(flops=n * 2**31, transcendentals=0, bytes_accessed=n * 2**20),
        name="ladder_" + "_".join(str(g) for g in classes),
    )(*operands)


def finish_kernel(order, mirror_ref, own_ref, r1_ref, r2_ref, r3_ref, out_ref, sum_s, pos_s):
    core = place()[2]
    total = own_ref[0] + r1_ref[...] + r2_ref[...] + r3_ref[...]
    sum_s[0] = total[:, 0:128]
    sum_s[1] = total[:, 128:256]
    for a8 in range(8):
        for k in range(2):
            strip = sum_s[k, pl.ds(a8, CLS, stride=8), :]
            for c in range(4):
                g = order[k * 4 + c]
                pos_s[g * CLS : (g + 1) * CLS, a8 * 32 : (a8 + 1) * 32] = strip[:, c * 32 : (c + 1) * 32]
    lane = lax.broadcasted_iota(jnp.int32, (ROWS, ROWS), 1)
    position = jnp.where(core == 1, jnp.broadcast_to(mirror_ref[...], (ROWS, ROWS)), lane)
    move = (lax.broadcasted_iota(jnp.int32, (ROWS, ROWS), 0) == position).astype(F32)
    out = lax.dot_general(
        pos_s[...], move, TN, preferred_element_type=F32, precision=lax.Precision.HIGHEST
    )
    out_ref[...] = out.reshape(8, 32, ROWS)


def finish(order, mirror, parts):
    out = pl.pallas_call(
        functools.partial(finish_kernel, order),
        out_shape=jax.ShapeDtypeStruct((8, 32, ROWS), F32),
        in_specs=[spec(pltpu.VMEM)] * 5,
        out_specs=spec(pltpu.VMEM),
        scratch_shapes=[pltpu.VMEM((2, 64, 128), F32), pltpu.VMEM((ROWS, 256), F32)],
        compiler_params=params(6),
        name="finish",
    )(mirror.reshape(1, ROWS), *parts)
    return jnp.transpose(out, (2, 0, 1))


def shards(cholesky, amplitudes, mirror):
    core = lax.axis_index("occ") & 1

    received = to_sibling(pack_tiles(mirror, amplitudes))
    quarters = lax.all_to_all(
        cholesky.reshape(4, 512, 128),
        "vir",
        0,
        0,
        axis_index_groups=[[4 * h + y for y in range(4)] for h in range(IRREPS)],
        tiled=True,
    )
    own, mine = order_rows(quarters)

    x1 = over_x(own, 1, 3)
    z0 = over_z(mine)
    x1_twin, z0_twin = to_sibling(x1), to_sibling(z0)
    x2 = over_x(lax.dynamic_slice_in_dim(x1, core * 1024, 1024, 0), 3, 1)
    zx1 = over_z(x1)
    x2_twin, zx1_twin = to_sibling(x2), to_sibling(zx1)
    zx2 = over_z(x2)
    zx2_twin = to_sibling(zx2)

    common = (mirror, amplitudes, received, own)
    first = ladder((0,), *common, (), ())
    near = ladder((1, 2, 6), *common, ((1,), (2, 6)), (z0, z0_twin, x1, x1_twin), (first,))
    far = ladder(
        (3, 7, 4, 5), *common, ((3, 7), (4,), (5,)), (zx1, zx1_twin, x2, x2_twin, zx2, zx2_twin), (near,)
    )
    parts = [far] + [over_y(far[k], k) for k in range(1, 4)]
    return finish((0, 1, 2, 6, 3, 7, 4, 5), mirror, parts)


def solution(mesh):
    placed = (P(None, "vir", None), P("occ", None, None, None), P("occ"))
    return jax.shard_map(
        shards, mesh=mesh, in_specs=placed, out_specs=P("occ", "vir", None), check_vma=False
    )
```

```python
import functools

import jax
import jax.numpy as jnp
from jax import lax
from jax.experimental import pallas as pl
from jax.experimental.pallas import tpu as pltpu
from jax.sharding import PartitionSpec as P

IRREPS = 8
CLS = 8
ROWS = IRREPS * CLS
NT = (((1,), (1,)), ((), ()))
BF16 = jnp.bfloat16
F32 = jnp.float32
MIB = 2**20


def permute(value, move):
    pairs = []
    for occ in range(4):
        for vir in range(32):
            to_occ, to_vir = move(occ, vir)
            pairs.append((occ * 32 + vir, to_occ * 32 + to_vir))
    return lax.ppermute(value, ("occ", "vir"), pairs)


def over_y(value, k):
    return permute(value, lambda occ, vir: (occ, vir ^ k))


def over_x(value, even, odd):
    return permute(value, lambda occ, vir: (occ, vir ^ (8 * (odd if occ & 1 else even))))


def over_z(value):
    return permute(value, lambda occ, vir: (occ ^ (2 if occ & 1 else 0), vir ^ 4))


def to_sibling(value):
    return permute(value, lambda occ, vir: (occ ^ 1, vir))


def spec(space):
    return pl.BlockSpec(memory_space=space)


def params(mib):
    return pltpu.CompilerParams(vmem_limit_bytes=mib * MIB)


def place():
    vir, core = lax.axis_index("vir"), lax.axis_index("occ") & 1
    return lax.shift_right_logical(vir, 2), vir & 3, core


def pack_kernel(mirror_ref, amp_ref, own_ref, out_ref, sems, own_sems):
    h = place()[0]
    for g in range(IRREPS):
        for j in range(CLS):
            row = g * CLS + j
            target = out_ref.at[g, mirror_ref[row] - g * CLS]
            pltpu.make_async_copy(amp_ref.at[row, h ^ g], target, sems.at[g]).start()
    own_copies = []
    for g in range(IRREPS):
        source = amp_ref.at[pl.ds(g * CLS, CLS), h]
        own_copies.append(pltpu.make_async_copy(source, own_ref.at[g], own_sems.at[g]))
        own_copies[-1].start()
    for g in range(IRREPS):
        pltpu.make_async_copy(out_ref.at[g], out_ref.at[g], sems.at[g]).wait()
    for copy in own_copies:
        copy.wait()


def pack_tiles(mirror, amplitudes):
    shape = (IRREPS, CLS, 128, 128)
    return pl.pallas_call(
        pack_kernel,
        out_shape=(jax.ShapeDtypeStruct(shape, BF16), jax.ShapeDtypeStruct(shape, BF16)),
        in_specs=[spec(pltpu.SMEM), spec(pltpu.HBM)],
        out_specs=(spec(pltpu.VMEM), spec(pltpu.VMEM)),
        scratch_shapes=[
            pltpu.SemaphoreType.DMA((IRREPS,)),
            pltpu.SemaphoreType.DMA((IRREPS,)),
        ],
        compiler_params=params(46),
        name="pack_tiles",
    )(mirror, amplitudes)


def rows_kernel(r0_ref, r1_ref, r2_ref, r3_ref, _, out_ref, all_ref):
    y = place()[1]
    for k, ref in enumerate((r0_ref, r1_ref, r2_ref, r3_ref)):
        all_ref[k ^ y] = ref[...]

    def step(i, _):
        start = pl.multiple_of(i * 16, 16)
        parts = [all_ref[q, pl.ds(start, 16), :].astype(F32) for q in range(4)]
        both = [p[0:8] for p in parts] + [p[8:16] for p in parts]
        out_ref[pl.ds(pl.multiple_of(i * 64, 64), 64), :] = jnp.concatenate(both, axis=0).astype(BF16)
        return 0

    lax.fori_loop(0, 32, step, 0, unroll=8)


def order_rows(quarters, token):
    return pl.pallas_call(
        rows_kernel,
        out_shape=jax.ShapeDtypeStruct((2048, 128), BF16),
        in_specs=[spec(pltpu.VMEM)] * 4 + [spec(pl.ANY)],
        out_specs=spec(pltpu.VMEM),
        scratch_shapes=[pltpu.VMEM((4, 512, 128), BF16)],
        compiler_params=params(6),
        name="order_rows",
    )(*quarters, token)


def relay(values, tokens):
    n = len(values)
    outs = pl.pallas_call(
        lambda *refs: None,
        out_shape=tuple(jax.ShapeDtypeStruct(v.shape, v.dtype) for v in values),
        in_specs=[spec(pl.ANY)] * (n + len(tokens)),
        out_specs=tuple(spec(pl.ANY) for _ in values),
        input_output_aliases={i: i for i in range(n)},
        compiler_params=params(1),
        name="relay",
    )(*values, *tokens)
    return outs


def half_kernel(value_ref, _, out_ref):
    core = place()[2]
    out_ref[...] = value_ref[pl.ds(pl.multiple_of(core * 1024, 1024), 1024), :]


def own_half(value, token):
    return pl.pallas_call(
        half_kernel,
        out_shape=jax.ShapeDtypeStruct((1024, 128), BF16),
        in_specs=[spec(pltpu.VMEM), spec(pl.ANY)],
        out_specs=spec(pltpu.VMEM),
        compiler_params=params(2),
        name="own_half",
    )(value, token)


def stage1_kernel(groups, tokens, own_ref, t_ref, tp_ref, *refs):
    places = [(ref, i, g) for ref, group in zip(refs[tokens:], groups) for i, g in enumerate(group)]
    for x_ref, i, g in places:
        for pair in range(4):
            j0, j1 = 2 * pair, 2 * pair + 1
            upper = jnp.concatenate([t_ref[g, j0], t_ref[g, j1]], axis=1)
            lower = jnp.concatenate([tp_ref[g, j0].T, tp_ref[g, j1].T], axis=1)
            weights = jnp.concatenate([upper, lower], axis=0)
            for part in range(4):
                own = own_ref[part * 512 : (part + 1) * 512, :]
                lhs = jnp.concatenate([own, own], axis=1)
                x = jnp.dot(lhs, weights, preferred_element_type=F32).astype(BF16)
                for k in range(2):
                    j = 2 * pair + k
                    for l in range(16):
                        lane = (part * 16 + l) * 128
                        x_ref[i, j * 32 : (j + 1) * 32, lane : lane + 128] = x[
                            l * 32 : (l + 1) * 32, k * 128 : (k + 1) * 128
                        ]


def stage1(groups, own, tiles, received, tokens=()):
    n = sum(len(group) for group in groups)
    return pl.pallas_call(
        functools.partial(stage1_kernel, groups, len(tokens)),
        out_shape=tuple(jax.ShapeDtypeStruct((len(group), 256, 8192), BF16) for group in groups),
        in_specs=[spec(pltpu.VMEM)] * 3 + [spec(pl.ANY)] * len(tokens),
        out_specs=tuple(spec(pltpu.VMEM) for _ in groups),
        compiler_params=params(8),
        cost_estimate=pl.CostEstimate(flops=n * 2**30, transcendentals=0, bytes_accessed=n * 2**18),
        name="stage1_" + "_".join(str(g) for group in groups for g in group),
    )(own, tiles, received, *tokens)


def stage2_kernel(blocks, n_x, n_b, carried, tokens, n, *refs):
    x_refs, refs = refs[:n_x], refs[n_x:]
    b_refs, refs = refs[:n_b], refs[n_b:]
    carry, refs = refs[:carried], refs[carried:]
    out_ref, r_s = refs[tokens:]
    _, y, core = place()

    def contract(x_ref, index, lane0, b_ref, rows):
        total = None
        for step in range(rows // 128):
            b = b_ref[step * 128 : (step + 1) * 128, :]
            bt = jnp.concatenate([b[l * 32 : (l + 1) * 32] for l in range(4)], axis=1)
            lane = lane0 + step * 512
            if not isinstance(lane, int):
                lane = pl.multiple_of(lane, 512)
            x = x_ref[index, :, pl.ds(lane, 512)]
            term = lax.dot_general(x, bt, NT, preferred_element_type=F32)
            total = term if total is None else total + term
        return total

    at = 0
    for kind, *slots in blocks:
        if kind == "all":
            ((k, index, to),) = slots
            r_s[to] = contract(x_refs[k], index, 0, b_refs[at], 2048)
            at += 1
        elif kind == "swap":
            (k, first, to_first), (_, second, to_second) = slots
            odd = core == 1
            r_s[jnp.where(odd, to_second, to_first)] = contract(
                x_refs[k], jnp.where(odd, second, first), 0, b_refs[at], 2048
            )
            r_s[jnp.where(odd, to_first, to_second)] = contract(
                x_refs[k], jnp.where(odd, first, second), 0, b_refs[at + 1], 2048
            )
            at += 2
        else:
            ((k, index, to),) = slots
            mine = contract(x_refs[k], index, core * 4096, b_refs[at], 1024)
            r_s[to] = mine + contract(x_refs[k], index, (1 - core) * 4096, b_refs[at + 1], 1024)
            at += 2
    for q in range(4):
        columns = [ref[q ^ y] for ref in carry]
        for i in range(n):
            r = r_s[i]
            columns.append(
                jnp.concatenate([r[j * 32 + q * 8 : j * 32 + q * 8 + 8] for j in range(CLS)], axis=0)
            )
        out_ref[q ^ y] = jnp.concatenate(columns, axis=1) if len(columns) > 1 else columns[0]


def stage2(name, n, blocks, xs, bs, carry=(), tokens=()):
    lanes = 32 * n + sum(c.shape[2] for c in carry)
    kernel = functools.partial(stage2_kernel, blocks, len(xs), len(bs), len(carry), len(tokens), n)
    return pl.pallas_call(
        kernel,
        out_shape=jax.ShapeDtypeStruct((4, 64, lanes), F32),
        in_specs=[spec(pltpu.VMEM)] * (len(xs) + len(bs) + len(carry)) + [spec(pl.ANY)] * len(tokens),
        out_specs=spec(pltpu.VMEM),
        scratch_shapes=[pltpu.VMEM((n, 256, 32), F32)],
        compiler_params=params(8),
        cost_estimate=pl.CostEstimate(flops=n * 2**30, transcendentals=0, bytes_accessed=n * 2**18),
        name="stage2_" + name,
    )(*xs, *bs, *carry, *tokens)


def finish_kernel(order, own_ref, r1_ref, r2_ref, r3_ref, out_ref, sum_s, pos_s):
    total = own_ref[0] + r1_ref[...] + r2_ref[...] + r3_ref[...]
    sum_s[0] = total[:, 0:128]
    sum_s[1] = total[:, 128:256]
    for a8 in range(8):
        for k in range(2):
            strip = sum_s[k, pl.ds(a8, CLS, stride=8), :]
            for c in range(4):
                g = order[k * 4 + c]
                pos_s[g * CLS : (g + 1) * CLS, a8 * 32 : (a8 + 1) * 32] = strip[:, c * 32 : (c + 1) * 32]
    out_ref[...] = pos_s[...].T.reshape(8, 32, ROWS)


def finish(order, parts):
    out = pl.pallas_call(
        functools.partial(finish_kernel, order),
        out_shape=jax.ShapeDtypeStruct((8, 32, ROWS), F32),
        in_specs=[spec(pltpu.VMEM)] * 4,
        out_specs=spec(pltpu.VMEM),
        scratch_shapes=[pltpu.VMEM((2, 64, 128), F32), pltpu.VMEM((ROWS, 256), F32)],
        compiler_params=params(6),
        name="finish",
    )(*parts)
    return jnp.transpose(out, (2, 0, 1))


def shards(cholesky, amplitudes, mirror):
    y = lax.axis_index("vir") & 3

    by_chunk = cholesky.reshape(4, 512, 128)
    quarters = [lax.dynamic_index_in_dim(by_chunk, y ^ k, 0, keepdims=False) for k in range(4)]
    quarters = [quarters[0]] + [over_y(quarters[k], k) for k in range(1, 4)]
    tiles, outgoing = pack_tiles(mirror, amplitudes)
    received = to_sibling(outgoing)
    own = order_rows(quarters, received)

    x1 = over_x(own, 1, 3)
    z0 = over_z(own)
    xc0, xc1, xc26, xc4 = stage1(((0,), (1,), (2, 6), (4,)), own, tiles, received)
    x1, z0 = relay((x1, z0), (xc0,))
    x1_twin = to_sibling(x1)
    x2 = over_x(own_half(x1, xc0), 3, 1)
    zx1 = over_z(x1)
    near = stage2(
        "near", 4, (("all", (0, 0, 0)), ("all", (1, 0, 1)), ("swap", (2, 0, 2), (2, 1, 3))),
        (xc0, xc1, xc26), (own, z0, x1, x1_twin),
    )
    x2, zx1 = relay((x2, zx1), (near,))
    x2_twin, zx1_twin = to_sibling(x2), to_sibling(zx1)
    zx2 = over_z(x2)
    xc37, xc5 = stage1(((3, 7), (5,)), own, tiles, received, (x2,))
    (zx2,) = relay((zx2,), (xc5,))
    zx2_twin = to_sibling(zx2)
    far = stage2(
        "far", 3, (("halves", (0, 0, 0)), ("swap", (1, 0, 1), (1, 1, 2))),
        (xc4, xc37), (x2, x2_twin, zx1, zx1_twin), (near,), (zx2,),
    )
    last = stage2("last", 1, (("halves", (0, 0, 0)),), (xc5,), (zx2, zx2_twin), (far,))
    parts = [last] + [over_y(last[k], k) for k in range(1, 4)]
    return finish((0, 1, 2, 6, 4, 3, 7, 5), parts)


def solution(mesh):
    placed = (P(None, "vir", None), P("occ", None, None, None), P("occ"))
    return jax.shard_map(
        shards, mesh=mesh, in_specs=placed, out_specs=P("occ", "vir", None), check_vma=False
    )
```

```python
import functools

import jax
import jax.numpy as jnp
from jax import lax
from jax.experimental import pallas as pl
from jax.experimental.pallas import tpu as pltpu
from jax.sharding import PartitionSpec as P

IRREPS = 8
CLS = 8
ROWS = IRREPS * CLS
NT = (((1,), (1,)), ((), ()))
BF16 = jnp.bfloat16
F32 = jnp.float32
MIB = 2**20


def permute(value, move):
    pairs = []
    for occ in range(4):
        for vir in range(32):
            to_occ, to_vir = move(occ, vir)
            pairs.append((occ * 32 + vir, to_occ * 32 + to_vir))
    return lax.ppermute(value, ("occ", "vir"), pairs)


def over_y(value, k):
    return permute(value, lambda occ, vir: (occ, vir ^ k))


def over_x(value, even, odd):
    return permute(value, lambda occ, vir: (occ, vir ^ (8 * (odd if occ & 1 else even))))


def over_z(value):
    return permute(value, lambda occ, vir: (occ ^ (2 if occ & 1 else 0), vir ^ 4))


def to_sibling(value):
    return permute(value, lambda occ, vir: (occ ^ 1, vir))


def spec(space):
    return pl.BlockSpec(memory_space=space)


def params(mib):
    return pltpu.CompilerParams(vmem_limit_bytes=mib * MIB)


def place():
    vir, core = lax.axis_index("vir"), lax.axis_index("occ") & 1
    return lax.shift_right_logical(vir, 2), vir & 3, core


def cut_kernel(chol_ref, *outs):
    _, y, core = place()
    for k, out_ref in enumerate(outs):
        out_ref[...] = chol_ref[pl.ds(pl.multiple_of((y ^ k) * 512 + core * 256, 256), 256), :]


def cut_chunks(cholesky):
    return pl.pallas_call(
        cut_kernel,
        out_shape=tuple(jax.ShapeDtypeStruct((256, 128), BF16) for _ in range(4)),
        in_specs=[spec(pltpu.VMEM)],
        out_specs=tuple(spec(pltpu.VMEM) for _ in range(4)),
        compiler_params=params(4),
        name="cut_chunks",
    )(cholesky.reshape(2048, 128))


def pack_kernel(amp_ref, _, own_ref, *refs):
    outs, sems, own_sems = refs[:-2], refs[-2], refs[-1]
    h = place()[0]
    per = IRREPS // len(outs)
    copies = []
    for g in range(IRREPS):
        rows = amp_ref.at[pl.ds(g * CLS, CLS)]
        copies.append(pltpu.make_async_copy(rows.at[:, h ^ g], outs[g // per].at[g % per], sems.at[g]))
        copies.append(pltpu.make_async_copy(rows.at[:, h], own_ref.at[g], own_sems.at[g]))
    for copy in copies:
        copy.start()
    for copy in copies:
        copy.wait()


def pack_tiles(amplitudes, token, pieces):
    shape = (IRREPS, CLS, 128, 128)
    piece = jax.ShapeDtypeStruct((IRREPS // pieces, CLS, 128, 128), BF16)
    outs = pl.pallas_call(
        pack_kernel,
        out_shape=(jax.ShapeDtypeStruct(shape, BF16),) + (piece,) * pieces,
        in_specs=[spec(pltpu.HBM), spec(pl.ANY)],
        out_specs=(spec(pltpu.VMEM),) * (1 + pieces),
        scratch_shapes=[pltpu.SemaphoreType.DMA((IRREPS,)), pltpu.SemaphoreType.DMA((IRREPS,))],
        compiler_params=params(46),
        name="pack_tiles",
    )(amplitudes, token)
    return outs[0], outs[1:]


def rows_kernel(r0_ref, r1_ref, r2_ref, r3_ref, _, out_ref, all_ref):
    y = place()[1]
    for k, ref in enumerate((r0_ref, r1_ref, r2_ref, r3_ref)):
        all_ref[k ^ y] = ref[...]

    def step(i, _):
        start = pl.multiple_of(i * 16, 16)
        parts = [all_ref[q, pl.ds(start, 16), :].astype(F32) for q in range(4)]
        both = [p[0:8] for p in parts] + [p[8:16] for p in parts]
        out_ref[pl.ds(pl.multiple_of(i * 64, 64), 64), :] = jnp.concatenate(both, axis=0).astype(BF16)
        return 0

    lax.fori_loop(0, 16, step, 0, unroll=8)


def order_rows(quarters, token):
    return pl.pallas_call(
        rows_kernel,
        out_shape=jax.ShapeDtypeStruct((1024, 128), BF16),
        in_specs=[spec(pltpu.VMEM)] * 4 + [spec(pl.ANY)],
        out_specs=spec(pltpu.VMEM),
        scratch_shapes=[pltpu.VMEM((4, 256, 128), BF16)],
        compiler_params=params(6),
        name="order_rows",
    )(*quarters, token)


def relay(values, tokens):
    n = len(values)
    outs = pl.pallas_call(
        lambda *refs: None,
        out_shape=tuple(jax.ShapeDtypeStruct(v.shape, v.dtype) for v in values),
        in_specs=[spec(pl.ANY)] * (n + len(tokens)),
        out_specs=tuple(spec(pl.ANY) for _ in values),
        input_output_aliases={i: i for i in range(n)},
        compiler_params=params(1),
        name="relay",
    )(*values, *tokens)
    return outs


def join_kernel(first_ref, second_ref, _, both_ref, chosen_ref):
    core = place()[2]
    both_ref[0] = first_ref[...]
    both_ref[1] = second_ref[...]
    chosen_ref[...] = both_ref[core]


def join(first, second, token):
    return pl.pallas_call(
        join_kernel,
        out_shape=(
            jax.ShapeDtypeStruct((2, *first.shape), first.dtype),
            jax.ShapeDtypeStruct(first.shape, first.dtype),
        ),
        in_specs=[spec(pltpu.VMEM)] * 2 + [spec(pl.ANY)],
        out_specs=(spec(pltpu.VMEM), spec(pltpu.VMEM)),
        compiler_params=params(4),
        name="join",
    )(first, second, token)


def stage1_kernel(classes, pieces, tokens, mirror_ref, mine_ref, other_ref, t_ref, *refs):
    tp_refs, refs = refs[:pieces], refs[pieces + tokens :]
    per = IRREPS // pieces
    for x_ref, g in zip(refs, classes):
        tp_ref = tp_refs[g // per].at[g % per]
        for pair in range(4):
            j0, j1 = 2 * pair, 2 * pair + 1
            twins = [tp_ref[mirror_ref[g * CLS + j] - g * CLS].T for j in (j0, j1)]
            upper = jnp.concatenate([t_ref[g, j0], t_ref[g, j1]], axis=1)
            weights = jnp.concatenate([upper, jnp.concatenate(twins, axis=1)], axis=0)
            for part in range(4):
                own_ref = (mine_ref, other_ref)[part // 2]
                own = own_ref[(part % 2) * 512 : (part % 2 + 1) * 512, :]
                lhs = jnp.concatenate([own, own], axis=1)
                x = jnp.dot(lhs, weights, preferred_element_type=F32).astype(BF16)
                for k in range(2):
                    j = 2 * pair + k
                    for l in range(16):
                        lane = (part * 16 + l) * 128
                        x_ref[j * 32 : (j + 1) * 32, lane : lane + 128] = x[
                            l * 32 : (l + 1) * 32, k * 128 : (k + 1) * 128
                        ]


def stage1(classes, mirror, own, tiles, received, tokens=()):
    n = len(classes)
    return pl.pallas_call(
        functools.partial(stage1_kernel, classes, len(received), len(tokens)),
        out_shape=tuple(jax.ShapeDtypeStruct((256, 8192), BF16) for _ in classes),
        in_specs=[spec(pltpu.SMEM)]
        + [spec(pltpu.VMEM)] * (3 + len(received))
        + [spec(pl.ANY)] * len(tokens),
        out_specs=tuple(spec(pltpu.VMEM) for _ in classes),
        compiler_params=params(8),
        cost_estimate=pl.CostEstimate(flops=n * 2**30, transcendentals=0, bytes_accessed=n * 2**18),
        name="stage1_" + "_".join(str(g) for g in classes),
    )(mirror, *own, tiles, *received, *tokens)


def stage2_kernel(picks, n_b, carried, tokens, *refs):
    n = len(picks)
    x_refs, refs = refs[:n], refs[n:]
    b_refs, refs = refs[:n_b], refs[n_b:]
    carry, refs = refs[:carried], refs[carried:]
    out_ref, r_s = refs[tokens:]
    y = place()[1]
    for i, halves in enumerate(picks):
        total = None
        for half, (at, index) in enumerate(halves):
            b_ref = b_refs[at] if index is None else b_refs[at].at[index]
            for step in range(8):
                b = b_ref[step * 128 : (step + 1) * 128, :]
                bt = jnp.concatenate([b[l * 32 : (l + 1) * 32] for l in range(4)], axis=1)
                lane = half * 4096 + step * 512
                term = lax.dot_general(
                    x_refs[i][:, lane : lane + 512], bt, NT, preferred_element_type=F32
                )
                total = term if total is None else total + term
        r_s[i] = total
    for q in range(4):
        columns = [ref[q ^ y] for ref in carry]
        for i in range(n):
            r = r_s[i]
            columns.append(
                jnp.concatenate([r[j * 32 + q * 8 : j * 32 + q * 8 + 8] for j in range(CLS)], axis=0)
            )
        out_ref[q ^ y] = jnp.concatenate(columns, axis=1) if len(columns) > 1 else columns[0]


def stage2(name, xs, picks, bs, carry=(), tokens=()):
    n = len(xs)
    lanes = 32 * n + sum(c.shape[2] for c in carry)
    return pl.pallas_call(
        functools.partial(stage2_kernel, picks, len(bs), len(carry), len(tokens)),
        out_shape=jax.ShapeDtypeStruct((4, 64, lanes), F32),
        in_specs=[spec(pltpu.VMEM)] * (n + len(bs) + len(carry)) + [spec(pl.ANY)] * len(tokens),
        out_specs=spec(pltpu.VMEM),
        scratch_shapes=[pltpu.VMEM((n, 256, 32), F32)],
        compiler_params=params(8),
        cost_estimate=pl.CostEstimate(flops=n * 2**30, transcendentals=0, bytes_accessed=n * 2**18),
        name="stage2_" + name,
    )(*xs, *bs, *carry, *tokens)


def finish_kernel(order, own_ref, r1_ref, r2_ref, r3_ref, out_ref, sum_s, pos_s):
    total = own_ref[0] + r1_ref[...] + r2_ref[...] + r3_ref[...]
    sum_s[0] = total[:, 0:128]
    sum_s[1] = total[:, 128:256]
    for a8 in range(8):
        for k in range(2):
            strip = sum_s[k, pl.ds(a8, CLS, stride=8), :]
            for c in range(4):
                g = order[k * 4 + c]
                pos_s[g * CLS : (g + 1) * CLS, a8 * 32 : (a8 + 1) * 32] = strip[:, c * 32 : (c + 1) * 32]
    out_ref[...] = pos_s[...].T.reshape(8, 32, ROWS)


def finish(order, parts):
    out = pl.pallas_call(
        functools.partial(finish_kernel, order),
        out_shape=jax.ShapeDtypeStruct((8, 32, ROWS), F32),
        in_specs=[spec(pltpu.VMEM)] * 4,
        out_specs=spec(pltpu.VMEM),
        scratch_shapes=[pltpu.VMEM((2, 64, 128), F32), pltpu.VMEM((ROWS, 256), F32)],
        compiler_params=params(6),
        name="finish",
    )(*parts)
    return jnp.transpose(out, (2, 0, 1))


PIECES = 1


def shards(cholesky, amplitudes, mirror):
    chunks = cut_chunks(cholesky)
    quarters = (chunks[0],) + tuple(over_y(chunks[k], k) for k in range(1, 4))
    tiles, outgoing = pack_tiles(amplitudes, chunks[0], PIECES)
    received = tuple(to_sibling(piece) for piece in outgoing)
    mine = order_rows(quarters, tiles)
    own = (mine, to_sibling(mine))

    x1a, x1b, z0 = over_x(mine, 1, 1), over_x(mine, 3, 3), over_z(mine)
    xc0, xc1, xc2, xc6, xc4 = stage1((0, 1, 2, 6, 4), mirror, own, tiles, received)
    (z0,) = relay((z0,), (xc0,))
    x1, forward = join(x1a, x1b, xc0)
    x1_other, z0_other = to_sibling(x1), to_sibling(z0)
    x2 = over_x(forward, 3, 1)
    zx1 = over_z(x1)
    near = stage2(
        "near",
        (xc0, xc1, xc2, xc6),
        (((0, None), (1, None)), ((2, None), (3, None)), ((4, 0), (5, 0)), ((4, 1), (5, 1))),
        (*own, z0, z0_other, x1, x1_other),
    )
    (x2,) = relay((x2,), (near,))
    x2_other = to_sibling(x2)
    zx2 = over_z(x2)
    xc3, xc7, xc5 = stage1((3, 7, 5), mirror, own, tiles, received, (x2,))
    zx1, zx2 = relay((zx1, zx2), (xc5,))
    zx1_other, zx2_other = to_sibling(zx1), to_sibling(zx2)
    far = stage2("far", (xc4,), (((0, None), (1, None)),), (x2, x2_other), (near,), (zx1,))
    last = stage2(
        "last",
        (xc3, xc7, xc5),
        (((0, 0), (1, 0)), ((0, 1), (1, 1)), ((2, None), (3, None))),
        (zx1, zx1_other, zx2, zx2_other),
        (far,),
    )
    parts = [last] + [over_y(last[k], k) for k in range(1, 4)]
    return finish((0, 1, 2, 6, 4, 3, 7, 5), parts)


def solution(mesh):
    placed = (P(None, "vir", None), P("occ", None, None, None), P("occ"))
    return jax.shard_map(
        shards, mesh=mesh, in_specs=placed, out_specs=P("occ", "vir", None), check_vma=False
    )
```

```python
import functools

import jax
import jax.numpy as jnp
from jax import lax
from jax.experimental import pallas as pl
from jax.experimental.pallas import tpu as pltpu
from jax.sharding import PartitionSpec as P

IRREPS = 8
CLS = 8
ROWS = IRREPS * CLS
NT = (((1,), (1,)), ((), ()))
BF16 = jnp.bfloat16
F32 = jnp.float32
MIB = 2**20


def permute(value, move):
    pairs = []
    for occ in range(4):
        for vir in range(32):
            to_occ, to_vir = move(occ, vir)
            pairs.append((occ * 32 + vir, to_occ * 32 + to_vir))
    return lax.ppermute(value, ("occ", "vir"), pairs)


def over_y(value, k):
    return permute(value, lambda occ, vir: (occ, vir ^ k))


def over_x(value, even, odd):
    return permute(value, lambda occ, vir: (occ, vir ^ (8 * (odd if occ & 1 else even))))


def over_z(value):
    return permute(value, lambda occ, vir: (occ ^ (2 if occ & 1 else 0), vir ^ 4))


def to_sibling(value):
    return permute(value, lambda occ, vir: (occ ^ 1, vir))


def spec(space):
    return pl.BlockSpec(memory_space=space)


def params(mib):
    return pltpu.CompilerParams(vmem_limit_bytes=mib * MIB)


def place():
    vir, core = lax.axis_index("vir"), lax.axis_index("occ") & 1
    return lax.shift_right_logical(vir, 2), vir & 3, core


def send_kernel(chol_ref, amp_ref, *refs):
    chunks, tiles_ref, chunk_sems, tile_sems = refs[:4], refs[4], refs[5], refs[6]
    h, y, core = place()
    copies = []
    for k, out_ref in enumerate(chunks):
        start = pl.multiple_of((y ^ k) * 512 + core * 256, 256)
        copies.append(pltpu.make_async_copy(chol_ref.at[pl.ds(start, 256)], out_ref, chunk_sems.at[k]))
    for g in range(IRREPS):
        source = amp_ref.at[pl.ds(g * CLS, CLS), h ^ g]
        copies.append(pltpu.make_async_copy(source, tiles_ref.at[g], tile_sems.at[g]))
    for copy in copies:
        copy.start()
    for copy in copies:
        copy.wait()


def cut_to_send(cholesky, amplitudes):
    chunk = jax.ShapeDtypeStruct((256, 128), BF16)
    outs = pl.pallas_call(
        send_kernel,
        out_shape=(chunk,) * 4 + (jax.ShapeDtypeStruct((IRREPS, CLS, 128, 128), BF16),),
        in_specs=[spec(pltpu.HBM)] * 2,
        out_specs=(spec(pltpu.VMEM),) * 5,
        scratch_shapes=[pltpu.SemaphoreType.DMA((4,)), pltpu.SemaphoreType.DMA((IRREPS,))],
        compiler_params=params(46),
        name="cut_to_send",
    )(pltpu.with_memory_space_constraint(cholesky.reshape(2048, 128), pltpu.HBM), amplitudes)
    return outs[:4], outs[4]


def twist_kernel(mirror_ref, amp_ref, received_ref, own_ref, out_ref, sems):
    h = place()[0]
    copies = []
    for g in range(IRREPS):
        source = amp_ref.at[pl.ds(g * CLS, CLS), h]
        copies.append(pltpu.make_async_copy(source, own_ref.at[g], sems.at[g]))
        copies[-1].start()
    for g in range(IRREPS):
        for j in range(CLS):
            out_ref[g, j] = received_ref[g, mirror_ref[g * CLS + j] - g * CLS].T
    for copy in copies:
        copy.wait()


def twist_tiles(mirror, amplitudes, received):
    shape = jax.ShapeDtypeStruct((IRREPS, CLS, 128, 128), BF16)
    return pl.pallas_call(
        twist_kernel,
        out_shape=(shape, shape),
        in_specs=[spec(pltpu.SMEM), spec(pltpu.HBM), spec(pltpu.VMEM)],
        out_specs=(spec(pltpu.VMEM), spec(pltpu.VMEM)),
        scratch_shapes=[pltpu.SemaphoreType.DMA((IRREPS,))],
        compiler_params=params(46),
        name="twist_tiles",
    )(mirror, amplitudes, received)


def rows_kernel(r0_ref, r1_ref, r2_ref, r3_ref, _, out_ref, all_ref):
    y = place()[1]
    for k, ref in enumerate((r0_ref, r1_ref, r2_ref, r3_ref)):
        all_ref[k ^ y] = ref[...]

    def step(i, _):
        start = pl.multiple_of(i * 16, 16)
        parts = [all_ref[q, pl.ds(start, 16), :].astype(F32) for q in range(4)]
        both = [p[0:8] for p in parts] + [p[8:16] for p in parts]
        out_ref[pl.ds(pl.multiple_of(i * 64, 64), 64), :] = jnp.concatenate(both, axis=0).astype(BF16)
        return 0

    lax.fori_loop(0, 16, step, 0, unroll=8)


def order_rows(quarters, token):
    return pl.pallas_call(
        rows_kernel,
        out_shape=jax.ShapeDtypeStruct((1024, 128), BF16),
        in_specs=[spec(pltpu.VMEM)] * 4 + [spec(pl.ANY)],
        out_specs=spec(pltpu.VMEM),
        scratch_shapes=[pltpu.VMEM((4, 256, 128), BF16)],
        compiler_params=params(6),
        name="order_rows",
    )(*quarters, token)


def relay(values, tokens):
    n = len(values)
    outs = pl.pallas_call(
        lambda *refs: None,
        out_shape=tuple(jax.ShapeDtypeStruct(v.shape, v.dtype) for v in values),
        in_specs=[spec(pl.ANY)] * (n + len(tokens)),
        out_specs=tuple(spec(pl.ANY) for _ in values),
        input_output_aliases={i: i for i in range(n)},
        compiler_params=params(1),
        name="relay",
    )(*values, *tokens)
    return outs


def join_kernel(first_ref, second_ref, _, both_ref, chosen_ref):
    core = place()[2]
    both_ref[0] = first_ref[...]
    both_ref[1] = second_ref[...]
    chosen_ref[...] = both_ref[core]


def join(first, second, token):
    return pl.pallas_call(
        join_kernel,
        out_shape=(
            jax.ShapeDtypeStruct((2, *first.shape), first.dtype),
            jax.ShapeDtypeStruct(first.shape, first.dtype),
        ),
        in_specs=[spec(pltpu.VMEM)] * 2 + [spec(pl.ANY)],
        out_specs=(spec(pltpu.VMEM), spec(pltpu.VMEM)),
        compiler_params=params(4),
        name="join",
    )(first, second, token)


def stage1_kernel(classes, tokens, mine_ref, other_ref, t_ref, tp_ref, *refs):
    for x_ref, g in zip(refs[tokens:], classes):
        for pair in range(4):
            j0, j1 = 2 * pair, 2 * pair + 1
            upper = jnp.concatenate([t_ref[g, j0], t_ref[g, j1]], axis=1)
            lower = jnp.concatenate([tp_ref[g, j0], tp_ref[g, j1]], axis=1)
            weights = jnp.concatenate([upper, lower], axis=0)
            for part in range(4):
                own_ref = (mine_ref, other_ref)[part // 2]
                own = own_ref[(part % 2) * 512 : (part % 2 + 1) * 512, :]
                lhs = jnp.concatenate([own, own], axis=1)
                x = jnp.dot(lhs, weights, preferred_element_type=F32).astype(BF16)
                for k in range(2):
                    j = 2 * pair + k
                    for l in range(16):
                        lane = (part * 16 + l) * 128
                        x_ref[j * 32 : (j + 1) * 32, lane : lane + 128] = x[
                            l * 32 : (l + 1) * 32, k * 128 : (k + 1) * 128
                        ]


def stage1(classes, own, tiles, tokens=()):
    n = len(classes)
    return pl.pallas_call(
        functools.partial(stage1_kernel, classes, len(tokens)),
        out_shape=tuple(jax.ShapeDtypeStruct((256, 8192), BF16) for _ in classes),
        in_specs=[spec(pltpu.VMEM)] * 4 + [spec(pl.ANY)] * len(tokens),
        out_specs=tuple(spec(pltpu.VMEM) for _ in classes),
        compiler_params=params(8),
        cost_estimate=pl.CostEstimate(flops=n * 2**30, transcendentals=0, bytes_accessed=n * 2**18),
        name="stage1_" + "_".join(str(g) for g in classes),
    )(*own, *tiles, *tokens)


def stage2_kernel(picks, n_b, carried, tokens, *refs):
    n = len(picks)
    x_refs, refs = refs[:n], refs[n:]
    b_refs, refs = refs[:n_b], refs[n_b:]
    carry, refs = refs[:carried], refs[carried:]
    out_ref, r_s = refs[tokens:]
    y = place()[1]
    for i, halves in enumerate(picks):
        total = None
        for half, (at, index) in enumerate(halves):
            b_ref = b_refs[at] if index is None else b_refs[at].at[index]
            for step in range(8):
                b = b_ref[step * 128 : (step + 1) * 128, :]
                bt = jnp.concatenate([b[l * 32 : (l + 1) * 32] for l in range(4)], axis=1)
                lane = half * 4096 + step * 512
                term = lax.dot_general(
                    x_refs[i][:, lane : lane + 512], bt, NT, preferred_element_type=F32
                )
                total = term if total is None else total + term
        r_s[i] = total
    for q in range(4):
        columns = [ref[q ^ y] for ref in carry]
        for i in range(n):
            r = r_s[i]
            columns.append(
                jnp.concatenate([r[j * 32 + q * 8 : j * 32 + q * 8 + 8] for j in range(CLS)], axis=0)
            )
        out_ref[q ^ y] = jnp.concatenate(columns, axis=1) if len(columns) > 1 else columns[0]


def stage2(name, xs, picks, bs, carry=(), tokens=()):
    n = len(xs)
    lanes = 32 * n + sum(c.shape[2] for c in carry)
    return pl.pallas_call(
        functools.partial(stage2_kernel, picks, len(bs), len(carry), len(tokens)),
        out_shape=jax.ShapeDtypeStruct((4, 64, lanes), F32),
        in_specs=[spec(pltpu.VMEM)] * (n + len(bs) + len(carry)) + [spec(pl.ANY)] * len(tokens),
        out_specs=spec(pltpu.VMEM),
        scratch_shapes=[pltpu.VMEM((n, 256, 32), F32)],
        compiler_params=params(8),
        cost_estimate=pl.CostEstimate(flops=n * 2**30, transcendentals=0, bytes_accessed=n * 2**18),
        name="stage2_" + name,
    )(*xs, *bs, *carry, *tokens)


def finish_kernel(order, own_ref, r1_ref, r2_ref, r3_ref, out_ref, sum_s, pos_s):
    total = own_ref[0] + r1_ref[...] + r2_ref[...] + r3_ref[...]
    sum_s[0] = total[:, 0:128]
    sum_s[1] = total[:, 128:256]
    for a8 in range(8):
        for k in range(2):
            strip = sum_s[k, pl.ds(a8, CLS, stride=8), :]
            for c in range(4):
                g = order[k * 4 + c]
                pos_s[g * CLS : (g + 1) * CLS, a8 * 32 : (a8 + 1) * 32] = strip[:, c * 32 : (c + 1) * 32]
    out_ref[...] = pos_s[...].T.reshape(8, 32, ROWS)


def finish(order, parts):
    out = pl.pallas_call(
        functools.partial(finish_kernel, order),
        out_shape=jax.ShapeDtypeStruct((8, 32, ROWS), F32),
        in_specs=[spec(pltpu.VMEM)] * 4,
        out_specs=spec(pltpu.VMEM),
        scratch_shapes=[pltpu.VMEM((2, 64, 128), F32), pltpu.VMEM((ROWS, 256), F32)],
        compiler_params=params(6),
        name="finish",
    )(*parts)
    return jnp.transpose(out, (2, 0, 1))


def shards(cholesky, amplitudes, mirror):
    chunks, outgoing = cut_to_send(cholesky, amplitudes)
    quarters = {k: over_y(chunks[k], k) for k in (2, 1, 3)}
    tiles = twist_tiles(mirror, amplitudes, to_sibling(outgoing))
    mine = order_rows((chunks[0], quarters[1], quarters[2], quarters[3]), tiles[1])
    own = (mine, to_sibling(mine))

    x1a, x1b, z0 = over_x(mine, 1, 1), over_x(mine, 3, 3), over_z(mine)
    xc0, xc1, xc2, xc6, xc4 = stage1((0, 1, 2, 6, 4), own, tiles)
    (z0,) = relay((z0,), (xc0,))
    x1, forward = join(x1a, x1b, xc0)
    x1_other, z0_other = to_sibling(x1), to_sibling(z0)
    x2 = over_x(forward, 3, 1)
    zx1 = over_z(x1)
    near = stage2(
        "near",
        (xc0, xc1, xc2, xc6),
        (((0, None), (1, None)), ((2, None), (3, None)), ((4, 0), (5, 0)), ((4, 1), (5, 1))),
        (*own, z0, z0_other, x1, x1_other),
    )
    (x2,) = relay((x2,), (near,))
    x2_other = to_sibling(x2)
    zx2 = over_z(x2)
    xc3, xc7 = stage1((3, 7), own, tiles, (x2,))
    (zx1,) = relay((zx1,), (xc3,))
    zx1_other = to_sibling(zx1)
    (xc5,) = stage1((5,), own, tiles, (zx1, x2_other))
    (zx2,) = relay((zx2,), (xc5,))
    zx2_other = to_sibling(zx2)
    far = stage2("far", (xc4,), (((0, None), (1, None)),), (x2, x2_other), (near,), (zx2,))
    last = stage2(
        "last",
        (xc3, xc7, xc5),
        (((0, 0), (1, 0)), ((0, 1), (1, 1)), ((2, None), (3, None))),
        (zx1, zx1_other, zx2, zx2_other),
        (far,),
    )
    parts = {k: over_y(last[k], k) for k in (2, 1, 3)}
    return finish((0, 1, 2, 6, 4, 3, 7, 5), (last, parts[1], parts[2], parts[3]))


def solution(mesh):
    placed = (P(None, "vir", None), P("occ", None, None, None), P("occ"))
    return jax.shard_map(
        shards, mesh=mesh, in_specs=placed, out_specs=P("occ", "vir", None), check_vma=False
    )
```

```python
import functools

import jax
import jax.numpy as jnp
from jax import lax
from jax.experimental import pallas as pl
from jax.experimental.pallas import tpu as pltpu
from jax.sharding import PartitionSpec as P

IRREPS = 8
CLS = 8
ROWS = IRREPS * CLS
NT = (((1,), (1,)), ((), ()))
BF16 = jnp.bfloat16
F32 = jnp.float32
MIB = 2**20


def permute(value, move):
    pairs = []
    for occ in range(4):
        for vir in range(32):
            to_occ, to_vir = move(occ, vir)
            pairs.append((occ * 32 + vir, to_occ * 32 + to_vir))
    return lax.ppermute(value, ("occ", "vir"), pairs)


def over_y(value, k):
    return permute(value, lambda occ, vir: (occ, vir ^ k))


def over_ring(value, even, odd):
    return permute(value, lambda occ, vir: (occ, vir ^ (odd if occ & 1 else even)))


def over_x(value, even, odd):
    return permute(value, lambda occ, vir: (occ, vir ^ (8 * (odd if occ & 1 else even))))


def over_z(value):
    return permute(value, lambda occ, vir: (occ ^ (2 if occ & 1 else 0), vir ^ 4))


def to_sibling(value):
    return permute(value, lambda occ, vir: (occ ^ 1, vir))


def spec(space):
    return pl.BlockSpec(memory_space=space)


def params(mib):
    return pltpu.CompilerParams(vmem_limit_bytes=mib * MIB)


def place():
    vir, core = lax.axis_index("vir"), lax.axis_index("occ") & 1
    return lax.shift_right_logical(vir, 2), vir & 3, core


def send_kernel(chol_ref, amp_ref, *refs):
    chunks, tiles_ref, chunk_sems, tile_sems = refs[:4], refs[4], refs[5], refs[6]
    h, y, core = place()
    copies = []
    for k, out_ref in enumerate(chunks):
        start = pl.multiple_of((y ^ k) * 512 + core * 256, 256)
        copies.append(pltpu.make_async_copy(chol_ref.at[pl.ds(start, 256)], out_ref, chunk_sems.at[k]))
    for g in range(IRREPS):
        source = amp_ref.at[pl.ds(g * CLS, CLS), h ^ g]
        copies.append(pltpu.make_async_copy(source, tiles_ref.at[g], tile_sems.at[g]))
    for copy in copies:
        copy.start()
    for copy in copies:
        copy.wait()


def cut_to_send(cholesky, amplitudes):
    chunk = jax.ShapeDtypeStruct((256, 128), BF16)
    outs = pl.pallas_call(
        send_kernel,
        out_shape=(chunk,) * 4 + (jax.ShapeDtypeStruct((IRREPS, CLS, 128, 128), BF16),),
        in_specs=[spec(pltpu.HBM)] * 2,
        out_specs=(spec(pltpu.VMEM),) * 5,
        scratch_shapes=[pltpu.SemaphoreType.DMA((4,)), pltpu.SemaphoreType.DMA((IRREPS,))],
        compiler_params=params(46),
        name="cut_to_send",
    )(pltpu.with_memory_space_constraint(cholesky.reshape(2048, 128), pltpu.HBM), amplitudes)
    return outs[:4], outs[4]


def twist_kernel(mirror_ref, amp_ref, received_ref, own_ref, out_ref, sems):
    h = place()[0]
    copies = []
    for g in range(IRREPS):
        source = amp_ref.at[pl.ds(g * CLS, CLS), h]
        copies.append(pltpu.make_async_copy(source, own_ref.at[g], sems.at[g]))
        copies[-1].start()
    for g in range(IRREPS):
        for j in range(CLS):
            out_ref[g, j] = received_ref[g, mirror_ref[g * CLS + j] - g * CLS].T
    for copy in copies:
        copy.wait()


def twist_tiles(mirror, amplitudes, received):
    shape = jax.ShapeDtypeStruct((IRREPS, CLS, 128, 128), BF16)
    return pl.pallas_call(
        twist_kernel,
        out_shape=(shape, shape),
        in_specs=[spec(pltpu.SMEM), spec(pltpu.HBM), spec(pltpu.VMEM)],
        out_specs=(spec(pltpu.VMEM), spec(pltpu.VMEM)),
        scratch_shapes=[pltpu.SemaphoreType.DMA((IRREPS,))],
        compiler_params=params(46),
        name="twist_tiles",
    )(mirror, amplitudes, received)


def rows_kernel(r0_ref, r1_ref, r2_ref, r3_ref, _, out_ref, all_ref):
    y = place()[1]
    for k, ref in enumerate((r0_ref, r1_ref, r2_ref, r3_ref)):
        all_ref[k ^ y] = ref[...]

    def step(i, _):
        start = pl.multiple_of(i * 16, 16)
        parts = [all_ref[q, pl.ds(start, 16), :].astype(F32) for q in range(4)]
        both = [p[0:8] for p in parts] + [p[8:16] for p in parts]
        out_ref[pl.ds(pl.multiple_of(i * 64, 64), 64), :] = jnp.concatenate(both, axis=0).astype(BF16)
        return 0

    lax.fori_loop(0, 16, step, 0, unroll=8)


def order_rows(quarters, token):
    return pl.pallas_call(
        rows_kernel,
        out_shape=jax.ShapeDtypeStruct((1024, 128), BF16),
        in_specs=[spec(pltpu.VMEM)] * 4 + [spec(pl.ANY)],
        out_specs=spec(pltpu.VMEM),
        scratch_shapes=[pltpu.VMEM((4, 256, 128), BF16)],
        compiler_params=params(6),
        name="order_rows",
    )(*quarters, token)


def relay(values, tokens):
    n = len(values)
    outs = pl.pallas_call(
        lambda *refs: None,
        out_shape=tuple(jax.ShapeDtypeStruct(v.shape, v.dtype) for v in values),
        in_specs=[spec(pl.ANY)] * (n + len(tokens)),
        out_specs=tuple(spec(pl.ANY) for _ in values),
        input_output_aliases={i: i for i in range(n)},
        compiler_params=params(1),
        name="relay",
    )(*values, *tokens)
    return outs


def join_kernel(first_ref, second_ref, _, both_ref, chosen_ref):
    core = place()[2]
    both_ref[0] = first_ref[...]
    both_ref[1] = second_ref[...]
    chosen_ref[...] = both_ref[core]


def join(first, second, token):
    return pl.pallas_call(
        join_kernel,
        out_shape=(
            jax.ShapeDtypeStruct((2, *first.shape), first.dtype),
            jax.ShapeDtypeStruct(first.shape, first.dtype),
        ),
        in_specs=[spec(pltpu.VMEM)] * 2 + [spec(pl.ANY)],
        out_specs=(spec(pltpu.VMEM), spec(pltpu.VMEM)),
        compiler_params=params(4),
        name="join",
    )(first, second, token)


def stage1_kernel(classes, tokens, mine_ref, other_ref, t_ref, tp_ref, *refs):
    for x_ref, g in zip(refs[tokens:], classes):
        for pair in range(4):
            j0, j1 = 2 * pair, 2 * pair + 1
            upper = jnp.concatenate([t_ref[g, j0], t_ref[g, j1]], axis=1)
            lower = jnp.concatenate([tp_ref[g, j0], tp_ref[g, j1]], axis=1)
            weights = jnp.concatenate([upper, lower], axis=0)
            for part in range(4):
                own_ref = (mine_ref, other_ref)[part // 2]
                own = own_ref[(part % 2) * 512 : (part % 2 + 1) * 512, :]
                lhs = jnp.concatenate([own, own], axis=1)
                x = jnp.dot(lhs, weights, preferred_element_type=F32).astype(BF16)
                for k in range(2):
                    j = 2 * pair + k
                    for l in range(16):
                        lane = (part * 16 + l) * 128
                        x_ref[j * 32 : (j + 1) * 32, lane : lane + 128] = x[
                            l * 32 : (l + 1) * 32, k * 128 : (k + 1) * 128
                        ]


def stage1(classes, own, tiles, tokens=()):
    n = len(classes)
    return pl.pallas_call(
        functools.partial(stage1_kernel, classes, len(tokens)),
        out_shape=tuple(jax.ShapeDtypeStruct((256, 8192), BF16) for _ in classes),
        in_specs=[spec(pltpu.VMEM)] * 4 + [spec(pl.ANY)] * len(tokens),
        out_specs=tuple(spec(pltpu.VMEM) for _ in classes),
        compiler_params=params(8),
        cost_estimate=pl.CostEstimate(flops=n * 2**30, transcendentals=0, bytes_accessed=n * 2**18),
        name="stage1_" + "_".join(str(g) for g in classes),
    )(*own, *tiles, *tokens)


def stage2_kernel(picks, n_b, carried, tokens, *refs):
    n = len(picks)
    x_refs, refs = refs[:n], refs[n:]
    b_refs, refs = refs[:n_b], refs[n_b:]
    carry, refs = refs[:carried], refs[carried:]
    *outs, r_s = refs[tokens:]
    out_ref = outs[0]
    _, y, core = place()
    for i, halves in enumerate(picks):
        total = None
        for half, (at, index) in enumerate(halves):
            b_ref = b_refs[at] if index is None else b_refs[at].at[index]
            for step in range(8):
                b = b_ref[step * 128 : (step + 1) * 128, :]
                bt = jnp.concatenate([b[l * 32 : (l + 1) * 32] for l in range(4)], axis=1)
                lane = half * 4096 + step * 512
                term = lax.dot_general(
                    x_refs[i][:, lane : lane + 512], bt, NT, preferred_element_type=F32
                )
                total = term if total is None else total + term
        r_s[i] = total
    for q in range(4):
        columns = [ref[q ^ y] for ref in carry]
        for i in range(n):
            r = r_s[i]
            columns.append(
                jnp.concatenate([r[j * 32 + q * 8 : j * 32 + q * 8 + 8] for j in range(CLS)], axis=0)
            )
        out_ref[q ^ y] = jnp.concatenate(columns, axis=1) if len(columns) > 1 else columns[0]
    if len(outs) > 1:
        outs[1][0] = out_ref[1 + 2 * core]
        outs[1][1] = out_ref[2]
        outs[2][...] = out_ref[3 - 2 * core]


def stage2(name, xs, picks, bs, carry=(), tokens=(), split=False):
    n = len(xs)
    lanes = 32 * n + sum(c.shape[2] for c in carry)
    shapes = tuple(
        jax.ShapeDtypeStruct(shape, F32)
        for shape in ((4, 64, lanes), (2, 64, lanes), (64, lanes))[: 3 if split else 1]
    )
    outs = pl.pallas_call(
        functools.partial(stage2_kernel, picks, len(bs), len(carry), len(tokens)),
        out_shape=shapes,
        in_specs=[spec(pltpu.VMEM)] * (n + len(bs) + len(carry)) + [spec(pl.ANY)] * len(tokens),
        out_specs=tuple(spec(pltpu.VMEM) for _ in shapes),
        scratch_shapes=[pltpu.VMEM((n, 256, 32), F32)],
        compiler_params=params(8),
        cost_estimate=pl.CostEstimate(flops=n * 2**30, transcendentals=0, bytes_accessed=n * 2**18),
        name="stage2_" + name,
    )(*xs, *bs, *carry, *tokens)
    return outs if split else outs[0]


def pass_kernel(held_ref, first_ref, out_ref):
    out_ref[...] = held_ref[...] + first_ref[1]


def pass_on(held, first):
    return pl.pallas_call(
        pass_kernel,
        out_shape=jax.ShapeDtypeStruct(held.shape, F32),
        in_specs=[spec(pltpu.VMEM)] * 2,
        out_specs=spec(pltpu.VMEM),
        compiler_params=params(2),
        name="pass_on",
    )(held, first)


def finish_kernel(order, own_ref, first_ref, second_ref, out_ref, sum_s, pos_s):
    total = own_ref[0] + first_ref[0] + second_ref[...]
    sum_s[0] = total[:, 0:128]
    sum_s[1] = total[:, 128:256]
    for a8 in range(8):
        for k in range(2):
            strip = sum_s[k, pl.ds(a8, CLS, stride=8), :]
            for c in range(4):
                g = order[k * 4 + c]
                pos_s[g * CLS : (g + 1) * CLS, a8 * 32 : (a8 + 1) * 32] = strip[:, c * 32 : (c + 1) * 32]
    out_ref[...] = pos_s[...].T.reshape(8, 32, ROWS)


def finish(order, parts):
    out = pl.pallas_call(
        functools.partial(finish_kernel, order),
        out_shape=jax.ShapeDtypeStruct((8, 32, ROWS), F32),
        in_specs=[spec(pltpu.VMEM)] * 3,
        out_specs=spec(pltpu.VMEM),
        scratch_shapes=[pltpu.VMEM((2, 64, 128), F32), pltpu.VMEM((ROWS, 256), F32)],
        compiler_params=params(6),
        name="finish",
    )(*parts)
    return jnp.transpose(out, (2, 0, 1))


def shards(cholesky, amplitudes, mirror):
    chunks, outgoing = cut_to_send(cholesky, amplitudes)
    quarters = {k: over_y(chunks[k], k) for k in (2, 1, 3)}
    tiles = twist_tiles(mirror, amplitudes, to_sibling(outgoing))
    mine = order_rows((chunks[0], quarters[1], quarters[2], quarters[3]), tiles[1])
    own = (mine, to_sibling(mine))

    x1a, x1b, z0 = over_x(mine, 1, 1), over_x(mine, 3, 3), over_z(mine)
    xc0, xc1, xc2, xc6, xc4 = stage1((0, 1, 2, 6, 4), own, tiles)
    (z0,) = relay((z0,), (xc0,))
    x1, forward = join(x1a, x1b, xc0)
    x1_other, z0_other = to_sibling(x1), to_sibling(z0)
    x2 = over_x(forward, 3, 1)
    zx1 = over_z(x1)
    near = stage2(
        "near",
        (xc0, xc1, xc2, xc6),
        (((0, None), (1, None)), ((2, None), (3, None)), ((4, 0), (5, 0)), ((4, 1), (5, 1))),
        (*own, z0, z0_other, x1, x1_other),
    )
    (x2,) = relay((x2,), (near,))
    x2_other = to_sibling(x2)
    zx2 = over_z(x2)
    xc3, xc7 = stage1((3, 7), own, tiles, (x2,))
    (zx1,) = relay((zx1,), (xc3,))
    zx1_other = to_sibling(zx1)
    (xc5,) = stage1((5,), own, tiles, (zx1, x2_other))
    (zx2,) = relay((zx2,), (xc5,))
    zx2_other = to_sibling(zx2)
    far = stage2("far", (xc4,), (((0, None), (1, None)),), (x2, x2_other), (near,), (zx2,))
    last, offer, held = stage2(
        "last",
        (xc3, xc7, xc5),
        (((0, 0), (1, 0)), ((0, 1), (1, 1)), ((2, None), (3, None))),
        (zx1, zx1_other, zx2, zx2_other),
        (far,),
        split=True,
    )
    first = over_ring(offer, 1, 3)
    second = over_ring(pass_on(held, first), 3, 1)
    return finish((0, 1, 2, 6, 4, 3, 7, 5), (last, first, second))


def solution(mesh):
    placed = (P(None, "vir", None), P("occ", None, None, None), P("occ"))
    return jax.shard_map(
        shards, mesh=mesh, in_specs=placed, out_specs=P("occ", "vir", None), check_vma=False
    )
```

```python
import functools

import jax
import jax.numpy as jnp
from jax import lax
from jax.experimental import pallas as pl
from jax.experimental.pallas import tpu as pltpu
from jax.sharding import PartitionSpec as P

IRREPS = 8
CLS = 8
ROWS = IRREPS * CLS
NT = (((1,), (1,)), ((), ()))
BF16 = jnp.bfloat16
F32 = jnp.float32
MIB = 2**20


def permute(value, move):
    pairs = []
    for occ in range(4):
        for vir in range(32):
            to_occ, to_vir = move(occ, vir)
            pairs.append((occ * 32 + vir, to_occ * 32 + to_vir))
    return lax.ppermute(value, ("occ", "vir"), pairs)


def over_y(value, k):
    return permute(value, lambda occ, vir: (occ, vir ^ k))


def over_x(value, even, odd):
    return permute(value, lambda occ, vir: (occ, vir ^ (8 * (odd if occ & 1 else even))))


def over_z(value):
    return permute(value, lambda occ, vir: (occ ^ (2 if occ & 1 else 0), vir ^ 4))


def to_sibling(value):
    return permute(value, lambda occ, vir: (occ ^ 1, vir))


def spec(space):
    return pl.BlockSpec(memory_space=space)


def params(mib):
    return pltpu.CompilerParams(vmem_limit_bytes=mib * MIB)


def place():
    vir, core = lax.axis_index("vir"), lax.axis_index("occ") & 1
    return lax.shift_right_logical(vir, 2), vir & 3, core


def send_kernel(chol_ref, amp_ref, *refs):
    chunks, tiles_ref, chunk_sems, tile_sems = refs[:4], refs[4], refs[5], refs[6]
    h, y, core = place()
    copies = []
    for k, out_ref in enumerate(chunks):
        start = pl.multiple_of((y ^ k) * 512 + core * 256, 256)
        copies.append(pltpu.make_async_copy(chol_ref.at[pl.ds(start, 256)], out_ref, chunk_sems.at[k]))
    for g in range(IRREPS):
        source = amp_ref.at[pl.ds(g * CLS, CLS), h ^ g]
        copies.append(pltpu.make_async_copy(source, tiles_ref.at[g], tile_sems.at[g]))
    for copy in copies:
        copy.start()
    for copy in copies:
        copy.wait()


def cut_to_send(cholesky, amplitudes):
    chunk = jax.ShapeDtypeStruct((256, 128), BF16)
    outs = pl.pallas_call(
        send_kernel,
        out_shape=(chunk,) * 4 + (jax.ShapeDtypeStruct((IRREPS, CLS, 128, 128), BF16),),
        in_specs=[spec(pltpu.HBM)] * 2,
        out_specs=(spec(pltpu.VMEM),) * 5,
        scratch_shapes=[pltpu.SemaphoreType.DMA((4,)), pltpu.SemaphoreType.DMA((IRREPS,))],
        compiler_params=params(46),
        name="cut_to_send",
    )(pltpu.with_memory_space_constraint(cholesky.reshape(2048, 128), pltpu.HBM), amplitudes)
    return outs[:4], outs[4]


def twist_kernel(mirror_ref, amp_ref, received_ref, own_ref, out_ref, sems):
    h = place()[0]
    copies = []
    for g in range(IRREPS):
        source = amp_ref.at[pl.ds(g * CLS, CLS), h]
        copies.append(pltpu.make_async_copy(source, own_ref.at[g], sems.at[g]))
        copies[-1].start()
    for g in range(IRREPS):
        for j in range(CLS):
            out_ref[g, j] = received_ref[g, mirror_ref[g * CLS + j] - g * CLS].T
    for copy in copies:
        copy.wait()


def twist_tiles(mirror, amplitudes, received):
    shape = jax.ShapeDtypeStruct((IRREPS, CLS, 128, 128), BF16)
    return pl.pallas_call(
        twist_kernel,
        out_shape=(shape, shape),
        in_specs=[spec(pltpu.SMEM), spec(pltpu.HBM), spec(pltpu.VMEM)],
        out_specs=(spec(pltpu.VMEM), spec(pltpu.VMEM)),
        scratch_shapes=[pltpu.SemaphoreType.DMA((IRREPS,))],
        compiler_params=params(46),
        name="twist_tiles",
    )(mirror, amplitudes, received)


def rows_kernel(r0_ref, r2_ref, r1_ref, r3_ref, _, out_ref, all_ref):
    y = place()[1]
    for k, ref in enumerate((r0_ref, r1_ref, r2_ref, r3_ref)):
        all_ref[k ^ y] = ref[...]

    def step(i, _):
        start = pl.multiple_of(i * 16, 16)
        parts = [all_ref[q, pl.ds(start, 16), :].astype(F32) for q in range(4)]
        both = [p[0:8] for p in parts] + [p[8:16] for p in parts]
        out_ref[pl.ds(pl.multiple_of(i * 64, 64), 64), :] = jnp.concatenate(both, axis=0).astype(BF16)
        return 0

    lax.fori_loop(0, 16, step, 0, unroll=8)


def order_rows(quarters, token):
    return pl.pallas_call(
        rows_kernel,
        out_shape=jax.ShapeDtypeStruct((1024, 128), BF16),
        in_specs=[spec(pltpu.VMEM)] * 4 + [spec(pl.ANY)],
        out_specs=spec(pltpu.VMEM),
        scratch_shapes=[pltpu.VMEM((4, 256, 128), BF16)],
        compiler_params=params(6),
        name="order_rows",
    )(*quarters, token)


def relay(values, tokens):
    n = len(values)
    outs = pl.pallas_call(
        lambda *refs: None,
        out_shape=tuple(jax.ShapeDtypeStruct(v.shape, v.dtype) for v in values),
        in_specs=[spec(pl.ANY)] * (n + len(tokens)),
        out_specs=tuple(spec(pl.ANY) for _ in values),
        input_output_aliases={i: i for i in range(n)},
        compiler_params=params(1),
        name="relay",
    )(*values, *tokens)
    return outs


def join_kernel(first_ref, second_ref, _, both_ref, chosen_ref):
    core = place()[2]
    both_ref[0] = first_ref[...]
    both_ref[1] = second_ref[...]
    chosen_ref[...] = both_ref[core]


def join(first, second, token):
    return pl.pallas_call(
        join_kernel,
        out_shape=(
            jax.ShapeDtypeStruct((2, *first.shape), first.dtype),
            jax.ShapeDtypeStruct(first.shape, first.dtype),
        ),
        in_specs=[spec(pltpu.VMEM)] * 2 + [spec(pl.ANY)],
        out_specs=(spec(pltpu.VMEM), spec(pltpu.VMEM)),
        compiler_params=params(4),
        name="join",
    )(first, second, token)


def stage1_kernel(classes, tokens, mine_ref, other_ref, t_ref, tp_ref, *refs):
    for x_ref, g in zip(refs[tokens:], classes):
        for pair in range(4):
            j0, j1 = 2 * pair, 2 * pair + 1
            upper = jnp.concatenate([t_ref[g, j0], t_ref[g, j1]], axis=1)
            lower = jnp.concatenate([tp_ref[g, j0], tp_ref[g, j1]], axis=1)
            weights = jnp.concatenate([upper, lower], axis=0)
            for part in range(4):
                own_ref = (mine_ref, other_ref)[part // 2]
                own = own_ref[(part % 2) * 512 : (part % 2 + 1) * 512, :]
                lhs = jnp.concatenate([own, own], axis=1)
                x = jnp.dot(lhs, weights, preferred_element_type=F32).astype(BF16)
                for k in range(2):
                    j = 2 * pair + k
                    for l in range(16):
                        lane = (part * 16 + l) * 128
                        x_ref[j * 32 : (j + 1) * 32, lane : lane + 128] = x[
                            l * 32 : (l + 1) * 32, k * 128 : (k + 1) * 128
                        ]


def stage1(classes, own, tiles, tokens=()):
    n = len(classes)
    return pl.pallas_call(
        functools.partial(stage1_kernel, classes, len(tokens)),
        out_shape=tuple(jax.ShapeDtypeStruct((256, 8192), BF16) for _ in classes),
        in_specs=[spec(pltpu.VMEM)] * 4 + [spec(pl.ANY)] * len(tokens),
        out_specs=tuple(spec(pltpu.VMEM) for _ in classes),
        compiler_params=params(8),
        cost_estimate=pl.CostEstimate(flops=n * 2**30, transcendentals=0, bytes_accessed=n * 2**18),
        name="stage1_" + "_".join(str(g) for g in classes),
    )(*own, *tiles, *tokens)


def stage2_kernel(picks, n_b, carried, tokens, *refs):
    n = len(picks)
    x_refs, refs = refs[:n], refs[n:]
    b_refs, refs = refs[:n_b], refs[n_b:]
    carry, refs = refs[:carried], refs[carried:]
    out_ref, r_s = refs[tokens:]
    y = place()[1]
    for i, halves in enumerate(picks):
        total = None
        for half, (at, index) in enumerate(halves):
            b_ref = b_refs[at] if index is None else b_refs[at].at[index]
            for step in range(8):
                b = b_ref[step * 128 : (step + 1) * 128, :]
                bt = jnp.concatenate([b[l * 32 : (l + 1) * 32] for l in range(4)], axis=1)
                lane = half * 4096 + step * 512
                term = lax.dot_general(
                    x_refs[i][:, lane : lane + 512], bt, NT, preferred_element_type=F32
                )
                total = term if total is None else total + term
        r_s[i] = total
    for q in range(4):
        columns = [ref[q ^ y] for ref in carry]
        for i in range(n):
            r = r_s[i]
            columns.append(
                jnp.concatenate([r[j * 32 + q * 8 : j * 32 + q * 8 + 8] for j in range(CLS)], axis=0)
            )
        out_ref[q ^ y] = jnp.concatenate(columns, axis=1) if len(columns) > 1 else columns[0]


def stage2(name, xs, picks, bs, carry=(), tokens=()):
    n = len(xs)
    lanes = 32 * n + sum(c.shape[2] for c in carry)
    return pl.pallas_call(
        functools.partial(stage2_kernel, picks, len(bs), len(carry), len(tokens)),
        out_shape=jax.ShapeDtypeStruct((4, 64, lanes), F32),
        in_specs=[spec(pltpu.VMEM)] * (n + len(bs) + len(carry)) + [spec(pl.ANY)] * len(tokens),
        out_specs=spec(pltpu.VMEM),
        scratch_shapes=[pltpu.VMEM((n, 256, 32), F32)],
        compiler_params=params(8),
        cost_estimate=pl.CostEstimate(flops=n * 2**30, transcendentals=0, bytes_accessed=n * 2**18),
        name="stage2_" + name,
    )(*xs, *bs, *carry, *tokens)


def finish_kernel(order, own_ref, r1_ref, r2_ref, r3_ref, out_ref, sum_s, pos_s):
    total = own_ref[0] + r1_ref[...] + r2_ref[...] + r3_ref[...]
    sum_s[0] = total[:, 0:128]
    sum_s[1] = total[:, 128:256]
    for a8 in range(8):
        for k in range(2):
            strip = sum_s[k, pl.ds(a8, CLS, stride=8), :]
            for c in range(4):
                g = order[k * 4 + c]
                pos_s[g * CLS : (g + 1) * CLS, a8 * 32 : (a8 + 1) * 32] = strip[:, c * 32 : (c + 1) * 32]
    out_ref[...] = pos_s[...].T.reshape(8, 32, ROWS)


def finish(order, parts):
    out = pl.pallas_call(
        functools.partial(finish_kernel, order),
        out_shape=jax.ShapeDtypeStruct((8, 32, ROWS), F32),
        in_specs=[spec(pltpu.VMEM)] * 4,
        out_specs=spec(pltpu.VMEM),
        scratch_shapes=[pltpu.VMEM((2, 64, 128), F32), pltpu.VMEM((ROWS, 256), F32)],
        compiler_params=params(6),
        name="finish",
    )(*parts)
    return jnp.transpose(out, (2, 0, 1))


def shards(cholesky, amplitudes, mirror):
    chunks, outgoing = cut_to_send(cholesky, amplitudes)
    quarters = {k: over_y(chunks[k], k) for k in (2, 1, 3)}
    tiles = twist_tiles(mirror, amplitudes, to_sibling(outgoing))
    mine = order_rows((chunks[0], quarters[2], quarters[1], quarters[3]), tiles[1])
    own = (mine, to_sibling(mine))

    x1a, x1b, z0 = over_x(mine, 1, 1), over_x(mine, 3, 3), over_z(mine)
    xc0, xc1, xc2, xc6, xc4 = stage1((0, 1, 2, 6, 4), own, tiles)
    (z0,) = relay((z0,), (xc0,))
    x1, forward = join(x1a, x1b, xc0)
    x1_other, z0_other = to_sibling(x1), to_sibling(z0)
    x2 = over_x(forward, 3, 1)
    zx1 = over_z(x1)
    near = stage2(
        "near",
        (xc0, xc1, xc2, xc6),
        (((0, None), (1, None)), ((2, None), (3, None)), ((4, 0), (5, 0)), ((4, 1), (5, 1))),
        (*own, z0, z0_other, x1, x1_other),
    )
    (x2,) = relay((x2,), (near,))
    x2_other = to_sibling(x2)
    zx2 = over_z(x2)
    xc3, xc7 = stage1((3, 7), own, tiles, (x2,))
    (zx1,) = relay((zx1,), (xc3,))
    zx1_other = to_sibling(zx1)
    (xc5,) = stage1((5,), own, tiles, (zx1, x2_other))
    (zx2,) = relay((zx2,), (xc5,))
    zx2_other = to_sibling(zx2)
    far = stage2("far", (xc4,), (((0, None), (1, None)),), (x2, x2_other), (near,), (zx2,))
    last = stage2(
        "last",
        (xc3, xc7, xc5),
        (((0, 0), (1, 0)), ((0, 1), (1, 1)), ((2, None), (3, None))),
        (zx1, zx1_other, zx2, zx2_other),
        (far,),
    )
    parts = {k: over_y(last[k], k) for k in (2, 1, 3)}
    return finish((0, 1, 2, 6, 4, 3, 7, 5), (last, parts[2], parts[1], parts[3]))


def solution(mesh):
    placed = (P(None, "vir", None), P("occ", None, None, None), P("occ"))
    return jax.shard_map(
        shards, mesh=mesh, in_specs=placed, out_specs=P("occ", "vir", None), check_vma=False
    )
```

```python
import functools

import jax
import jax.numpy as jnp
from jax import lax
from jax.experimental import pallas as pl
from jax.experimental.pallas import tpu as pltpu
from jax.sharding import PartitionSpec as P

IRREPS = 8
CLS = 8
ROWS = IRREPS * CLS
NT = (((1,), (1,)), ((), ()))
BF16 = jnp.bfloat16
F32 = jnp.float32
MIB = 2**20


def permute(value, move):
    pairs = []
    for occ in range(4):
        for vir in range(32):
            to_occ, to_vir = move(occ, vir)
            pairs.append((occ * 32 + vir, to_occ * 32 + to_vir))
    return lax.ppermute(value, ("occ", "vir"), pairs)


def over_y(value, k):
    return permute(value, lambda occ, vir: (occ, vir ^ k))


def over_x(value, even, odd):
    return permute(value, lambda occ, vir: (occ, vir ^ (8 * (odd if occ & 1 else even))))


def over_z(value):
    return permute(value, lambda occ, vir: (occ ^ (2 if occ & 1 else 0), vir ^ 4))


def to_sibling(value):
    return permute(value, lambda occ, vir: (occ ^ 1, vir))


def spec(space):
    return pl.BlockSpec(memory_space=space)


def params(mib):
    return pltpu.CompilerParams(vmem_limit_bytes=mib * MIB)


def place():
    vir, core = lax.axis_index("vir"), lax.axis_index("occ") & 1
    return lax.shift_right_logical(vir, 2), vir & 3, core


def send_kernel(chol_ref, amp_ref, *refs):
    chunks, tiles_ref, chunk_sems, tile_sems = refs[:4], refs[4], refs[5], refs[6]
    h, y, core = place()
    copies = []
    for k, out_ref in enumerate(chunks):
        start = pl.multiple_of((y ^ k) * 512 + core * 256, 256)
        copies.append(pltpu.make_async_copy(chol_ref.at[pl.ds(start, 256)], out_ref, chunk_sems.at[k]))
    for g in range(IRREPS):
        source = amp_ref.at[pl.ds(g * CLS, CLS), h ^ g]
        copies.append(pltpu.make_async_copy(source, tiles_ref.at[g], tile_sems.at[g]))
    for copy in copies:
        copy.start()
    for copy in copies:
        copy.wait()


def cut_to_send(cholesky, amplitudes):
    chunk = jax.ShapeDtypeStruct((256, 128), BF16)
    outs = pl.pallas_call(
        send_kernel,
        out_shape=(chunk,) * 4 + (jax.ShapeDtypeStruct((IRREPS, CLS, 128, 128), BF16),),
        in_specs=[spec(pltpu.HBM)] * 2,
        out_specs=(spec(pltpu.VMEM),) * 5,
        scratch_shapes=[pltpu.SemaphoreType.DMA((4,)), pltpu.SemaphoreType.DMA((IRREPS,))],
        compiler_params=params(46),
        name="cut_to_send",
    )(pltpu.with_memory_space_constraint(cholesky.reshape(2048, 128), pltpu.HBM), amplitudes)
    return outs[:4], outs[4]


def twist_kernel(mirror_ref, amp_ref, received_ref, own_ref, out_ref, sems):
    h = place()[0]
    copies = []
    for g in range(IRREPS):
        source = amp_ref.at[pl.ds(g * CLS, CLS), h]
        copies.append(pltpu.make_async_copy(source, own_ref.at[g], sems.at[g]))
        copies[-1].start()
    for g in range(IRREPS):
        for j in range(CLS):
            out_ref[g, j] = received_ref[g, mirror_ref[g * CLS + j] - g * CLS].T
    for copy in copies:
        copy.wait()


def twist_tiles(mirror, amplitudes, received):
    shape = jax.ShapeDtypeStruct((IRREPS, CLS, 128, 128), BF16)
    return pl.pallas_call(
        twist_kernel,
        out_shape=(shape, shape),
        in_specs=[spec(pltpu.SMEM), spec(pltpu.HBM), spec(pltpu.VMEM)],
        out_specs=(spec(pltpu.VMEM), spec(pltpu.VMEM)),
        scratch_shapes=[pltpu.SemaphoreType.DMA((IRREPS,))],
        compiler_params=params(46),
        name="twist_tiles",
    )(mirror, amplitudes, received)


def rows_kernel(r0_ref, r2_ref, r1_ref, r3_ref, _, out_ref, all_ref):
    y = place()[1]
    for k, ref in enumerate((r0_ref, r1_ref, r2_ref, r3_ref)):
        all_ref[k ^ y] = ref[...]

    def step(i, _):
        start = pl.multiple_of(i * 16, 16)
        parts = [all_ref[q, pl.ds(start, 16), :].astype(F32) for q in range(4)]
        both = [p[0:8] for p in parts] + [p[8:16] for p in parts]
        out_ref[pl.ds(pl.multiple_of(i * 64, 64), 64), :] = jnp.concatenate(both, axis=0).astype(BF16)
        return 0

    lax.fori_loop(0, 16, step, 0, unroll=8)


def order_rows(quarters, token):
    return pl.pallas_call(
        rows_kernel,
        out_shape=jax.ShapeDtypeStruct((1024, 128), BF16),
        in_specs=[spec(pltpu.VMEM)] * 4 + [spec(pl.ANY)],
        out_specs=spec(pltpu.VMEM),
        scratch_shapes=[pltpu.VMEM((4, 256, 128), BF16)],
        compiler_params=params(6),
        name="order_rows",
    )(*quarters, token)


def relay(values, tokens):
    n = len(values)
    outs = pl.pallas_call(
        lambda *refs: None,
        out_shape=tuple(jax.ShapeDtypeStruct(v.shape, v.dtype) for v in values),
        in_specs=[spec(pl.ANY)] * (n + len(tokens)),
        out_specs=tuple(spec(pl.ANY) for _ in values),
        input_output_aliases={i: i for i in range(n)},
        compiler_params=params(1),
        name="relay",
    )(*values, *tokens)
    return outs


def join_kernel(first_ref, second_ref, _, both_ref, chosen_ref):
    core = place()[2]
    both_ref[0] = first_ref[...]
    both_ref[1] = second_ref[...]
    chosen_ref[...] = both_ref[core]


def join(first, second, token):
    return pl.pallas_call(
        join_kernel,
        out_shape=(
            jax.ShapeDtypeStruct((2, *first.shape), first.dtype),
            jax.ShapeDtypeStruct(first.shape, first.dtype),
        ),
        in_specs=[spec(pltpu.VMEM)] * 2 + [spec(pl.ANY)],
        out_specs=(spec(pltpu.VMEM), spec(pltpu.VMEM)),
        compiler_params=params(4),
        name="join",
    )(first, second, token)


def stage1_kernel(classes, tokens, mine_ref, other_ref, t_ref, tp_ref, *refs):
    for x_ref, g in zip(refs[tokens:], classes):
        for pair in range(4):
            j0, j1 = 2 * pair, 2 * pair + 1
            upper = jnp.concatenate([t_ref[g, j0], t_ref[g, j1]], axis=1)
            lower = jnp.concatenate([tp_ref[g, j0], tp_ref[g, j1]], axis=1)
            weights = jnp.concatenate([upper, lower], axis=0)
            for part in range(16):
                own_ref = (mine_ref, other_ref)[part // 8]
                own = own_ref[(part % 8) * 128 : (part % 8 + 1) * 128, :]
                lhs = jnp.concatenate([own, own], axis=1)
                x = jnp.dot(lhs, weights, preferred_element_type=F32).astype(BF16)
                for k in range(2):
                    j = 2 * pair + k
                    for l in range(4):
                        lane = (part * 4 + l) * 128
                        x_ref[j * 32 : (j + 1) * 32, lane : lane + 128] = x[
                            l * 32 : (l + 1) * 32, k * 128 : (k + 1) * 128
                        ]


def stage1(classes, own, tiles, tokens=(), weight=1):
    n = len(classes)
    return pl.pallas_call(
        functools.partial(stage1_kernel, classes, len(tokens)),
        out_shape=tuple(jax.ShapeDtypeStruct((256, 8192), BF16) for _ in classes),
        in_specs=[spec(pltpu.VMEM)] * 4 + [spec(pl.ANY)] * len(tokens),
        out_specs=tuple(spec(pltpu.VMEM) for _ in classes),
        compiler_params=params(8),
        cost_estimate=pl.CostEstimate(flops=int(n * weight * 2**30), transcendentals=0, bytes_accessed=2**10),
        name="stage1_" + "_".join(str(g) for g in classes),
    )(*own, *tiles, *tokens)


def stage2_kernel(picks, n_b, carried, tokens, *refs):
    n = len(picks)
    x_refs, refs = refs[:n], refs[n:]
    b_refs, refs = refs[:n_b], refs[n_b:]
    carry, refs = refs[:carried], refs[carried:]
    out_ref, r_s = refs[tokens:]
    y = place()[1]
    for i, halves in enumerate(picks):
        total = None
        for half, (at, index) in enumerate(halves):
            b_ref = b_refs[at] if index is None else b_refs[at].at[index]
            for step in range(16):
                b = b_ref[step * 64 : (step + 1) * 64, :]
                bt = jnp.concatenate([b[0:32], b[32:64]], axis=1)
                lane = half * 4096 + step * 256
                term = lax.dot_general(
                    x_refs[i][:, lane : lane + 256], bt, NT, preferred_element_type=F32
                )
                total = term if total is None else total + term
        r_s[i] = total
    for q in range(4):
        columns = [ref[q ^ y] for ref in carry]
        for i in range(n):
            r = r_s[i]
            columns.append(
                jnp.concatenate([r[j * 32 + q * 8 : j * 32 + q * 8 + 8] for j in range(CLS)], axis=0)
            )
        out_ref[q ^ y] = jnp.concatenate(columns, axis=1) if len(columns) > 1 else columns[0]


def stage2(name, xs, picks, bs, carry=(), tokens=(), weight=1):
    n = len(xs)
    lanes = 32 * n + sum(c.shape[2] for c in carry)
    return pl.pallas_call(
        functools.partial(stage2_kernel, picks, len(bs), len(carry), len(tokens)),
        out_shape=jax.ShapeDtypeStruct((4, 64, lanes), F32),
        in_specs=[spec(pltpu.VMEM)] * (n + len(bs) + len(carry)) + [spec(pl.ANY)] * len(tokens),
        out_specs=spec(pltpu.VMEM),
        scratch_shapes=[pltpu.VMEM((n, 256, 32), F32)],
        compiler_params=params(8),
        cost_estimate=pl.CostEstimate(flops=int(n * weight * 2**30), transcendentals=0, bytes_accessed=2**10),
        name="stage2_" + name,
    )(*xs, *bs, *carry, *tokens)


def finish_kernel(order, own_ref, r1_ref, r2_ref, r3_ref, out_ref, sum_s, pos_s):
    total = own_ref[0] + r1_ref[...] + r2_ref[...] + r3_ref[...]
    sum_s[0] = total[:, 0:128]
    sum_s[1] = total[:, 128:256]
    for a8 in range(8):
        for k in range(2):
            strip = sum_s[k, pl.ds(a8, CLS, stride=8), :]
            for c in range(4):
                g = order[k * 4 + c]
                pos_s[g * CLS : (g + 1) * CLS, a8 * 32 : (a8 + 1) * 32] = strip[:, c * 32 : (c + 1) * 32]
    out_ref[...] = pos_s[...].T.reshape(8, 32, ROWS)


def finish(order, parts):
    out = pl.pallas_call(
        functools.partial(finish_kernel, order),
        out_shape=jax.ShapeDtypeStruct((8, 32, ROWS), F32),
        in_specs=[spec(pltpu.VMEM)] * 4,
        out_specs=spec(pltpu.VMEM),
        scratch_shapes=[pltpu.VMEM((2, 64, 128), F32), pltpu.VMEM((ROWS, 256), F32)],
        compiler_params=params(6),
        name="finish",
    )(*parts)
    return jnp.transpose(out, (2, 0, 1))


SA, NEAR, SB, SC = 1, 0, 4, 1


def shards(cholesky, amplitudes, mirror):
    chunks, outgoing = cut_to_send(cholesky, amplitudes)
    quarters = {k: over_y(chunks[k], k) for k in (2, 1, 3)}
    tiles = twist_tiles(mirror, amplitudes, to_sibling(outgoing))
    mine = order_rows((chunks[0], quarters[2], quarters[1], quarters[3]), tiles[1])
    own = (mine, to_sibling(mine))

    x1a, x1b, z0 = over_x(mine, 1, 1), over_x(mine, 3, 3), over_z(mine)
    xc0, xc1, xc2, xc6, xc4 = stage1((0, 1, 2, 6, 4), own, tiles, (), SA)
    (z0,) = relay((z0,), (xc0,))
    x1, forward = join(x1a, x1b, xc0)
    x1_other, z0_other = to_sibling(x1), to_sibling(z0)
    x2 = over_x(forward, 3, 1)
    zx1 = over_z(x1)
    near = stage2(
        "near",
        (xc0, xc1, xc2, xc6),
        (((0, None), (1, None)), ((2, None), (3, None)), ((4, 0), (5, 0)), ((4, 1), (5, 1))),
        (*own, z0, z0_other, x1, x1_other),
        weight=NEAR,
    )
    (x2,) = relay((x2,), (near,))
    x2_other = to_sibling(x2)
    zx2 = over_z(x2)
    xc3, xc7 = stage1((3, 7), own, tiles, (x2,), SB)
    (zx1,) = relay((zx1,), (xc3,))
    zx1_other = to_sibling(zx1)
    (xc5,) = stage1((5,), own, tiles, (zx1, x2_other), SC)
    (zx2,) = relay((zx2,), (xc5,))
    zx2_other = to_sibling(zx2)
    far = stage2("far", (xc4,), (((0, None), (1, None)),), (x2, x2_other), (near,), (zx2,))
    last = stage2(
        "last",
        (xc3, xc7, xc5),
        (((0, 0), (1, 0)), ((0, 1), (1, 1)), ((2, None), (3, None))),
        (zx1, zx1_other, zx2, zx2_other),
        (far,),
    )
    parts = {k: over_y(last[k], k) for k in (2, 1, 3)}
    return finish((0, 1, 2, 6, 4, 3, 7, 5), (last, parts[2], parts[1], parts[3]))


def solution(mesh):
    placed = (P(None, "vir", None), P("occ", None, None, None), P("occ"))
    return jax.shard_map(
        shards, mesh=mesh, in_specs=placed, out_specs=P("occ", "vir", None), check_vma=False
    )
```

```python
import functools

import jax
import jax.numpy as jnp
from jax import lax
from jax.experimental import pallas as pl
from jax.experimental.pallas import tpu as pltpu
from jax.sharding import PartitionSpec as P

IRREPS = 8
CLS = 8
ROWS = IRREPS * CLS
NT = (((1,), (1,)), ((), ()))
BF16 = jnp.bfloat16
F32 = jnp.float32
MIB = 2**20


def permute(value, move):
    pairs = []
    for occ in range(4):
        for vir in range(32):
            to_occ, to_vir = move(occ, vir)
            pairs.append((occ * 32 + vir, to_occ * 32 + to_vir))
    return lax.ppermute(value, ("occ", "vir"), pairs)


def over_y(value, k):
    return permute(value, lambda occ, vir: (occ, vir ^ k))


def over_x(value, even, odd):
    return permute(value, lambda occ, vir: (occ, vir ^ (8 * (odd if occ & 1 else even))))


def over_z(value):
    return permute(value, lambda occ, vir: (occ ^ (2 if occ & 1 else 0), vir ^ 4))


def to_sibling(value):
    return permute(value, lambda occ, vir: (occ ^ 1, vir))


def spec(space):
    return pl.BlockSpec(memory_space=space)


def params(mib):
    return pltpu.CompilerParams(vmem_limit_bytes=mib * MIB)


def place():
    vir, core = lax.axis_index("vir"), lax.axis_index("occ") & 1
    return lax.shift_right_logical(vir, 2), vir & 3, core


def send_kernel(chol_ref, amp_ref, *refs):
    chunks, tiles_ref, chunk_sems, tile_sems = refs[:4], refs[4], refs[5], refs[6]
    h, y, core = place()
    copies = []
    for k, out_ref in enumerate(chunks):
        start = pl.multiple_of((y ^ k) * 512 + core * 256, 256)
        copies.append(pltpu.make_async_copy(chol_ref.at[pl.ds(start, 256)], out_ref, chunk_sems.at[k]))
    for g in range(IRREPS):
        source = amp_ref.at[pl.ds(g * CLS, CLS), h ^ g]
        copies.append(pltpu.make_async_copy(source, tiles_ref.at[g], tile_sems.at[g]))
    for copy in copies:
        copy.start()
    for copy in copies:
        copy.wait()


def cut_to_send(cholesky, amplitudes):
    chunk = jax.ShapeDtypeStruct((256, 128), BF16)
    outs = pl.pallas_call(
        send_kernel,
        out_shape=(chunk,) * 4 + (jax.ShapeDtypeStruct((IRREPS, CLS, 128, 128), BF16),),
        in_specs=[spec(pltpu.HBM)] * 2,
        out_specs=(spec(pltpu.VMEM),) * 5,
        scratch_shapes=[pltpu.SemaphoreType.DMA((4,)), pltpu.SemaphoreType.DMA((IRREPS,))],
        compiler_params=params(46),
        name="cut_to_send",
    )(pltpu.with_memory_space_constraint(cholesky.reshape(2048, 128), pltpu.HBM), amplitudes)
    return outs[:4], outs[4]


def twist_kernel(mirror_ref, amp_ref, received_ref, own_ref, out_ref, sems):
    h = place()[0]
    copies = []
    for g in range(IRREPS):
        source = amp_ref.at[pl.ds(g * CLS, CLS), h]
        copies.append(pltpu.make_async_copy(source, own_ref.at[g], sems.at[g]))
        copies[-1].start()
    for g in range(IRREPS):
        for j in range(CLS):
            out_ref[g, j] = received_ref[g, mirror_ref[g * CLS + j] - g * CLS].T
    for copy in copies:
        copy.wait()


def twist_tiles(mirror, amplitudes, received):
    shape = jax.ShapeDtypeStruct((IRREPS, CLS, 128, 128), BF16)
    return pl.pallas_call(
        twist_kernel,
        out_shape=(shape, shape),
        in_specs=[spec(pltpu.SMEM), spec(pltpu.HBM), spec(pltpu.VMEM)],
        out_specs=(spec(pltpu.VMEM), spec(pltpu.VMEM)),
        scratch_shapes=[pltpu.SemaphoreType.DMA((IRREPS,))],
        compiler_params=params(46),
        name="twist_tiles",
    )(mirror, amplitudes, received)


def rows_kernel(r0_ref, r2_ref, r1_ref, r3_ref, _, out_ref, all_ref):
    y = place()[1]
    for k, ref in enumerate((r0_ref, r1_ref, r2_ref, r3_ref)):
        all_ref[k ^ y] = ref[...]

    def step(i, _):
        start = pl.multiple_of(i * 16, 16)
        parts = [all_ref[q, pl.ds(start, 16), :].astype(F32) for q in range(4)]
        both = [p[0:8] for p in parts] + [p[8:16] for p in parts]
        out_ref[pl.ds(pl.multiple_of(i * 64, 64), 64), :] = jnp.concatenate(both, axis=0).astype(BF16)
        return 0

    lax.fori_loop(0, 16, step, 0, unroll=8)


def order_rows(quarters, token):
    return pl.pallas_call(
        rows_kernel,
        out_shape=jax.ShapeDtypeStruct((1024, 128), BF16),
        in_specs=[spec(pltpu.VMEM)] * 4 + [spec(pl.ANY)],
        out_specs=spec(pltpu.VMEM),
        scratch_shapes=[pltpu.VMEM((4, 256, 128), BF16)],
        compiler_params=params(6),
        name="order_rows",
    )(*quarters, token)


def relay(values, tokens):
    n = len(values)
    outs = pl.pallas_call(
        lambda *refs: None,
        out_shape=tuple(jax.ShapeDtypeStruct(v.shape, v.dtype) for v in values),
        in_specs=[spec(pl.ANY)] * (n + len(tokens)),
        out_specs=tuple(spec(pl.ANY) for _ in values),
        input_output_aliases={i: i for i in range(n)},
        compiler_params=params(1),
        name="relay",
    )(*values, *tokens)
    return outs


def join_kernel(first_ref, second_ref, _, both_ref, chosen_ref):
    core = place()[2]
    both_ref[0] = first_ref[...]
    both_ref[1] = second_ref[...]
    chosen_ref[...] = both_ref[core]


def join(first, second, token):
    return pl.pallas_call(
        join_kernel,
        out_shape=(
            jax.ShapeDtypeStruct((2, *first.shape), first.dtype),
            jax.ShapeDtypeStruct(first.shape, first.dtype),
        ),
        in_specs=[spec(pltpu.VMEM)] * 2 + [spec(pl.ANY)],
        out_specs=(spec(pltpu.VMEM), spec(pltpu.VMEM)),
        compiler_params=params(4),
        name="join",
    )(first, second, token)


def stage1_kernel(work, tokens, mine_ref, *refs):
    both = any(half == 1 for _, half in work)
    other_ref, refs = (refs[0], refs[1:]) if both else (None, refs)
    t_ref, tp_ref, x_refs = refs[0], refs[1], refs[2 + tokens :]
    for g in dict.fromkeys(g for g, _ in work):
        for pair in range(4):
            j0, j1 = 2 * pair, 2 * pair + 1
            upper = jnp.concatenate([t_ref[g, j0], t_ref[g, j1]], axis=1)
            lower = jnp.concatenate([tp_ref[g, j0], tp_ref[g, j1]], axis=1)
            weights = jnp.concatenate([upper, lower], axis=0)
            for x_ref, (own_g, half) in zip(x_refs, work):
                if own_g != g:
                    continue
                own_ref = (mine_ref, other_ref)[half]
                for part in range(8):
                    own = own_ref[part * 128 : (part + 1) * 128, :]
                    lhs = jnp.concatenate([own, own], axis=1)
                    x = jnp.dot(lhs, weights, preferred_element_type=F32).astype(BF16)
                    for k in range(2):
                        j = 2 * pair + k
                        for l in range(4):
                            lane = (part * 4 + l) * 128
                            x_ref[j * 32 : (j + 1) * 32, lane : lane + 128] = x[
                                l * 32 : (l + 1) * 32, k * 128 : (k + 1) * 128
                            ]


def stage1(work, own, tiles, tokens=(), weight=1):
    if all(half == 0 for _, half in work):
        own = own[:1]
    flops = int(len(work) * weight * 2**29)
    return pl.pallas_call(
        functools.partial(stage1_kernel, work, len(tokens)),
        out_shape=tuple(jax.ShapeDtypeStruct((256, 4096), BF16) for _ in work),
        in_specs=[spec(pltpu.VMEM)] * (len(own) + 2) + [spec(pl.ANY)] * len(tokens),
        out_specs=tuple(spec(pltpu.VMEM) for _ in work),
        compiler_params=params(8),
        cost_estimate=pl.CostEstimate(flops=flops, transcendentals=0, bytes_accessed=2**10),
        name="stage1_" + "_".join(str(g) for g in dict.fromkeys(g for g, _ in work)),
    )(*own, *tiles, *tokens)


def halves(*classes):
    return tuple((g, half) for g in classes for half in range(2))


def stage2_kernel(picks, n_b, carried, tokens, *refs):
    n = len(picks)
    x_refs, refs = refs[: 2 * n], refs[2 * n :]
    b_refs, refs = refs[:n_b], refs[n_b:]
    carry, refs = refs[:carried], refs[carried:]
    out_ref, r_s = refs[tokens:]
    y = place()[1]
    for i, halves in enumerate(picks):
        total = None
        for half, (at, index) in enumerate(halves):
            b_ref = b_refs[at] if index is None else b_refs[at].at[index]
            for step in range(16):
                b = b_ref[step * 64 : (step + 1) * 64, :]
                bt = jnp.concatenate([b[0:32], b[32:64]], axis=1)
                x = x_refs[2 * i + half][:, step * 256 : (step + 1) * 256]
                term = lax.dot_general(x, bt, NT, preferred_element_type=F32)
                total = term if total is None else total + term
        r_s[i] = total
    for q in range(4):
        columns = [ref[q ^ y] for ref in carry]
        for i in range(n):
            r = r_s[i]
            columns.append(
                jnp.concatenate([r[j * 32 + q * 8 : j * 32 + q * 8 + 8] for j in range(CLS)], axis=0)
            )
        out_ref[q ^ y] = jnp.concatenate(columns, axis=1) if len(columns) > 1 else columns[0]


def stage2(name, xs, picks, bs, carry=(), tokens=(), weight=1):
    n = len(picks)
    lanes = 32 * n + sum(c.shape[2] for c in carry)
    return pl.pallas_call(
        functools.partial(stage2_kernel, picks, len(bs), len(carry), len(tokens)),
        out_shape=jax.ShapeDtypeStruct((4, 64, lanes), F32),
        in_specs=[spec(pltpu.VMEM)] * (2 * n + len(bs) + len(carry)) + [spec(pl.ANY)] * len(tokens),
        out_specs=spec(pltpu.VMEM),
        scratch_shapes=[pltpu.VMEM((n, 256, 32), F32)],
        compiler_params=params(8),
        cost_estimate=pl.CostEstimate(flops=int(n * weight * 2**30), transcendentals=0, bytes_accessed=2**10),
        name="stage2_" + name,
    )(*xs, *bs, *carry, *tokens)


def finish_kernel(order, own_ref, r1_ref, r2_ref, r3_ref, out_ref, sum_s, pos_s):
    total = own_ref[0] + r1_ref[...] + r2_ref[...] + r3_ref[...]
    sum_s[0] = total[:, 0:128]
    sum_s[1] = total[:, 128:256]
    for a8 in range(8):
        for k in range(2):
            strip = sum_s[k, pl.ds(a8, CLS, stride=8), :]
            for c in range(4):
                g = order[k * 4 + c]
                pos_s[g * CLS : (g + 1) * CLS, a8 * 32 : (a8 + 1) * 32] = strip[:, c * 32 : (c + 1) * 32]
    out_ref[...] = pos_s[...].T.reshape(8, 32, ROWS)


def finish(order, parts):
    out = pl.pallas_call(
        functools.partial(finish_kernel, order),
        out_shape=jax.ShapeDtypeStruct((8, 32, ROWS), F32),
        in_specs=[spec(pltpu.VMEM)] * 4,
        out_specs=spec(pltpu.VMEM),
        scratch_shapes=[pltpu.VMEM((2, 64, 128), F32), pltpu.VMEM((ROWS, 256), F32)],
        compiler_params=params(6),
        name="finish",
    )(*parts)
    return jnp.transpose(out, (2, 0, 1))


FAST, SLOW = 0, 8


def shards(cholesky, amplitudes, mirror):
    chunks, outgoing = cut_to_send(cholesky, amplitudes)
    quarters = {k: over_y(chunks[k], k) for k in (2, 1, 3)}
    tiles = twist_tiles(mirror, amplitudes, to_sibling(outgoing))
    mine = order_rows((chunks[0], quarters[2], quarters[1], quarters[3]), tiles[1])
    own = (mine, to_sibling(mine))

    x1a, x1b, z0 = over_x(mine, 1, 1), over_x(mine, 3, 3), over_z(mine)
    x0m, x0o, *xs = stage1(halves(0, 1, 2, 6, 4), own, tiles)
    (z0,) = relay((z0,), (x0o,))
    x1, forward = join(x1a, x1b, x0o)
    x2 = over_x(forward, 3, 1)
    zx1 = over_z(x1)
    x1_other, z0_other = to_sibling(x1), to_sibling(z0)
    x37 = stage1(halves(3, 7), own, tiles, (forward,), FAST)
    self0 = stage2("self", (x0m, x0o), (((0, None), (1, None)),), own, (), (x37[0],), FAST)
    (x2,) = relay((x2,), (self0,))
    zx2 = over_z(x2)
    x2_other = to_sibling(x2)
    near = stage2(
        "near",
        xs[0:6],
        (((0, None), (1, None)), ((2, 0), (3, 0)), ((2, 1), (3, 1))),
        (z0, z0_other, x1, x1_other),
        (self0,),
        (x2,),
        SLOW,
    )
    (zx1,) = relay((zx1,), (near,))
    zx1_other = to_sibling(zx1)
    x5 = stage1(halves(5), own, tiles, (zx1,))
    (zx2,) = relay((zx2,), (x5[0],))
    zx2_other = to_sibling(zx2)
    far = stage2("far", xs[6:8], (((0, None), (1, None)),), (x2, x2_other), (near,), (zx2,))
    last = stage2(
        "last",
        (*x37, *x5),
        (((0, 0), (1, 0)), ((0, 1), (1, 1)), ((2, None), (3, None))),
        (zx1, zx1_other, zx2, zx2_other),
        (far,),
    )
    parts = {k: over_y(last[k], k) for k in (2, 1, 3)}
    return finish((0, 1, 2, 6, 4, 3, 7, 5), (last, parts[2], parts[1], parts[3]))


def solution(mesh):
    placed = (P(None, "vir", None), P("occ", None, None, None), P("occ"))
    return jax.shard_map(
        shards, mesh=mesh, in_specs=placed, out_specs=P("occ", "vir", None), check_vma=False
    )
```

```python
import functools

import jax
import jax.numpy as jnp
from jax import lax
from jax.experimental import pallas as pl
from jax.experimental.pallas import tpu as pltpu
from jax.sharding import PartitionSpec as P

IRREPS = 8
CLS = 8
ROWS = IRREPS * CLS
NT = (((1,), (1,)), ((), ()))
BF16 = jnp.bfloat16
F32 = jnp.float32
MIB = 2**20


def permute(value, move):
    pairs = []
    for occ in range(4):
        for vir in range(32):
            to_occ, to_vir = move(occ, vir)
            pairs.append((occ * 32 + vir, to_occ * 32 + to_vir))
    return lax.ppermute(value, ("occ", "vir"), pairs)


def over_y(value, k):
    return permute(value, lambda occ, vir: (occ, vir ^ k))


def over_x(value, even, odd):
    return permute(value, lambda occ, vir: (occ, vir ^ (8 * (odd if occ & 1 else even))))


def over_z(value):
    return permute(value, lambda occ, vir: (occ ^ (2 if occ & 1 else 0), vir ^ 4))


def to_sibling(value):
    return permute(value, lambda occ, vir: (occ ^ 1, vir))


def spec(space):
    return pl.BlockSpec(memory_space=space)


def params(mib):
    return pltpu.CompilerParams(vmem_limit_bytes=mib * MIB)


def place():
    vir, core = lax.axis_index("vir"), lax.axis_index("occ") & 1
    return lax.shift_right_logical(vir, 2), vir & 3, core


def send_kernel(chol_ref, amp_ref, *refs):
    chunks, tiles_ref, chunk_sems, tile_sems = refs[:4], refs[4], refs[5], refs[6]
    h, y, core = place()
    copies = []
    for k, out_ref in enumerate(chunks):
        start = pl.multiple_of((y ^ k) * 512 + core * 256, 256)
        copies.append(pltpu.make_async_copy(chol_ref.at[pl.ds(start, 256)], out_ref, chunk_sems.at[k]))
    for g in range(IRREPS):
        source = amp_ref.at[pl.ds(g * CLS, CLS), h ^ g]
        copies.append(pltpu.make_async_copy(source, tiles_ref.at[g], tile_sems.at[g]))
    for copy in copies:
        copy.start()
    for copy in copies:
        copy.wait()


def cut_to_send(cholesky, amplitudes):
    chunk = jax.ShapeDtypeStruct((256, 128), BF16)
    outs = pl.pallas_call(
        send_kernel,
        out_shape=(chunk,) * 4 + (jax.ShapeDtypeStruct((IRREPS, CLS, 128, 128), BF16),),
        in_specs=[spec(pltpu.HBM)] * 2,
        out_specs=(spec(pltpu.VMEM),) * 5,
        scratch_shapes=[pltpu.SemaphoreType.DMA((4,)), pltpu.SemaphoreType.DMA((IRREPS,))],
        compiler_params=params(46),
        name="cut_to_send",
    )(pltpu.with_memory_space_constraint(cholesky.reshape(2048, 128), pltpu.HBM), amplitudes)
    return outs[:4], outs[4]


def twist_kernel(mirror_ref, amp_ref, received_ref, own_ref, out_ref, sems):
    h = place()[0]
    copies = []
    for g in range(IRREPS):
        source = amp_ref.at[pl.ds(g * CLS, CLS), h]
        copies.append(pltpu.make_async_copy(source, own_ref.at[g], sems.at[g]))
        copies[-1].start()
    for g in range(IRREPS):
        for j in range(CLS):
            out_ref[g, j] = received_ref[g, mirror_ref[g * CLS + j] - g * CLS].T
    for copy in copies:
        copy.wait()


def twist_tiles(mirror, amplitudes, received):
    shape = jax.ShapeDtypeStruct((IRREPS, CLS, 128, 128), BF16)
    return pl.pallas_call(
        twist_kernel,
        out_shape=(shape, shape),
        in_specs=[spec(pltpu.SMEM), spec(pltpu.HBM), spec(pltpu.VMEM)],
        out_specs=(spec(pltpu.VMEM), spec(pltpu.VMEM)),
        scratch_shapes=[pltpu.SemaphoreType.DMA((IRREPS,))],
        compiler_params=params(46),
        name="twist_tiles",
    )(mirror, amplitudes, received)


def rows_kernel(r0_ref, r2_ref, r1_ref, r3_ref, _, out_ref, all_ref):
    y = place()[1]
    for k, ref in enumerate((r0_ref, r1_ref, r2_ref, r3_ref)):
        all_ref[k ^ y] = ref[...]

    def step(i, _):
        start = pl.multiple_of(i * 16, 16)
        parts = [all_ref[q, pl.ds(start, 16), :].astype(F32) for q in range(4)]
        both = [p[0:8] for p in parts] + [p[8:16] for p in parts]
        out_ref[pl.ds(pl.multiple_of(i * 64, 64), 64), :] = jnp.concatenate(both, axis=0).astype(BF16)
        return 0

    lax.fori_loop(0, 16, step, 0, unroll=8)


def order_rows(quarters, token):
    return pl.pallas_call(
        rows_kernel,
        out_shape=jax.ShapeDtypeStruct((1024, 128), BF16),
        in_specs=[spec(pltpu.VMEM)] * 4 + [spec(pl.ANY)],
        out_specs=spec(pltpu.VMEM),
        scratch_shapes=[pltpu.VMEM((4, 256, 128), BF16)],
        compiler_params=params(6),
        name="order_rows",
    )(*quarters, token)


def relay(values, tokens):
    n = len(values)
    outs = pl.pallas_call(
        lambda *refs: None,
        out_shape=tuple(jax.ShapeDtypeStruct(v.shape, v.dtype) for v in values),
        in_specs=[spec(pl.ANY)] * (n + len(tokens)),
        out_specs=tuple(spec(pl.ANY) for _ in values),
        input_output_aliases={i: i for i in range(n)},
        compiler_params=params(1),
        name="relay",
    )(*values, *tokens)
    return outs


def join_kernel(mine_ref, other_ref, out_ref):
    out_ref[0] = mine_ref[...]
    out_ref[1] = other_ref[...]


def join(mine, other):
    return pl.pallas_call(
        join_kernel,
        out_shape=jax.ShapeDtypeStruct((2, *mine.shape), mine.dtype),
        in_specs=[spec(pltpu.VMEM)] * 2,
        out_specs=spec(pltpu.VMEM),
        compiler_params=params(4),
        name="join",
    )(mine, other)


def first_kernel(value_ref, _, out_ref, first_ref):
    first_ref[...] = value_ref[0]


def with_first(value, token):
    return pl.pallas_call(
        first_kernel,
        out_shape=(
            jax.ShapeDtypeStruct(value.shape, value.dtype),
            jax.ShapeDtypeStruct(value.shape[1:], value.dtype),
        ),
        in_specs=[spec(pltpu.VMEM), spec(pl.ANY)],
        out_specs=(spec(pl.ANY), spec(pltpu.VMEM)),
        input_output_aliases={0: 0},
        compiler_params=params(4),
        name="with_first",
    )(value, token)


def on_core(pair):
    return pair[0] if pair[0] == pair[1] else jnp.where(place()[2] == 1, pair[1], pair[0])


def stage1_kernel(work, tokens, mine_ref, *refs):
    both = any(half == 1 for _, half in work)
    other_ref, refs = (refs[0], refs[1:]) if both else (None, refs)
    t_ref, tp_ref, x_refs = refs[0], refs[1], refs[2 + tokens :]
    for slot in dict.fromkeys(slot for slot, _ in work):
        g = on_core(slot)
        for pair in range(4):
            j0, j1 = 2 * pair, 2 * pair + 1
            upper = jnp.concatenate([t_ref[g, j0], t_ref[g, j1]], axis=1)
            lower = jnp.concatenate([tp_ref[g, j0], tp_ref[g, j1]], axis=1)
            weights = jnp.concatenate([upper, lower], axis=0)
            for x_ref, (its_slot, half) in zip(x_refs, work):
                if its_slot != slot:
                    continue
                own_ref = (mine_ref, other_ref)[half]
                for part in range(8):
                    own = own_ref[part * 128 : (part + 1) * 128, :]
                    lhs = jnp.concatenate([own, own], axis=1)
                    x = jnp.dot(lhs, weights, preferred_element_type=F32).astype(BF16)
                    for k in range(2):
                        j = 2 * pair + k
                        for l in range(4):
                            lane = (part * 4 + l) * 128
                            x_ref[j * 32 : (j + 1) * 32, lane : lane + 128] = x[
                                l * 32 : (l + 1) * 32, k * 128 : (k + 1) * 128
                            ]


def stage1(work, own, tiles, tokens=(), weight=1):
    if all(half == 0 for _, half in work):
        own = own[:1]
    flops = int(len(work) * weight * 2**29)
    return pl.pallas_call(
        functools.partial(stage1_kernel, work, len(tokens)),
        out_shape=tuple(jax.ShapeDtypeStruct((256, 4096), BF16) for _ in work),
        in_specs=[spec(pltpu.VMEM)] * (len(own) + 2) + [spec(pl.ANY)] * len(tokens),
        out_specs=tuple(spec(pltpu.VMEM) for _ in work),
        compiler_params=params(8),
        cost_estimate=pl.CostEstimate(flops=flops, transcendentals=0, bytes_accessed=2**10),
        name="stage1_" + "_".join(str(slot[0]) for slot in dict.fromkeys(slot for slot, _ in work)),
    )(*own, *tiles, *tokens)


def halves(*slots):
    return tuple((slot, half) for slot in slots for half in range(2))


def stage2_kernel(picks, n_b, carried, tokens, *refs):
    n = len(picks)
    x_refs, refs = refs[: 2 * n], refs[2 * n :]
    b_refs, refs = refs[:n_b], refs[n_b:]
    carry, refs = refs[:carried], refs[carried:]
    out_ref, r_s = refs[tokens:]
    y = place()[1]
    for i, halves in enumerate(picks):
        total = None
        for half, (at, index) in enumerate(halves):
            b_ref = b_refs[at] if index is None else b_refs[at].at[index]
            for step in range(16):
                b = b_ref[step * 64 : (step + 1) * 64, :]
                bt = jnp.concatenate([b[0:32], b[32:64]], axis=1)
                x = x_refs[2 * i + half][:, step * 256 : (step + 1) * 256]
                term = lax.dot_general(x, bt, NT, preferred_element_type=F32)
                total = term if total is None else total + term
        r_s[i] = total
    for q in range(4):
        columns = [ref[q ^ y] for ref in carry]
        for i in range(n):
            r = r_s[i]
            columns.append(
                jnp.concatenate([r[j * 32 + q * 8 : j * 32 + q * 8 + 8] for j in range(CLS)], axis=0)
            )
        out_ref[q ^ y] = jnp.concatenate(columns, axis=1) if len(columns) > 1 else columns[0]


def stage2(name, xs, picks, bs, carry=(), tokens=(), weight=1):
    n = len(picks)
    lanes = 32 * n + sum(c.shape[2] for c in carry)
    return pl.pallas_call(
        functools.partial(stage2_kernel, picks, len(bs), len(carry), len(tokens)),
        out_shape=jax.ShapeDtypeStruct((4, 64, lanes), F32),
        in_specs=[spec(pltpu.VMEM)] * (2 * n + len(bs) + len(carry)) + [spec(pl.ANY)] * len(tokens),
        out_specs=spec(pltpu.VMEM),
        scratch_shapes=[pltpu.VMEM((n, 256, 32), F32)],
        compiler_params=params(8),
        cost_estimate=pl.CostEstimate(flops=int(n * weight * 2**30), transcendentals=0, bytes_accessed=2**10),
        name="stage2_" + name,
    )(*xs, *bs, *carry, *tokens)


def finish_kernel(order, own_ref, r1_ref, r2_ref, r3_ref, out_ref, sum_s, pos_s):
    total = own_ref[0] + r1_ref[...] + r2_ref[...] + r3_ref[...]
    sum_s[0] = total[:, 0:128]
    sum_s[1] = total[:, 128:256]
    for a8 in range(8):
        for k in range(2):
            strip = sum_s[k, pl.ds(a8, CLS, stride=8), :]
            for c in range(4):
                rows = pl.ds(pl.multiple_of(on_core(order[k * 4 + c]) * CLS, CLS), CLS)
                pos_s[rows, a8 * 32 : (a8 + 1) * 32] = strip[:, c * 32 : (c + 1) * 32]
    out_ref[...] = pos_s[...].T.reshape(8, 32, ROWS)


def finish(order, parts):
    out = pl.pallas_call(
        functools.partial(finish_kernel, order),
        out_shape=jax.ShapeDtypeStruct((8, 32, ROWS), F32),
        in_specs=[spec(pltpu.VMEM)] * 4,
        out_specs=spec(pltpu.VMEM),
        scratch_shapes=[pltpu.VMEM((2, 64, 128), F32), pltpu.VMEM((ROWS, 256), F32)],
        compiler_params=params(6),
        name="finish",
    )(*parts)
    return jnp.transpose(out, (2, 0, 1))


FAST, SLOW = 0, 8


def shards(cholesky, amplitudes, mirror):
    chunks, outgoing = cut_to_send(cholesky, amplitudes)
    quarters = {k: over_y(chunks[k], k) for k in (2, 1, 3)}
    tiles = twist_tiles(mirror, amplitudes, to_sibling(outgoing))
    mine = order_rows((chunks[0], quarters[2], quarters[1], quarters[3]), tiles[1])
    own = (mine, to_sibling(mine))

    c0, c1, c4, c5 = ((g, g) for g in (0, 1, 4, 5))
    c26, c62, c37, c73 = (2, 6), (6, 2), (3, 7), (7, 3)
    z0 = over_z(mine)
    x1 = over_x(join(*own), 1, 3)
    x0m, x0o, *xs = stage1(halves(c0, c1, c26, c62, c4, c37), own, tiles)
    (z0,) = relay((z0,), (x0o,))
    x1, x1_first = with_first(x1, x0o)
    x2 = over_x(x1_first, 3, 1)
    zx1 = over_z(x1)
    x1_other, z0_other = to_sibling(x1), to_sibling(z0)
    x73 = stage1(halves(c73), own, tiles, (x1_first,), FAST)
    self0 = stage2("self", (x0m, x0o), (((0, None), (1, None)),), own, (), (x73[0],), FAST)
    (x2,) = relay((x2,), (self0,))
    zx2 = over_z(x2)
    x2_other = to_sibling(x2)
    near = stage2(
        "near",
        xs[0:6],
        (((0, None), (1, None)), ((2, 0), (2, 1)), ((3, 1), (3, 0))),
        (z0, z0_other, x1, x1_other),
        (self0,),
        (x2,),
        SLOW,
    )
    (zx1,) = relay((zx1,), (near,))
    zx1_other = to_sibling(zx1)
    x5 = stage1(halves(c5), own, tiles, (zx1,))
    (zx2,) = relay((zx2,), (x5[0],))
    zx2_other = to_sibling(zx2)
    far = stage2("far", xs[6:8], (((0, None), (1, None)),), (x2, x2_other), (near,), (zx2,))
    last = stage2(
        "last",
        (*xs[8:10], *x73, *x5),
        (((0, 0), (0, 1)), ((1, 1), (1, 0)), ((2, None), (3, None))),
        (zx1, zx1_other, zx2, zx2_other),
        (far,),
    )
    parts = {k: over_y(last[k], k) for k in (2, 1, 3)}
    return finish((c0, c1, c26, c62, c4, c37, c73, c5), (last, parts[2], parts[1], parts[3]))


def solution(mesh):
    placed = (P(None, "vir", None), P("occ", None, None, None), P("occ"))
    return jax.shard_map(
        shards, mesh=mesh, in_specs=placed, out_specs=P("occ", "vir", None), check_vma=False
    )
```

```python
import functools

import jax
import jax.numpy as jnp
from jax import lax
from jax.experimental import pallas as pl
from jax.experimental.pallas import tpu as pltpu
from jax.sharding import PartitionSpec as P

IRREPS = 8
CLS = 8
ROWS = IRREPS * CLS
NT = (((1,), (1,)), ((), ()))
BF16 = jnp.bfloat16
F32 = jnp.float32
MIB = 2**20


def permute(value, move):
    pairs = []
    for occ in range(4):
        for vir in range(32):
            to_occ, to_vir = move(occ, vir)
            pairs.append((occ * 32 + vir, to_occ * 32 + to_vir))
    return lax.ppermute(value, ("occ", "vir"), pairs)


def over_y(value, k):
    return permute(value, lambda occ, vir: (occ, vir ^ k))


def over_x(value, even, odd):
    return permute(value, lambda occ, vir: (occ, vir ^ (8 * (odd if occ & 1 else even))))


def over_z(value):
    return permute(value, lambda occ, vir: (occ ^ (2 if occ & 1 else 0), vir ^ 4))


def to_sibling(value):
    return permute(value, lambda occ, vir: (occ ^ 1, vir))


def spec(space):
    return pl.BlockSpec(memory_space=space)


def params(mib):
    return pltpu.CompilerParams(vmem_limit_bytes=mib * MIB)


def place():
    vir, core = lax.axis_index("vir"), lax.axis_index("occ") & 1
    return lax.shift_right_logical(vir, 2), vir & 3, core


def send_kernel(chol_ref, amp_ref, *refs):
    chunks, tiles_ref, chunk_sems, tile_sems = refs[:4], refs[4], refs[5], refs[6]
    h, y, core = place()
    copies = []
    for k, out_ref in enumerate(chunks):
        start = pl.multiple_of((y ^ k) * 512 + core * 256, 256)
        copies.append(pltpu.make_async_copy(chol_ref.at[pl.ds(start, 256)], out_ref, chunk_sems.at[k]))
    for g in range(IRREPS):
        source = amp_ref.at[pl.ds(g * CLS, CLS), h ^ g]
        copies.append(pltpu.make_async_copy(source, tiles_ref.at[g], tile_sems.at[g]))
    for copy in copies:
        copy.start()
    for copy in copies:
        copy.wait()


def cut_to_send(cholesky, amplitudes):
    chunk = jax.ShapeDtypeStruct((256, 128), BF16)
    outs = pl.pallas_call(
        send_kernel,
        out_shape=(chunk,) * 4 + (jax.ShapeDtypeStruct((IRREPS, CLS, 128, 128), BF16),),
        in_specs=[spec(pltpu.HBM)] * 2,
        out_specs=(spec(pltpu.VMEM),) * 5,
        scratch_shapes=[pltpu.SemaphoreType.DMA((4,)), pltpu.SemaphoreType.DMA((IRREPS,))],
        compiler_params=params(46),
        name="cut_to_send",
    )(pltpu.with_memory_space_constraint(cholesky.reshape(2048, 128), pltpu.HBM), amplitudes)
    return outs[:4], outs[4]


def twist_kernel(mirror_ref, amp_ref, received_ref, own_ref, out_ref, sems):
    h = place()[0]
    copies = []
    for g in range(IRREPS):
        source = amp_ref.at[pl.ds(g * CLS, CLS), h]
        copies.append(pltpu.make_async_copy(source, own_ref.at[g], sems.at[g]))
        copies[-1].start()
    for g in range(IRREPS):
        for j in range(CLS):
            out_ref[g, j] = received_ref[g, mirror_ref[g * CLS + j] - g * CLS].T
    for copy in copies:
        copy.wait()


def twist_tiles(mirror, amplitudes, received):
    shape = jax.ShapeDtypeStruct((IRREPS, CLS, 128, 128), BF16)
    return pl.pallas_call(
        twist_kernel,
        out_shape=(shape, shape),
        in_specs=[spec(pltpu.SMEM), spec(pltpu.HBM), spec(pltpu.VMEM)],
        out_specs=(spec(pltpu.VMEM), spec(pltpu.VMEM)),
        scratch_shapes=[pltpu.SemaphoreType.DMA((IRREPS,))],
        compiler_params=params(46),
        name="twist_tiles",
    )(mirror, amplitudes, received)


def rows_kernel(r0_ref, r2_ref, r1_ref, r3_ref, _, out_ref, all_ref):
    y = place()[1]
    for k, ref in enumerate((r0_ref, r1_ref, r2_ref, r3_ref)):
        all_ref[k ^ y] = ref[...]

    def step(i, _):
        start = pl.multiple_of(i * 16, 16)
        parts = [all_ref[q, pl.ds(start, 16), :].astype(F32) for q in range(4)]
        both = [p[0:8] for p in parts] + [p[8:16] for p in parts]
        out_ref[pl.ds(pl.multiple_of(i * 64, 64), 64), :] = jnp.concatenate(both, axis=0).astype(BF16)
        return 0

    lax.fori_loop(0, 16, step, 0, unroll=8)


def order_rows(quarters, token):
    return pl.pallas_call(
        rows_kernel,
        out_shape=jax.ShapeDtypeStruct((1024, 128), BF16),
        in_specs=[spec(pltpu.VMEM)] * 4 + [spec(pl.ANY)],
        out_specs=spec(pltpu.VMEM),
        scratch_shapes=[pltpu.VMEM((4, 256, 128), BF16)],
        compiler_params=params(6),
        name="order_rows",
    )(*quarters, token)


def relay(values, tokens):
    n = len(values)
    outs = pl.pallas_call(
        lambda *refs: None,
        out_shape=tuple(jax.ShapeDtypeStruct(v.shape, v.dtype) for v in values),
        in_specs=[spec(pl.ANY)] * (n + len(tokens)),
        out_specs=tuple(spec(pl.ANY) for _ in values),
        input_output_aliases={i: i for i in range(n)},
        compiler_params=params(1),
        cost_estimate=pl.CostEstimate(flops=0, transcendentals=0, bytes_accessed=0),
        name="relay",
    )(*values, *tokens)
    return outs


def join_kernel(first_ref, second_ref, third_ref, _, pair_ref, all_ref):
    for i, ref in enumerate((first_ref, second_ref)):
        pair_ref[i] = ref[...]
        all_ref[i] = ref[...]
    all_ref[2] = third_ref[...]


def join(first, second, third, token):
    return pl.pallas_call(
        join_kernel,
        out_shape=tuple(jax.ShapeDtypeStruct((n, *first.shape), first.dtype) for n in (2, 3)),
        in_specs=[spec(pltpu.VMEM)] * 3 + [spec(pl.ANY)],
        out_specs=(spec(pltpu.VMEM), spec(pltpu.VMEM)),
        compiler_params=params(4),
        cost_estimate=pl.CostEstimate(flops=0, transcendentals=0, bytes_accessed=0),
        name="join",
    )(first, second, third, token)


def on_core(pair):
    return pair[0] if pair[0] == pair[1] else jnp.where(place()[2] == 1, pair[1], pair[0])


def stage1_kernel(work, tokens, mine_ref, *refs):
    both = any(half == 1 for _, half in work)
    other_ref, refs = (refs[0], refs[1:]) if both else (None, refs)
    t_ref, tp_ref, x_refs = refs[0], refs[1], refs[2 + tokens :]
    for slot in dict.fromkeys(slot for slot, _ in work):
        g = on_core(slot)
        for pair in range(4):
            j0, j1 = 2 * pair, 2 * pair + 1
            upper = jnp.concatenate([t_ref[g, j0], t_ref[g, j1]], axis=1)
            lower = jnp.concatenate([tp_ref[g, j0], tp_ref[g, j1]], axis=1)
            weights = jnp.concatenate([upper, lower], axis=0)
            for x_ref, (its_slot, half) in zip(x_refs, work):
                if its_slot != slot:
                    continue
                own_ref = (mine_ref, other_ref)[half]
                for part in range(8):
                    own = own_ref[part * 128 : (part + 1) * 128, :]
                    lhs = jnp.concatenate([own, own], axis=1)
                    x = jnp.dot(lhs, weights, preferred_element_type=F32).astype(BF16)
                    for k in range(2):
                        j = 2 * pair + k
                        for l in range(4):
                            lane = (part * 4 + l) * 128
                            x_ref[j * 32 : (j + 1) * 32, lane : lane + 128] = x[
                                l * 32 : (l + 1) * 32, k * 128 : (k + 1) * 128
                            ]


def stage1(work, own, tiles, tokens=(), weight=1):
    if all(half == 0 for _, half in work):
        own = own[:1]
    flops = int(len(work) * weight * 2**29)
    return pl.pallas_call(
        functools.partial(stage1_kernel, work, len(tokens)),
        out_shape=tuple(jax.ShapeDtypeStruct((256, 4096), BF16) for _ in work),
        in_specs=[spec(pltpu.VMEM)] * (len(own) + 2) + [spec(pl.ANY)] * len(tokens),
        out_specs=tuple(spec(pltpu.VMEM) for _ in work),
        compiler_params=params(8),
        cost_estimate=pl.CostEstimate(flops=flops, transcendentals=0, bytes_accessed=2**10),
        name="stage1_" + "_".join(str(slot[0]) for slot in dict.fromkeys(slot for slot, _ in work)),
    )(*own, *tiles, *tokens)


def halves(*slots):
    return tuple((slot, half) for slot in slots for half in range(2))


def stage2_kernel(picks, n_b, carried, tokens, *refs):
    n = len(picks)
    x_refs, refs = refs[: 2 * n], refs[2 * n :]
    b_refs, refs = refs[:n_b], refs[n_b:]
    carry, refs = refs[:carried], refs[carried:]
    out_ref, r_s = refs[tokens:]
    y = place()[1]
    for i, halves in enumerate(picks):
        total = None
        for half, (at, index) in enumerate(halves):
            b_ref = b_refs[at] if index is None else b_refs[at].at[index]
            for step in range(16):
                b = b_ref[step * 64 : (step + 1) * 64, :]
                bt = jnp.concatenate([b[0:32], b[32:64]], axis=1)
                x = x_refs[2 * i + half][:, step * 256 : (step + 1) * 256]
                term = lax.dot_general(x, bt, NT, preferred_element_type=F32)
                total = term if total is None else total + term
        r_s[i] = total
    for q in range(4):
        columns = [ref[q ^ y] for ref in carry]
        for i in range(n):
            r = r_s[i]
            columns.append(
                jnp.concatenate([r[j * 32 + q * 8 : j * 32 + q * 8 + 8] for j in range(CLS)], axis=0)
            )
        out_ref[q ^ y] = jnp.concatenate(columns, axis=1) if len(columns) > 1 else columns[0]


def stage2(name, xs, picks, bs, carry=(), tokens=(), weight=1):
    n = len(picks)
    lanes = 32 * n + sum(c.shape[2] for c in carry)
    return pl.pallas_call(
        functools.partial(stage2_kernel, picks, len(bs), len(carry), len(tokens)),
        out_shape=jax.ShapeDtypeStruct((4, 64, lanes), F32),
        in_specs=[spec(pltpu.VMEM)] * (2 * n + len(bs) + len(carry)) + [spec(pl.ANY)] * len(tokens),
        out_specs=spec(pltpu.VMEM),
        scratch_shapes=[pltpu.VMEM((n, 256, 32), F32)],
        compiler_params=params(8),
        cost_estimate=pl.CostEstimate(flops=int(n * weight * 2**30), transcendentals=0, bytes_accessed=2**10),
        name="stage2_" + name,
    )(*xs, *bs, *carry, *tokens)


def finish_kernel(order, own_ref, r1_ref, r2_ref, r3_ref, out_ref, sum_s, pos_s):
    total = own_ref[0] + r1_ref[...] + r2_ref[...] + r3_ref[...]
    sum_s[0] = total[:, 0:128]
    sum_s[1] = total[:, 128:256]
    for a8 in range(8):
        for k in range(2):
            strip = sum_s[k, pl.ds(a8, CLS, stride=8), :]
            for c in range(4):
                rows = pl.ds(pl.multiple_of(on_core(order[k * 4 + c]) * CLS, CLS), CLS)
                pos_s[rows, a8 * 32 : (a8 + 1) * 32] = strip[:, c * 32 : (c + 1) * 32]
    out_ref[...] = pos_s[...].T.reshape(8, 32, ROWS)


def finish(order, parts):
    out = pl.pallas_call(
        functools.partial(finish_kernel, order),
        out_shape=jax.ShapeDtypeStruct((8, 32, ROWS), F32),
        in_specs=[spec(pltpu.VMEM)] * 4,
        out_specs=spec(pltpu.VMEM),
        scratch_shapes=[pltpu.VMEM((2, 64, 128), F32), pltpu.VMEM((ROWS, 256), F32)],
        compiler_params=params(6),
        name="finish",
    )(*parts)
    return jnp.transpose(out, (2, 0, 1))


FAST, SLOW = 0, 8


def shards(cholesky, amplitudes, mirror):
    chunks, outgoing = cut_to_send(cholesky, amplitudes)
    quarters = {k: over_y(chunks[k], k) for k in (2, 1, 3)}
    tiles = twist_tiles(mirror, amplitudes, to_sibling(outgoing))
    mine = order_rows((chunks[0], quarters[2], quarters[1], quarters[3]), tiles[1])
    own = (mine, to_sibling(mine))

    c0, c1, c4, c5 = ((g, g) for g in (0, 1, 4, 5))
    c26, c62, c37, c73 = (2, 6), (6, 2), (3, 7), (7, 3)
    x1a, x1b, z0 = over_x(mine, 1, 3), over_x(mine, 3, 1), over_z(mine)
    x0m, x0o, *xs = stage1(halves(c0, c1, c26, c62, c4), own, tiles)
    (x1a,) = relay((x1a,), (x0o,))
    x2 = over_x(x1a, 3, 1)
    x1, near_blocks = join(x1a, x1b, z0, x0o)
    zx1 = over_z(x1)
    other_blocks = to_sibling(near_blocks)
    x37 = stage1(halves(c37, c73), own, tiles, (x1,), FAST)
    self0 = stage2("self", (x0m, x0o), (((0, None), (1, None)),), own, (), (x37[0],), FAST)
    (x2,) = relay((x2,), (self0,))
    zx2 = over_z(x2)
    x2_other = to_sibling(x2)
    near = stage2(
        "near",
        xs[0:6],
        (((0, 2), (1, 2)), ((0, 0), (1, 1)), ((0, 1), (1, 0))),
        (near_blocks, other_blocks),
        (self0,),
        (x2,),
        SLOW,
    )
    (zx1,) = relay((zx1,), (near,))
    zx1_other = to_sibling(zx1)
    x5 = stage1(halves(c5), own, tiles, (zx1,))
    (zx2,) = relay((zx2,), (x5[0],))
    zx2_other = to_sibling(zx2)
    far = stage2("far", xs[6:8], (((0, None), (1, None)),), (x2, x2_other), (near,), (zx2,))
    last = stage2(
        "last",
        (*x37, *x5),
        (((0, 0), (1, 1)), ((0, 1), (1, 0)), ((2, None), (3, None))),
        (zx1, zx1_other, zx2, zx2_other),
        (far,),
    )
    parts = {k: over_y(last[k], k) for k in (2, 1, 3)}
    return finish((c0, c1, c26, c62, c4, c37, c73, c5), (last, parts[2], parts[1], parts[3]))


def solution(mesh):
    placed = (P(None, "vir", None), P("occ", None, None, None), P("occ"))
    return jax.shard_map(
        shards, mesh=mesh, in_specs=placed, out_specs=P("occ", "vir", None), check_vma=False
    )
```

```python
import functools

import jax
import jax.numpy as jnp
from jax import lax
from jax.experimental import pallas as pl
from jax.experimental.pallas import tpu as pltpu
from jax.sharding import PartitionSpec as P

IRREPS = 8
CLS = 8
ROWS = IRREPS * CLS
NT = (((1,), (1,)), ((), ()))
BF16 = jnp.bfloat16
F32 = jnp.float32
MIB = 2**20


def permute(value, move):
    pairs = []
    for occ in range(4):
        for vir in range(32):
            to_occ, to_vir = move(occ, vir)
            pairs.append((occ * 32 + vir, to_occ * 32 + to_vir))
    return lax.ppermute(value, ("occ", "vir"), pairs)


def over_y(value, k):
    return permute(value, lambda occ, vir: (occ, vir ^ k))


def over_x(value, even, odd):
    return permute(value, lambda occ, vir: (occ, vir ^ (8 * (odd if occ & 1 else even))))


def over_z(value):
    return permute(value, lambda occ, vir: (occ ^ (2 if occ & 1 else 0), vir ^ 4))


def to_sibling(value):
    return permute(value, lambda occ, vir: (occ ^ 1, vir))


def spec(space):
    return pl.BlockSpec(memory_space=space)


def params(mib):
    return pltpu.CompilerParams(vmem_limit_bytes=mib * MIB)


def place():
    vir, core = lax.axis_index("vir"), lax.axis_index("occ") & 1
    return lax.shift_right_logical(vir, 2), vir & 3, core


def send_kernel(chol_ref, amp_ref, *refs):
    chunks, tiles_ref, chunk_sems, tile_sems = refs[:4], refs[4], refs[5], refs[6]
    h, y, core = place()
    copies = []
    for k, out_ref in enumerate(chunks):
        start = pl.multiple_of((y ^ k) * 512 + core * 256, 256)
        copies.append(pltpu.make_async_copy(chol_ref.at[pl.ds(start, 256)], out_ref, chunk_sems.at[k]))
    for g in range(IRREPS):
        source = amp_ref.at[pl.ds(g * CLS, CLS), h ^ g]
        copies.append(pltpu.make_async_copy(source, tiles_ref.at[g], tile_sems.at[g]))
    for copy in copies:
        copy.start()
    for copy in copies:
        copy.wait()


def cut_to_send(cholesky, amplitudes):
    chunk = jax.ShapeDtypeStruct((256, 128), BF16)
    outs = pl.pallas_call(
        send_kernel,
        out_shape=(chunk,) * 4 + (jax.ShapeDtypeStruct((IRREPS, CLS, 128, 128), BF16),),
        in_specs=[spec(pltpu.HBM)] * 2,
        out_specs=(spec(pltpu.VMEM),) * 5,
        scratch_shapes=[pltpu.SemaphoreType.DMA((4,)), pltpu.SemaphoreType.DMA((IRREPS,))],
        compiler_params=params(46),
        name="cut_to_send",
    )(pltpu.with_memory_space_constraint(cholesky.reshape(2048, 128), pltpu.HBM), amplitudes)
    return outs[:4], outs[4]


def twist_kernel(mirror_ref, amp_ref, received_ref, own_ref, out_ref, sems):
    h = place()[0]
    copies = []
    for g in range(IRREPS):
        source = amp_ref.at[pl.ds(g * CLS, CLS), h]
        copies.append(pltpu.make_async_copy(source, own_ref.at[g], sems.at[g]))
        copies[-1].start()
    for g in range(IRREPS):
        for j in range(CLS):
            out_ref[g, j] = received_ref[g, mirror_ref[g * CLS + j] - g * CLS].T
    for copy in copies:
        copy.wait()


def twist_tiles(mirror, amplitudes, received):
    shape = jax.ShapeDtypeStruct((IRREPS, CLS, 128, 128), BF16)
    return pl.pallas_call(
        twist_kernel,
        out_shape=(shape, shape),
        in_specs=[spec(pltpu.SMEM), spec(pltpu.HBM), spec(pltpu.VMEM)],
        out_specs=(spec(pltpu.VMEM), spec(pltpu.VMEM)),
        scratch_shapes=[pltpu.SemaphoreType.DMA((IRREPS,))],
        compiler_params=params(46),
        name="twist_tiles",
    )(mirror, amplitudes, received)


def rows_kernel(r0_ref, r2_ref, r1_ref, r3_ref, _, out_ref, all_ref):
    y = place()[1]
    for k, ref in enumerate((r0_ref, r1_ref, r2_ref, r3_ref)):
        all_ref[k ^ y] = ref[...]

    def step(i, _):
        start = pl.multiple_of(i * 16, 16)
        parts = [all_ref[q, pl.ds(start, 16), :].astype(F32) for q in range(4)]
        both = [p[0:8] for p in parts] + [p[8:16] for p in parts]
        out_ref[pl.ds(pl.multiple_of(i * 64, 64), 64), :] = jnp.concatenate(both, axis=0).astype(BF16)
        return 0

    lax.fori_loop(0, 16, step, 0, unroll=8)


def order_rows(quarters, token):
    return pl.pallas_call(
        rows_kernel,
        out_shape=jax.ShapeDtypeStruct((1024, 128), BF16),
        in_specs=[spec(pltpu.VMEM)] * 4 + [spec(pl.ANY)],
        out_specs=spec(pltpu.VMEM),
        scratch_shapes=[pltpu.VMEM((4, 256, 128), BF16)],
        compiler_params=params(6),
        name="order_rows",
    )(*quarters, token)


def relay(values, tokens, weight=0):
    n = len(values)
    outs = pl.pallas_call(
        lambda *refs: None,
        out_shape=tuple(jax.ShapeDtypeStruct(v.shape, v.dtype) for v in values),
        in_specs=[spec(pl.ANY)] * (n + len(tokens)),
        out_specs=tuple(spec(pl.ANY) for _ in values),
        input_output_aliases={i: i for i in range(n)},
        compiler_params=params(1),
        cost_estimate=pl.CostEstimate(flops=int(weight * 2**30), transcendentals=0, bytes_accessed=0),
        name="relay",
    )(*values, *tokens)
    return outs


def join_kernel(first_ref, second_ref, third_ref, _, pair_ref, all_ref):
    for i, ref in enumerate((first_ref, second_ref)):
        pair_ref[i] = ref[...]
        all_ref[i] = ref[...]
    all_ref[2] = third_ref[...]


def join(first, second, third, token):
    return pl.pallas_call(
        join_kernel,
        out_shape=tuple(jax.ShapeDtypeStruct((n, *first.shape), first.dtype) for n in (2, 3)),
        in_specs=[spec(pltpu.VMEM)] * 3 + [spec(pl.ANY)],
        out_specs=(spec(pltpu.VMEM), spec(pltpu.VMEM)),
        compiler_params=params(4),
        cost_estimate=pl.CostEstimate(flops=0, transcendentals=0, bytes_accessed=0),
        name="join",
    )(first, second, third, token)


def on_core(pair):
    return pair[0] if pair[0] == pair[1] else jnp.where(place()[2] == 1, pair[1], pair[0])


def stage1_kernel(work, tokens, mine_ref, *refs):
    both = any(half == 1 for _, half in work)
    other_ref, refs = (refs[0], refs[1:]) if both else (None, refs)
    t_ref, tp_ref, x_refs = refs[0], refs[1], refs[2 + tokens :]
    for slot in dict.fromkeys(slot for slot, _ in work):
        g = on_core(slot)
        for pair in range(4):
            j0, j1 = 2 * pair, 2 * pair + 1
            upper = jnp.concatenate([t_ref[g, j0], t_ref[g, j1]], axis=1)
            lower = jnp.concatenate([tp_ref[g, j0], tp_ref[g, j1]], axis=1)
            weights = jnp.concatenate([upper, lower], axis=0)
            for x_ref, (its_slot, half) in zip(x_refs, work):
                if its_slot != slot:
                    continue
                own_ref = (mine_ref, other_ref)[half]
                for part in range(8):
                    own = own_ref[part * 128 : (part + 1) * 128, :]
                    lhs = jnp.concatenate([own, own], axis=1)
                    x = jnp.dot(lhs, weights, preferred_element_type=F32).astype(BF16)
                    for k in range(2):
                        j = 2 * pair + k
                        for l in range(4):
                            lane = (part * 4 + l) * 128
                            x_ref[j * 32 : (j + 1) * 32, lane : lane + 128] = x[
                                l * 32 : (l + 1) * 32, k * 128 : (k + 1) * 128
                            ]


def stage1(work, own, tiles, tokens=(), weight=1):
    if all(half == 0 for _, half in work):
        own = own[:1]
    flops = int(len(work) * weight * 2**29)
    return pl.pallas_call(
        functools.partial(stage1_kernel, work, len(tokens)),
        out_shape=tuple(jax.ShapeDtypeStruct((256, 4096), BF16) for _ in work),
        in_specs=[spec(pltpu.VMEM)] * (len(own) + 2) + [spec(pl.ANY)] * len(tokens),
        out_specs=tuple(spec(pltpu.VMEM) for _ in work),
        compiler_params=params(8),
        cost_estimate=pl.CostEstimate(flops=flops, transcendentals=0, bytes_accessed=2**10),
        name="stage1_" + "_".join(str(slot[0]) for slot in dict.fromkeys(slot for slot, _ in work)),
    )(*own, *tiles, *tokens)


def halves(*slots):
    return tuple((slot, half) for slot in slots for half in range(2))


def stage2_kernel(picks, n_b, carried, tokens, *refs):
    n = len(picks)
    x_refs, refs = refs[: 2 * n], refs[2 * n :]
    b_refs, refs = refs[:n_b], refs[n_b:]
    carry, refs = refs[:carried], refs[carried:]
    out_ref, r_s = refs[tokens:]
    y = place()[1]
    for i, halves in enumerate(picks):
        total = None
        for half, (at, index) in enumerate(halves):
            b_ref = b_refs[at] if index is None else b_refs[at].at[index]
            for step in range(16):
                b = b_ref[step * 64 : (step + 1) * 64, :]
                bt = jnp.concatenate([b[0:32], b[32:64]], axis=1)
                x = x_refs[2 * i + half][:, step * 256 : (step + 1) * 256]
                term = lax.dot_general(x, bt, NT, preferred_element_type=F32)
                total = term if total is None else total + term
        r_s[i] = total
    for q in range(4):
        columns = [ref[q ^ y] for ref in carry]
        for i in range(n):
            r = r_s[i]
            columns.append(
                jnp.concatenate([r[j * 32 + q * 8 : j * 32 + q * 8 + 8] for j in range(CLS)], axis=0)
            )
        out_ref[q ^ y] = jnp.concatenate(columns, axis=1) if len(columns) > 1 else columns[0]


def stage2(name, xs, picks, bs, carry=(), tokens=(), weight=1):
    n = len(picks)
    lanes = 32 * n + sum(c.shape[2] for c in carry)
    return pl.pallas_call(
        functools.partial(stage2_kernel, picks, len(bs), len(carry), len(tokens)),
        out_shape=jax.ShapeDtypeStruct((4, 64, lanes), F32),
        in_specs=[spec(pltpu.VMEM)] * (2 * n + len(bs) + len(carry)) + [spec(pl.ANY)] * len(tokens),
        out_specs=spec(pltpu.VMEM),
        scratch_shapes=[pltpu.VMEM((n, 256, 32), F32)],
        compiler_params=params(8),
        cost_estimate=pl.CostEstimate(flops=int(n * weight * 2**30), transcendentals=0, bytes_accessed=2**10),
        name="stage2_" + name,
    )(*xs, *bs, *carry, *tokens)


def finish_kernel(order, own_ref, r1_ref, r2_ref, r3_ref, out_ref, sum_s, pos_s):
    total = own_ref[0] + r1_ref[...] + r2_ref[...] + r3_ref[...]
    sum_s[0] = total[:, 0:128]
    sum_s[1] = total[:, 128:256]
    for a8 in range(8):
        for k in range(2):
            strip = sum_s[k, pl.ds(a8, CLS, stride=8), :]
            for c in range(4):
                rows = pl.ds(pl.multiple_of(on_core(order[k * 4 + c]) * CLS, CLS), CLS)
                pos_s[rows, a8 * 32 : (a8 + 1) * 32] = strip[:, c * 32 : (c + 1) * 32]
    out_ref[...] = pos_s[...].T.reshape(8, 32, ROWS)


def finish(order, parts):
    out = pl.pallas_call(
        functools.partial(finish_kernel, order),
        out_shape=jax.ShapeDtypeStruct((8, 32, ROWS), F32),
        in_specs=[spec(pltpu.VMEM)] * 4,
        out_specs=spec(pltpu.VMEM),
        scratch_shapes=[pltpu.VMEM((2, 64, 128), F32), pltpu.VMEM((ROWS, 256), F32)],
        compiler_params=params(6),
        name="finish",
    )(*parts)
    return jnp.transpose(out, (2, 0, 1))


FAST, SLOW, HOLD = 0, 8, 16


def shards(cholesky, amplitudes, mirror):
    chunks, outgoing = cut_to_send(cholesky, amplitudes)
    quarters = {k: over_y(chunks[k], k) for k in (2, 1, 3)}
    tiles = twist_tiles(mirror, amplitudes, to_sibling(outgoing))
    mine = order_rows((chunks[0], quarters[2], quarters[1], quarters[3]), tiles[1])
    own = (mine, to_sibling(mine))

    c0, c1, c4, c5 = ((g, g) for g in (0, 1, 4, 5))
    c26, c62, c37, c73 = (2, 6), (6, 2), (3, 7), (7, 3)
    x1a, x1b, z0 = over_x(mine, 1, 3), over_x(mine, 3, 1), over_z(mine)
    x0m, x0o, *xs = stage1(halves(c0, c1, c26, c62, c4), own, tiles)
    (x1a,) = relay((x1a,), (x0o,))
    x2 = over_x(x1a, 3, 1)
    x1, near_blocks = join(x1a, x1b, z0, x0o)
    zx1 = over_z(x1)
    other_blocks = to_sibling(near_blocks)
    x37 = stage1(halves(c37, c73), own, tiles, (x1,), FAST)
    self0 = stage2("self", (x0m, x0o), (((0, None), (1, None)),), own, (), (x37[0],), FAST)
    (x2,) = relay((x2,), (self0,), HOLD)
    zx2 = over_z(x2)
    x2_other = to_sibling(x2)
    near = stage2(
        "near",
        xs[0:6],
        (((0, 2), (1, 2)), ((0, 0), (1, 1)), ((0, 1), (1, 0))),
        (near_blocks, other_blocks),
        (self0,),
        (x2,),
        SLOW,
    )
    (zx1,) = relay((zx1,), (near,))
    zx1_other = to_sibling(zx1)
    x5 = stage1(halves(c5), own, tiles, (zx1,))
    (zx2,) = relay((zx2,), (x5[0],))
    zx2_other = to_sibling(zx2)
    far = stage2("far", xs[6:8], (((0, None), (1, None)),), (x2, x2_other), (near,), (zx2,))
    last = stage2(
        "last",
        (*x37, *x5),
        (((0, 0), (1, 1)), ((0, 1), (1, 0)), ((2, None), (3, None))),
        (zx1, zx1_other, zx2, zx2_other),
        (far,),
    )
    parts = {k: over_y(last[k], k) for k in (2, 1, 3)}
    return finish((c0, c1, c26, c62, c4, c37, c73, c5), (last, parts[2], parts[1], parts[3]))


def solution(mesh):
    placed = (P(None, "vir", None), P("occ", None, None, None), P("occ"))
    return jax.shard_map(
        shards, mesh=mesh, in_specs=placed, out_specs=P("occ", "vir", None), check_vma=False
    )
```

```python
import functools

import jax
import jax.numpy as jnp
from jax import lax
from jax.experimental import pallas as pl
from jax.experimental.pallas import tpu as pltpu
from jax.sharding import PartitionSpec as P

IRREPS = 8
CLS = 8
ROWS = IRREPS * CLS
NT = (((1,), (1,)), ((), ()))
BF16 = jnp.bfloat16
F32 = jnp.float32
MIB = 2**20


def permute(value, move):
    pairs = []
    for occ in range(4):
        for vir in range(32):
            to_occ, to_vir = move(occ, vir)
            pairs.append((occ * 32 + vir, to_occ * 32 + to_vir))
    return lax.ppermute(value, ("occ", "vir"), pairs)


def over_y(value, k):
    return permute(value, lambda occ, vir: (occ, vir ^ k))


def over_x(value, even, odd):
    return permute(value, lambda occ, vir: (occ, vir ^ (8 * (odd if occ & 1 else even))))


def over_z(value):
    return permute(value, lambda occ, vir: (occ ^ (2 if occ & 1 else 0), vir ^ 4))


def to_sibling(value):
    return permute(value, lambda occ, vir: (occ ^ 1, vir))


def spec(space):
    return pl.BlockSpec(memory_space=space)


def params(mib):
    return pltpu.CompilerParams(vmem_limit_bytes=mib * MIB)


def place():
    vir, core = lax.axis_index("vir"), lax.axis_index("occ") & 1
    return lax.shift_right_logical(vir, 2), vir & 3, core


def send_kernel(chol_ref, amp_ref, *refs):
    chunks, tiles_ref, chunk_sems, tile_sems = refs[:4], refs[4], refs[5], refs[6]
    h, y, core = place()
    copies = []
    for k, out_ref in enumerate(chunks):
        start = pl.multiple_of((y ^ k) * 512 + core * 256, 256)
        copies.append(pltpu.make_async_copy(chol_ref.at[pl.ds(start, 256)], out_ref, chunk_sems.at[k]))
    for g in range(IRREPS):
        source = amp_ref.at[pl.ds(g * CLS, CLS), h ^ g]
        copies.append(pltpu.make_async_copy(source, tiles_ref.at[g], tile_sems.at[g]))
    for copy in copies:
        copy.start()
    for copy in copies:
        copy.wait()


def cut_to_send(cholesky, amplitudes):
    chunk = jax.ShapeDtypeStruct((256, 128), BF16)
    outs = pl.pallas_call(
        send_kernel,
        out_shape=(chunk,) * 4 + (jax.ShapeDtypeStruct((IRREPS, CLS, 128, 128), BF16),),
        in_specs=[spec(pltpu.HBM)] * 2,
        out_specs=(spec(pltpu.VMEM),) * 5,
        scratch_shapes=[pltpu.SemaphoreType.DMA((4,)), pltpu.SemaphoreType.DMA((IRREPS,))],
        compiler_params=params(46),
        name="cut_to_send",
    )(pltpu.with_memory_space_constraint(cholesky.reshape(2048, 128), pltpu.HBM), amplitudes)
    return outs[:4], outs[4]


def twist_kernel(mirror_ref, amp_ref, received_ref, own_ref, out_ref, sems):
    h = place()[0]
    copies = []
    for g in range(IRREPS):
        source = amp_ref.at[pl.ds(g * CLS, CLS), h]
        copies.append(pltpu.make_async_copy(source, own_ref.at[g], sems.at[g]))
        copies[-1].start()
    for g in range(IRREPS):
        for j in range(CLS):
            out_ref[g, j] = received_ref[g, mirror_ref[g * CLS + j] - g * CLS].T
    for copy in copies:
        copy.wait()


def twist_tiles(mirror, amplitudes, received):
    shape = jax.ShapeDtypeStruct((IRREPS, CLS, 128, 128), BF16)
    return pl.pallas_call(
        twist_kernel,
        out_shape=(shape, shape),
        in_specs=[spec(pltpu.SMEM), spec(pltpu.HBM), spec(pltpu.VMEM)],
        out_specs=(spec(pltpu.VMEM), spec(pltpu.VMEM)),
        scratch_shapes=[pltpu.SemaphoreType.DMA((IRREPS,))],
        compiler_params=params(46),
        name="twist_tiles",
    )(mirror, amplitudes, received)


def rows_kernel(r0_ref, r2_ref, r1_ref, r3_ref, _, out_ref, all_ref):
    y = place()[1]
    for k, ref in enumerate((r0_ref, r1_ref, r2_ref, r3_ref)):
        all_ref[k ^ y] = ref[...]

    def step(i, _):
        start = pl.multiple_of(i * 16, 16)
        parts = [all_ref[q, pl.ds(start, 16), :].astype(F32) for q in range(4)]
        both = [p[0:8] for p in parts] + [p[8:16] for p in parts]
        out_ref[pl.ds(pl.multiple_of(i * 64, 64), 64), :] = jnp.concatenate(both, axis=0).astype(BF16)
        return 0

    lax.fori_loop(0, 16, step, 0, unroll=8)


def order_rows(quarters, token):
    return pl.pallas_call(
        rows_kernel,
        out_shape=jax.ShapeDtypeStruct((1024, 128), BF16),
        in_specs=[spec(pltpu.VMEM)] * 4 + [spec(pl.ANY)],
        out_specs=spec(pltpu.VMEM),
        scratch_shapes=[pltpu.VMEM((4, 256, 128), BF16)],
        compiler_params=params(6),
        name="order_rows",
    )(*quarters, token)


def relay(values, tokens, weight=0):
    n = len(values)
    outs = pl.pallas_call(
        lambda *refs: None,
        out_shape=tuple(jax.ShapeDtypeStruct(v.shape, v.dtype) for v in values),
        in_specs=[spec(pl.ANY)] * (n + len(tokens)),
        out_specs=tuple(spec(pl.ANY) for _ in values),
        input_output_aliases={i: i for i in range(n)},
        compiler_params=params(1),
        cost_estimate=pl.CostEstimate(flops=int(weight * 2**30), transcendentals=0, bytes_accessed=0),
        name="relay",
    )(*values, *tokens)
    return outs


def join_kernel(*refs):
    for i, ref in enumerate(refs[:-2]):
        refs[-1][i] = ref[...]


def join(values, token):
    n = len(values)
    return pl.pallas_call(
        join_kernel,
        out_shape=jax.ShapeDtypeStruct((n, *values[0].shape), values[0].dtype),
        in_specs=[spec(pltpu.VMEM)] * n + [spec(pl.ANY)],
        out_specs=spec(pltpu.VMEM),
        compiler_params=params(4),
        cost_estimate=pl.CostEstimate(flops=0, transcendentals=0, bytes_accessed=0),
        name="join",
    )(*values, token)


def on_core(pair):
    return pair[0] if pair[0] == pair[1] else jnp.where(place()[2] == 1, pair[1], pair[0])


def stage1_kernel(work, tokens, mine_ref, *refs):
    both = any(half == 1 for _, half in work)
    other_ref, refs = (refs[0], refs[1:]) if both else (None, refs)
    t_ref, tp_ref, x_refs = refs[0], refs[1], refs[2 + tokens :]
    for slot in dict.fromkeys(slot for slot, _ in work):
        g = on_core(slot)
        for pair in range(4):
            j0, j1 = 2 * pair, 2 * pair + 1
            upper = jnp.concatenate([t_ref[g, j0], t_ref[g, j1]], axis=1)
            lower = jnp.concatenate([tp_ref[g, j0], tp_ref[g, j1]], axis=1)
            weights = jnp.concatenate([upper, lower], axis=0)
            for x_ref, (its_slot, half) in zip(x_refs, work):
                if its_slot != slot:
                    continue
                own_ref = (mine_ref, other_ref)[half]
                for part in range(8):
                    own = own_ref[part * 128 : (part + 1) * 128, :]
                    lhs = jnp.concatenate([own, own], axis=1)
                    x = jnp.dot(lhs, weights, preferred_element_type=F32).astype(BF16)
                    for k in range(2):
                        j = 2 * pair + k
                        for l in range(4):
                            lane = (part * 4 + l) * 128
                            x_ref[j * 32 : (j + 1) * 32, lane : lane + 128] = x[
                                l * 32 : (l + 1) * 32, k * 128 : (k + 1) * 128
                            ]


def stage1(work, own, tiles, tokens=(), weight=1):
    if all(half == 0 for _, half in work):
        own = own[:1]
    flops = int(len(work) * weight * 2**29)
    return pl.pallas_call(
        functools.partial(stage1_kernel, work, len(tokens)),
        out_shape=tuple(jax.ShapeDtypeStruct((256, 4096), BF16) for _ in work),
        in_specs=[spec(pltpu.VMEM)] * (len(own) + 2) + [spec(pl.ANY)] * len(tokens),
        out_specs=tuple(spec(pltpu.VMEM) for _ in work),
        compiler_params=params(8),
        cost_estimate=pl.CostEstimate(flops=flops, transcendentals=0, bytes_accessed=2**10),
        name="stage1_" + "_".join(str(slot[0]) for slot in dict.fromkeys(slot for slot, _ in work)),
    )(*own, *tiles, *tokens)


def halves(*slots):
    return tuple((slot, half) for slot in slots for half in range(2))


def stage2_kernel(picks, n_b, carried, tokens, *refs):
    n = len(picks)
    x_refs, refs = refs[: 2 * n], refs[2 * n :]
    b_refs, refs = refs[:n_b], refs[n_b:]
    carry, refs = refs[:carried], refs[carried:]
    out_ref, r_s = refs[tokens:]
    y = place()[1]
    for i, halves in enumerate(picks):
        total = None
        for half, (at, index) in enumerate(halves):
            b_ref = b_refs[at] if index is None else b_refs[at].at[index]
            for step in range(16):
                b = b_ref[step * 64 : (step + 1) * 64, :]
                bt = jnp.concatenate([b[0:32], b[32:64]], axis=1)
                x = x_refs[2 * i + half][:, step * 256 : (step + 1) * 256]
                term = lax.dot_general(x, bt, NT, preferred_element_type=F32)
                total = term if total is None else total + term
        r_s[i] = total
    for q in range(4):
        columns = [ref[q ^ y] for ref in carry]
        for i in range(n):
            r = r_s[i]
            columns.append(
                jnp.concatenate([r[j * 32 + q * 8 : j * 32 + q * 8 + 8] for j in range(CLS)], axis=0)
            )
        out_ref[q ^ y] = jnp.concatenate(columns, axis=1) if len(columns) > 1 else columns[0]


def stage2(name, xs, picks, bs, carry=(), tokens=(), weight=1):
    n = len(picks)
    lanes = 32 * n + sum(c.shape[2] for c in carry)
    return pl.pallas_call(
        functools.partial(stage2_kernel, picks, len(bs), len(carry), len(tokens)),
        out_shape=jax.ShapeDtypeStruct((4, 64, lanes), F32),
        in_specs=[spec(pltpu.VMEM)] * (2 * n + len(bs) + len(carry)) + [spec(pl.ANY)] * len(tokens),
        out_specs=spec(pltpu.VMEM),
        scratch_shapes=[pltpu.VMEM((n, 256, 32), F32)],
        compiler_params=params(8),
        cost_estimate=pl.CostEstimate(flops=int(n * weight * 2**30), transcendentals=0, bytes_accessed=2**10),
        name="stage2_" + name,
    )(*xs, *bs, *carry, *tokens)


def finish_kernel(order, own_ref, r1_ref, r2_ref, r3_ref, out_ref, sum_s, pos_s):
    total = own_ref[0] + r1_ref[...] + r2_ref[...] + r3_ref[...]
    sum_s[0] = total[:, 0:128]
    sum_s[1] = total[:, 128:256]
    for a8 in range(8):
        for k in range(2):
            strip = sum_s[k, pl.ds(a8, CLS, stride=8), :]
            for c in range(4):
                rows = pl.ds(pl.multiple_of(on_core(order[k * 4 + c]) * CLS, CLS), CLS)
                pos_s[rows, a8 * 32 : (a8 + 1) * 32] = strip[:, c * 32 : (c + 1) * 32]
    out_ref[...] = pos_s[...].T.reshape(8, 32, ROWS)


def finish(order, parts):
    out = pl.pallas_call(
        functools.partial(finish_kernel, order),
        out_shape=jax.ShapeDtypeStruct((8, 32, ROWS), F32),
        in_specs=[spec(pltpu.VMEM)] * 4,
        out_specs=spec(pltpu.VMEM),
        scratch_shapes=[pltpu.VMEM((2, 64, 128), F32), pltpu.VMEM((ROWS, 256), F32)],
        compiler_params=params(6),
        name="finish",
    )(*parts)
    return jnp.transpose(out, (2, 0, 1))


FAST, SLOW, HOLD = 0, 8, 16


def shards(cholesky, amplitudes, mirror):
    chunks, outgoing = cut_to_send(cholesky, amplitudes)
    quarters = {k: over_y(chunks[k], k) for k in (2, 1, 3)}
    tiles = twist_tiles(mirror, amplitudes, to_sibling(outgoing))
    mine = order_rows((chunks[0], quarters[2], quarters[1], quarters[3]), tiles[1])
    own = (mine, to_sibling(mine))

    c0, c1, c4, c5 = ((g, g) for g in (0, 1, 4, 5))
    c26, c62, c37, c73 = (2, 6), (6, 2), (3, 7), (7, 3)
    x1a, z0 = over_x(mine, 1, 3), over_z(mine)
    x0m, x0o = stage1(halves(c0), own, tiles)
    again = join((mine,), x0o)
    x1b = over_x(again, 3, 1).reshape(1024, 128)
    xs = stage1(halves(c1, c26, c62, c4), own, tiles, (again,))
    (x1a,) = relay((x1a,), (xs[2],))
    x2 = over_x(x1a, 3, 1)
    x1 = join((x1a, x1b), xs[2])
    near_blocks = join((x1a, x1b, z0), xs[2])
    zx1 = over_z(x1)
    other_blocks = to_sibling(near_blocks)
    x37 = stage1(halves(c37, c73), own, tiles, (x1,), FAST)
    self0 = stage2("self", (x0m, x0o), (((0, None), (1, None)),), own, (), (x37[0],), FAST)
    (x2,) = relay((x2,), (self0,), HOLD)
    zx2 = over_z(x2)
    x2_other = to_sibling(x2)
    near = stage2(
        "near",
        xs[0:6],
        (((0, 2), (1, 2)), ((0, 0), (1, 1)), ((0, 1), (1, 0))),
        (near_blocks, other_blocks),
        (self0,),
        (x2,),
        SLOW,
    )
    (zx1,) = relay((zx1,), (near,))
    zx1_other = to_sibling(zx1)
    x5 = stage1(halves(c5), own, tiles, (zx1,))
    (zx2,) = relay((zx2,), (x5[0],))
    zx2_other = to_sibling(zx2)
    far = stage2("far", xs[6:8], (((0, None), (1, None)),), (x2, x2_other), (near,), (zx2,))
    last = stage2(
        "last",
        (*x37, *x5),
        (((0, 0), (1, 1)), ((0, 1), (1, 0)), ((2, None), (3, None))),
        (zx1, zx1_other, zx2, zx2_other),
        (far,),
    )
    parts = {k: over_y(last[k], k) for k in (2, 1, 3)}
    return finish((c0, c1, c26, c62, c4, c37, c73, c5), (last, parts[2], parts[1], parts[3]))


def solution(mesh):
    placed = (P(None, "vir", None), P("occ", None, None, None), P("occ"))
    return jax.shard_map(
        shards, mesh=mesh, in_specs=placed, out_specs=P("occ", "vir", None), check_vma=False
    )
```

```python
import functools

import jax
import jax.numpy as jnp
from jax import lax
from jax.experimental import pallas as pl
from jax.experimental.pallas import tpu as pltpu
from jax.sharding import PartitionSpec as P

IRREPS = 8
CLS = 8
ROWS = IRREPS * CLS
NT = (((1,), (1,)), ((), ()))
BF16 = jnp.bfloat16
F32 = jnp.float32
MIB = 2**20


def permute(value, move):
    pairs = []
    for occ in range(4):
        for vir in range(32):
            to_occ, to_vir = move(occ, vir)
            pairs.append((occ * 32 + vir, to_occ * 32 + to_vir))
    return lax.ppermute(value, ("occ", "vir"), pairs)


def over_y(value, k):
    return permute(value, lambda occ, vir: (occ, vir ^ k))


def over_x(value, even, odd):
    return permute(value, lambda occ, vir: (occ, vir ^ (8 * (odd if occ & 1 else even))))


def over_z(value):
    return permute(value, lambda occ, vir: (occ ^ (2 if occ & 1 else 0), vir ^ 4))


def to_sibling(value):
    return permute(value, lambda occ, vir: (occ ^ 1, vir))


def spec(space):
    return pl.BlockSpec(memory_space=space)


def params(mib):
    return pltpu.CompilerParams(vmem_limit_bytes=mib * MIB)


def place():
    vir, core = lax.axis_index("vir"), lax.axis_index("occ") & 1
    return lax.shift_right_logical(vir, 2), vir & 3, core


def send_kernel(chol_ref, amp_ref, *refs):
    chunks, tiles_ref, chunk_sems, tile_sems = refs[:4], refs[4], refs[5], refs[6]
    h, y, core = place()
    copies = []
    for k, out_ref in enumerate(chunks):
        start = pl.multiple_of((y ^ k) * 512 + core * 256, 256)
        copies.append(pltpu.make_async_copy(chol_ref.at[pl.ds(start, 256)], out_ref, chunk_sems.at[k]))
    for g in range(IRREPS):
        source = amp_ref.at[pl.ds(g * CLS, CLS), h ^ g]
        copies.append(pltpu.make_async_copy(source, tiles_ref.at[g], tile_sems.at[g]))
    for copy in copies:
        copy.start()
    for copy in copies:
        copy.wait()


def cut_to_send(cholesky, amplitudes):
    chunk = jax.ShapeDtypeStruct((256, 128), BF16)
    outs = pl.pallas_call(
        send_kernel,
        out_shape=(chunk,) * 4 + (jax.ShapeDtypeStruct((IRREPS, CLS, 128, 128), BF16),),
        in_specs=[spec(pltpu.HBM)] * 2,
        out_specs=(spec(pltpu.VMEM),) * 5,
        scratch_shapes=[pltpu.SemaphoreType.DMA((4,)), pltpu.SemaphoreType.DMA((IRREPS,))],
        compiler_params=params(46),
        name="cut_to_send",
    )(pltpu.with_memory_space_constraint(cholesky.reshape(2048, 128), pltpu.HBM), amplitudes)
    return outs[:4], outs[4]


def twist_kernel(mirror_ref, amp_ref, received_ref, own_ref, out_ref, sems):
    h = place()[0]
    copies = []
    for g in range(IRREPS):
        source = amp_ref.at[pl.ds(g * CLS, CLS), h]
        copies.append(pltpu.make_async_copy(source, own_ref.at[g], sems.at[g]))
        copies[-1].start()
    for g in range(IRREPS):
        for j in range(CLS):
            out_ref[g, j] = received_ref[g, mirror_ref[g * CLS + j] - g * CLS].T
    for copy in copies:
        copy.wait()


def twist_tiles(mirror, amplitudes, received):
    shape = jax.ShapeDtypeStruct((IRREPS, CLS, 128, 128), BF16)
    return pl.pallas_call(
        twist_kernel,
        out_shape=(shape, shape),
        in_specs=[spec(pltpu.SMEM), spec(pltpu.HBM), spec(pltpu.VMEM)],
        out_specs=(spec(pltpu.VMEM), spec(pltpu.VMEM)),
        scratch_shapes=[pltpu.SemaphoreType.DMA((IRREPS,))],
        compiler_params=params(46),
        name="twist_tiles",
    )(mirror, amplitudes, received)


def rows_kernel(r0_ref, r2_ref, r1_ref, r3_ref, _, out_ref, all_ref):
    y = place()[1]
    for k, ref in enumerate((r0_ref, r1_ref, r2_ref, r3_ref)):
        all_ref[k ^ y] = ref[...]

    def step(i, _):
        start = pl.multiple_of(i * 16, 16)
        parts = [all_ref[q, pl.ds(start, 16), :].astype(F32) for q in range(4)]
        both = [p[0:8] for p in parts] + [p[8:16] for p in parts]
        out_ref[pl.ds(pl.multiple_of(i * 64, 64), 64), :] = jnp.concatenate(both, axis=0).astype(BF16)
        return 0

    lax.fori_loop(0, 16, step, 0, unroll=8)


def order_rows(quarters, token):
    return pl.pallas_call(
        rows_kernel,
        out_shape=jax.ShapeDtypeStruct((1024, 128), BF16),
        in_specs=[spec(pltpu.VMEM)] * 4 + [spec(pl.ANY)],
        out_specs=spec(pltpu.VMEM),
        scratch_shapes=[pltpu.VMEM((4, 256, 128), BF16)],
        compiler_params=params(6),
        name="order_rows",
    )(*quarters, token)


def relay(values, tokens, weight=0):
    n = len(values)
    outs = pl.pallas_call(
        lambda *refs: None,
        out_shape=tuple(jax.ShapeDtypeStruct(v.shape, v.dtype) for v in values),
        in_specs=[spec(pl.ANY)] * (n + len(tokens)),
        out_specs=tuple(spec(pl.ANY) for _ in values),
        input_output_aliases={i: i for i in range(n)},
        compiler_params=params(1),
        cost_estimate=pl.CostEstimate(flops=int(weight * 2**30), transcendentals=0, bytes_accessed=0),
        name="relay",
    )(*values, *tokens)
    return outs


def join_kernel(first_ref, second_ref, third_ref, _, pair_ref, all_ref):
    for i, ref in enumerate((first_ref, second_ref)):
        pair_ref[i] = ref[...]
        all_ref[i] = ref[...]
    all_ref[2] = third_ref[...]


def join(first, second, third, token):
    return pl.pallas_call(
        join_kernel,
        out_shape=tuple(jax.ShapeDtypeStruct((n, *first.shape), first.dtype) for n in (2, 3)),
        in_specs=[spec(pltpu.VMEM)] * 3 + [spec(pl.ANY)],
        out_specs=(spec(pltpu.VMEM), spec(pltpu.VMEM)),
        compiler_params=params(4),
        cost_estimate=pl.CostEstimate(flops=0, transcendentals=0, bytes_accessed=0),
        name="join",
    )(first, second, third, token)


def on_core(pair):
    return pair[0] if pair[0] == pair[1] else jnp.where(place()[2] == 1, pair[1], pair[0])


def stage1_kernel(work, tokens, mine_ref, *refs):
    both = any(half == 1 for _, half in work)
    other_ref, refs = (refs[0], refs[1:]) if both else (None, refs)
    t_ref, tp_ref, x_refs = refs[0], refs[1], refs[2 + tokens :]
    for slot in dict.fromkeys(slot for slot, _ in work):
        g = on_core(slot)
        for pair in range(4):
            j0, j1 = 2 * pair, 2 * pair + 1
            upper = jnp.concatenate([t_ref[g, j0], t_ref[g, j1]], axis=1)
            lower = jnp.concatenate([tp_ref[g, j0], tp_ref[g, j1]], axis=1)
            weights = jnp.concatenate([upper, lower], axis=0)
            for x_ref, (its_slot, half) in zip(x_refs, work):
                if its_slot != slot:
                    continue
                own_ref = (mine_ref, other_ref)[half]
                for part in range(8):
                    own = own_ref[part * 128 : (part + 1) * 128, :]
                    lhs = jnp.concatenate([own, own], axis=1)
                    x = jnp.dot(lhs, weights, preferred_element_type=F32).astype(BF16)
                    for k in range(2):
                        j = 2 * pair + k
                        for l in range(4):
                            lane = (part * 4 + l) * 128
                            x_ref[j * 32 : (j + 1) * 32, lane : lane + 128] = x[
                                l * 32 : (l + 1) * 32, k * 128 : (k + 1) * 128
                            ]


def stage1(work, own, tiles, tokens=(), weight=1):
    if all(half == 0 for _, half in work):
        own = own[:1]
    flops = int(len(work) * weight * 2**29)
    return pl.pallas_call(
        functools.partial(stage1_kernel, work, len(tokens)),
        out_shape=tuple(jax.ShapeDtypeStruct((256, 4096), BF16) for _ in work),
        in_specs=[spec(pltpu.VMEM)] * (len(own) + 2) + [spec(pl.ANY)] * len(tokens),
        out_specs=tuple(spec(pltpu.VMEM) for _ in work),
        compiler_params=params(8),
        cost_estimate=pl.CostEstimate(flops=flops, transcendentals=0, bytes_accessed=2**10),
        name="stage1_" + "_".join(str(slot[0]) for slot in dict.fromkeys(slot for slot, _ in work)),
    )(*own, *tiles, *tokens)


def halves(*slots):
    return tuple((slot, half) for slot in slots for half in range(2))


def stage2_kernel(picks, n_b, carried, tokens, *refs):
    n = len(picks)
    x_refs, refs = refs[: 2 * n], refs[2 * n :]
    b_refs, refs = refs[:n_b], refs[n_b:]
    carry, refs = refs[:carried], refs[carried:]
    out_ref, r_s = refs[tokens:]
    y = place()[1]
    for i, halves in enumerate(picks):
        total = None
        for half, (at, index) in enumerate(halves):
            b_ref = b_refs[at] if index is None else b_refs[at].at[index]
            for step in range(16):
                b = b_ref[step * 64 : (step + 1) * 64, :]
                bt = jnp.concatenate([b[0:32], b[32:64]], axis=1)
                x = x_refs[2 * i + half][:, step * 256 : (step + 1) * 256]
                term = lax.dot_general(x, bt, NT, preferred_element_type=F32)
                total = term if total is None else total + term
        r_s[i] = total
    for q in range(4):
        columns = [ref[q ^ y] for ref in carry]
        for i in range(n):
            r = r_s[i]
            columns.append(
                jnp.concatenate([r[j * 32 + q * 8 : j * 32 + q * 8 + 8] for j in range(CLS)], axis=0)
            )
        out_ref[q ^ y] = jnp.concatenate(columns, axis=1) if len(columns) > 1 else columns[0]


def stage2(name, xs, picks, bs, carry=(), tokens=(), weight=1):
    n = len(picks)
    lanes = 32 * n + sum(c.shape[2] for c in carry)
    return pl.pallas_call(
        functools.partial(stage2_kernel, picks, len(bs), len(carry), len(tokens)),
        out_shape=jax.ShapeDtypeStruct((4, 64, lanes), F32),
        in_specs=[spec(pltpu.VMEM)] * (2 * n + len(bs) + len(carry)) + [spec(pl.ANY)] * len(tokens),
        out_specs=spec(pltpu.VMEM),
        scratch_shapes=[pltpu.VMEM((n, 256, 32), F32)],
        compiler_params=params(8),
        cost_estimate=pl.CostEstimate(flops=int(n * weight * 2**30), transcendentals=0, bytes_accessed=2**10),
        name="stage2_" + name,
    )(*xs, *bs, *carry, *tokens)


def mixed_kernel(work, *refs):
    own, tiles, xs, refs = refs[:2], refs[2:4], refs[4:6], refs[7:]
    stage1_kernel(work, 0, *own, *tiles, *refs[: len(work)])
    stage2_kernel((((0, None), (1, None)),), 2, 0, 0, *xs, *own, *refs[len(work) :])


def mixed(work, own, tiles, xs, token):
    outs = pl.pallas_call(
        functools.partial(mixed_kernel, work),
        out_shape=tuple(jax.ShapeDtypeStruct((256, 4096), BF16) for _ in work)
        + (jax.ShapeDtypeStruct((4, 64, 32), F32),),
        in_specs=[spec(pltpu.VMEM)] * 6 + [spec(pl.ANY)],
        out_specs=tuple(spec(pltpu.VMEM) for _ in range(len(work) + 1)),
        scratch_shapes=[pltpu.VMEM((1, 256, 32), F32)],
        compiler_params=params(8),
        cost_estimate=pl.CostEstimate(flops=0, transcendentals=0, bytes_accessed=2**10),
        name="mixed",
    )(*own, *tiles, *xs, token)
    return outs[:-1], outs[-1]


def finish_kernel(order, own_ref, r1_ref, r2_ref, r3_ref, out_ref, sum_s, pos_s):
    total = own_ref[0] + r1_ref[...] + r2_ref[...] + r3_ref[...]
    sum_s[0] = total[:, 0:128]
    sum_s[1] = total[:, 128:256]
    for a8 in range(8):
        for k in range(2):
            strip = sum_s[k, pl.ds(a8, CLS, stride=8), :]
            for c in range(4):
                rows = pl.ds(pl.multiple_of(on_core(order[k * 4 + c]) * CLS, CLS), CLS)
                pos_s[rows, a8 * 32 : (a8 + 1) * 32] = strip[:, c * 32 : (c + 1) * 32]
    out_ref[...] = pos_s[...].T.reshape(8, 32, ROWS)


def finish(order, parts):
    out = pl.pallas_call(
        functools.partial(finish_kernel, order),
        out_shape=jax.ShapeDtypeStruct((8, 32, ROWS), F32),
        in_specs=[spec(pltpu.VMEM)] * 4,
        out_specs=spec(pltpu.VMEM),
        scratch_shapes=[pltpu.VMEM((2, 64, 128), F32), pltpu.VMEM((ROWS, 256), F32)],
        compiler_params=params(6),
        name="finish",
    )(*parts)
    return jnp.transpose(out, (2, 0, 1))


FAST, SLOW, HOLD = 0, 8, 16


def shards(cholesky, amplitudes, mirror):
    chunks, outgoing = cut_to_send(cholesky, amplitudes)
    quarters = {k: over_y(chunks[k], k) for k in (2, 1, 3)}
    tiles = twist_tiles(mirror, amplitudes, to_sibling(outgoing))
    mine = order_rows((chunks[0], quarters[2], quarters[1], quarters[3]), tiles[1])
    own = (mine, to_sibling(mine))

    c0, c1, c4, c5 = ((g, g) for g in (0, 1, 4, 5))
    c26, c62, c37, c73 = (2, 6), (6, 2), (3, 7), (7, 3)
    x1a, x1b, z0 = over_x(mine, 1, 3), over_x(mine, 3, 1), over_z(mine)
    x0m, x0o, *xs = stage1(halves(c0, c1, c26, c62, c4), own, tiles)
    (x1a,) = relay((x1a,), (x0o,))
    x2 = over_x(x1a, 3, 1)
    x1, near_blocks = join(x1a, x1b, z0, x0o)
    zx1 = over_z(x1)
    other_blocks = to_sibling(near_blocks)
    x37, self0 = mixed(halves(c37, c73), own, tiles, (x0m, x0o), x1)
    (x2,) = relay((x2,), (self0,), HOLD)
    zx2 = over_z(x2)
    x2_other = to_sibling(x2)
    near = stage2(
        "near",
        xs[0:6],
        (((0, 2), (1, 2)), ((0, 0), (1, 1)), ((0, 1), (1, 0))),
        (near_blocks, other_blocks),
        (self0,),
        (x2,),
        SLOW,
    )
    (zx1,) = relay((zx1,), (near,))
    zx1_other = to_sibling(zx1)
    x5 = stage1(halves(c5), own, tiles, (zx1,))
    (zx2,) = relay((zx2,), (x5[0],))
    zx2_other = to_sibling(zx2)
    far = stage2("far", xs[6:8], (((0, None), (1, None)),), (x2, x2_other), (near,), (zx2,))
    last = stage2(
        "last",
        (*x37, *x5),
        (((0, 0), (1, 1)), ((0, 1), (1, 0)), ((2, None), (3, None))),
        (zx1, zx1_other, zx2, zx2_other),
        (far,),
    )
    parts = {k: over_y(last[k], k) for k in (2, 1, 3)}
    return finish((c0, c1, c26, c62, c4, c37, c73, c5), (last, parts[2], parts[1], parts[3]))


def solution(mesh):
    placed = (P(None, "vir", None), P("occ", None, None, None), P("occ"))
    return jax.shard_map(
        shards, mesh=mesh, in_specs=placed, out_specs=P("occ", "vir", None), check_vma=False
    )
```

```python
import functools

import jax
import jax.numpy as jnp
from jax import lax
from jax.experimental import pallas as pl
from jax.experimental.pallas import tpu as pltpu
from jax.sharding import PartitionSpec as P

IRREPS = 8
CLS = 8
ROWS = IRREPS * CLS
NT = (((1,), (1,)), ((), ()))
BF16 = jnp.bfloat16
F32 = jnp.float32
MIB = 2**20


def permute(value, move):
    pairs = []
    for occ in range(4):
        for vir in range(32):
            to_occ, to_vir = move(occ, vir)
            pairs.append((occ * 32 + vir, to_occ * 32 + to_vir))
    return lax.ppermute(value, ("occ", "vir"), pairs)


def over_y(value, k):
    return permute(value, lambda occ, vir: (occ, vir ^ k))


def over_x(value, even, odd):
    return permute(value, lambda occ, vir: (occ, vir ^ (8 * (odd if occ & 1 else even))))


def over_z(value):
    return permute(value, lambda occ, vir: (occ ^ (2 if occ & 1 else 0), vir ^ 4))


def to_sibling(value):
    return permute(value, lambda occ, vir: (occ ^ 1, vir))


def spec(space):
    return pl.BlockSpec(memory_space=space)


def params(mib):
    return pltpu.CompilerParams(vmem_limit_bytes=mib * MIB)


def place():
    vir, core = lax.axis_index("vir"), lax.axis_index("occ") & 1
    return lax.shift_right_logical(vir, 2), vir & 3, core


def send_kernel(chol_ref, amp_ref, *refs):
    chunks, tiles_ref, chunk_sems, tile_sems = refs[:4], refs[4], refs[5], refs[6]
    h, y, core = place()
    copies = []
    for k, out_ref in enumerate(chunks):
        start = pl.multiple_of((y ^ k) * 512 + core * 256, 256)
        copies.append(pltpu.make_async_copy(chol_ref.at[pl.ds(start, 256)], out_ref, chunk_sems.at[k]))
    for g in range(IRREPS):
        source = amp_ref.at[pl.ds(g * CLS, CLS), h ^ g]
        copies.append(pltpu.make_async_copy(source, tiles_ref.at[g], tile_sems.at[g]))
    for copy in copies:
        copy.start()
    for copy in copies:
        copy.wait()


def cut_to_send(cholesky, amplitudes):
    chunk = jax.ShapeDtypeStruct((256, 128), BF16)
    outs = pl.pallas_call(
        send_kernel,
        out_shape=(chunk,) * 4 + (jax.ShapeDtypeStruct((IRREPS, CLS, 128, 128), BF16),),
        in_specs=[spec(pltpu.HBM)] * 2,
        out_specs=(spec(pltpu.VMEM),) * 5,
        scratch_shapes=[pltpu.SemaphoreType.DMA((4,)), pltpu.SemaphoreType.DMA((IRREPS,))],
        compiler_params=params(46),
        name="cut_to_send",
    )(pltpu.with_memory_space_constraint(cholesky.reshape(2048, 128), pltpu.HBM), amplitudes)
    return outs[:4], outs[4]


def twist_kernel(mirror_ref, amp_ref, received_ref, own_ref, out_ref, sems):
    h = place()[0]
    copies = []
    for g in range(IRREPS):
        source = amp_ref.at[pl.ds(g * CLS, CLS), h]
        copies.append(pltpu.make_async_copy(source, own_ref.at[g], sems.at[g]))
        copies[-1].start()
    for g in range(IRREPS):
        for j in range(CLS):
            out_ref[g, j] = received_ref[g, mirror_ref[g * CLS + j] - g * CLS].T
    for copy in copies:
        copy.wait()


def twist_tiles(mirror, amplitudes, received):
    shape = jax.ShapeDtypeStruct((IRREPS, CLS, 128, 128), BF16)
    return pl.pallas_call(
        twist_kernel,
        out_shape=(shape, shape),
        in_specs=[spec(pltpu.SMEM), spec(pltpu.HBM), spec(pltpu.VMEM)],
        out_specs=(spec(pltpu.VMEM), spec(pltpu.VMEM)),
        scratch_shapes=[pltpu.SemaphoreType.DMA((IRREPS,))],
        compiler_params=params(46),
        name="twist_tiles",
    )(mirror, amplitudes, received)


def rows_kernel(r0_ref, r2_ref, r1_ref, r3_ref, _, out_ref, all_ref):
    y = place()[1]
    for k, ref in enumerate((r0_ref, r1_ref, r2_ref, r3_ref)):
        all_ref[k ^ y] = ref[...]

    def step(i, _):
        start = pl.multiple_of(i * 16, 16)
        parts = [all_ref[q, pl.ds(start, 16), :].astype(F32) for q in range(4)]
        both = [p[0:8] for p in parts] + [p[8:16] for p in parts]
        out_ref[pl.ds(pl.multiple_of(i * 64, 64), 64), :] = jnp.concatenate(both, axis=0).astype(BF16)
        return 0

    lax.fori_loop(0, 16, step, 0, unroll=8)


def order_rows(quarters, token):
    return pl.pallas_call(
        rows_kernel,
        out_shape=jax.ShapeDtypeStruct((1024, 128), BF16),
        in_specs=[spec(pltpu.VMEM)] * 4 + [spec(pl.ANY)],
        out_specs=spec(pltpu.VMEM),
        scratch_shapes=[pltpu.VMEM((4, 256, 128), BF16)],
        compiler_params=params(6),
        name="order_rows",
    )(*quarters, token)


def relay(values, tokens, weight=0):
    n = len(values)
    outs = pl.pallas_call(
        lambda *refs: None,
        out_shape=tuple(jax.ShapeDtypeStruct(v.shape, v.dtype) for v in values),
        in_specs=[spec(pl.ANY)] * (n + len(tokens)),
        out_specs=tuple(spec(pl.ANY) for _ in values),
        input_output_aliases={i: i for i in range(n)},
        compiler_params=params(1),
        cost_estimate=pl.CostEstimate(flops=int(weight * 2**30), transcendentals=0, bytes_accessed=0),
        name="relay",
    )(*values, *tokens)
    return outs


def join_kernel(*refs):
    for i, ref in enumerate(refs[:-2]):
        refs[-1][i] = ref[...]


def join(values, token):
    n = len(values)
    return pl.pallas_call(
        join_kernel,
        out_shape=jax.ShapeDtypeStruct((n, *values[0].shape), values[0].dtype),
        in_specs=[spec(pltpu.VMEM)] * n + [spec(pl.ANY)],
        out_specs=spec(pltpu.VMEM),
        compiler_params=params(4),
        cost_estimate=pl.CostEstimate(flops=0, transcendentals=0, bytes_accessed=0),
        name="join",
    )(*values, token)


def on_core(pair):
    return pair[0] if pair[0] == pair[1] else jnp.where(place()[2] == 1, pair[1], pair[0])


def stage1_kernel(work, tokens, mine_ref, *refs):
    both = any(half == 1 for _, half in work)
    other_ref, refs = (refs[0], refs[1:]) if both else (None, refs)
    t_ref, tp_ref, x_refs = refs[0], refs[1], refs[2 + tokens :]
    for slot in dict.fromkeys(slot for slot, _ in work):
        g = on_core(slot)
        for pair in range(4):
            j0, j1 = 2 * pair, 2 * pair + 1
            upper = jnp.concatenate([t_ref[g, j0], t_ref[g, j1]], axis=1)
            lower = jnp.concatenate([tp_ref[g, j0], tp_ref[g, j1]], axis=1)
            weights = jnp.concatenate([upper, lower], axis=0)
            for x_ref, (its_slot, half) in zip(x_refs, work):
                if its_slot != slot:
                    continue
                own_ref = (mine_ref, other_ref)[half]
                for part in range(8):
                    own = own_ref[part * 128 : (part + 1) * 128, :]
                    lhs = jnp.concatenate([own, own], axis=1)
                    x = jnp.dot(lhs, weights, preferred_element_type=F32).astype(BF16)
                    for k in range(2):
                        j = 2 * pair + k
                        for l in range(4):
                            lane = (part * 4 + l) * 128
                            x_ref[j * 32 : (j + 1) * 32, lane : lane + 128] = x[
                                l * 32 : (l + 1) * 32, k * 128 : (k + 1) * 128
                            ]


def stage1(work, own, tiles, tokens=(), weight=1):
    if all(half == 0 for _, half in work):
        own = own[:1]
    flops = int(len(work) * weight * 2**29)
    return pl.pallas_call(
        functools.partial(stage1_kernel, work, len(tokens)),
        out_shape=tuple(jax.ShapeDtypeStruct((256, 4096), BF16) for _ in work),
        in_specs=[spec(pltpu.VMEM)] * (len(own) + 2) + [spec(pl.ANY)] * len(tokens),
        out_specs=tuple(spec(pltpu.VMEM) for _ in work),
        compiler_params=params(8),
        cost_estimate=pl.CostEstimate(flops=flops, transcendentals=0, bytes_accessed=2**10),
        name="stage1_" + "_".join(str(slot[0]) for slot in dict.fromkeys(slot for slot, _ in work)),
    )(*own, *tiles, *tokens)


def halves(*slots):
    return tuple((slot, half) for slot in slots for half in range(2))


def stage2_kernel(picks, n_b, carried, tokens, *refs):
    n = len(picks)
    x_refs, refs = refs[: 2 * n], refs[2 * n :]
    b_refs, refs = refs[:n_b], refs[n_b:]
    carry, refs = refs[:carried], refs[carried:]
    out_ref, r_s = refs[tokens:]
    y = place()[1]
    for i, halves in enumerate(picks):
        total = None
        for half, (at, index) in enumerate(halves):
            b_ref = b_refs[at] if index is None else b_refs[at].at[index]
            for step in range(16):
                b = b_ref[step * 64 : (step + 1) * 64, :]
                bt = jnp.concatenate([b[0:32], b[32:64]], axis=1)
                x = x_refs[2 * i + half][:, step * 256 : (step + 1) * 256]
                term = lax.dot_general(x, bt, NT, preferred_element_type=F32)
                total = term if total is None else total + term
        r_s[i] = total
    for q in range(4):
        columns = [ref[q ^ y] for ref in carry]
        for i in range(n):
            r = r_s[i]
            columns.append(
                jnp.concatenate([r[j * 32 + q * 8 : j * 32 + q * 8 + 8] for j in range(CLS)], axis=0)
            )
        out_ref[q ^ y] = jnp.concatenate(columns, axis=1) if len(columns) > 1 else columns[0]


def stage2(name, xs, picks, bs, carry=(), tokens=(), weight=1):
    n = len(picks)
    lanes = 32 * n + sum(c.shape[2] for c in carry)
    return pl.pallas_call(
        functools.partial(stage2_kernel, picks, len(bs), len(carry), len(tokens)),
        out_shape=jax.ShapeDtypeStruct((4, 64, lanes), F32),
        in_specs=[spec(pltpu.VMEM)] * (2 * n + len(bs) + len(carry)) + [spec(pl.ANY)] * len(tokens),
        out_specs=spec(pltpu.VMEM),
        scratch_shapes=[pltpu.VMEM((n, 256, 32), F32)],
        compiler_params=params(8),
        cost_estimate=pl.CostEstimate(flops=int(n * weight * 2**30), transcendentals=0, bytes_accessed=2**10),
        name="stage2_" + name,
    )(*xs, *bs, *carry, *tokens)


def mixed_kernel(work, *refs):
    own, tiles, xs, refs = refs[:2], refs[2:4], refs[4:6], refs[7:]
    stage1_kernel(work, 0, *own, *tiles, *refs[: len(work)])
    stage2_kernel((((0, None), (1, None)),), 2, 0, 0, *xs, *own, *refs[len(work) :])


def mixed(work, own, tiles, xs, token):
    outs = pl.pallas_call(
        functools.partial(mixed_kernel, work),
        out_shape=tuple(jax.ShapeDtypeStruct((256, 4096), BF16) for _ in work)
        + (jax.ShapeDtypeStruct((4, 64, 32), F32),),
        in_specs=[spec(pltpu.VMEM)] * 6 + [spec(pl.ANY)],
        out_specs=tuple(spec(pltpu.VMEM) for _ in range(len(work) + 1)),
        scratch_shapes=[pltpu.VMEM((1, 256, 32), F32)],
        compiler_params=params(8),
        cost_estimate=pl.CostEstimate(flops=0, transcendentals=0, bytes_accessed=2**10),
        name="mixed",
    )(*own, *tiles, *xs, token)
    return outs[:-1], outs[-1]


def finish_kernel(order, own_ref, r1_ref, r2_ref, r3_ref, out_ref, sum_s, pos_s):
    total = own_ref[0] + r1_ref[...] + r2_ref[...] + r3_ref[...]
    sum_s[0] = total[:, 0:128]
    sum_s[1] = total[:, 128:256]
    for a8 in range(8):
        for k in range(2):
            strip = sum_s[k, pl.ds(a8, CLS, stride=8), :]
            for c in range(4):
                rows = pl.ds(pl.multiple_of(on_core(order[k * 4 + c]) * CLS, CLS), CLS)
                pos_s[rows, a8 * 32 : (a8 + 1) * 32] = strip[:, c * 32 : (c + 1) * 32]
    out_ref[...] = pos_s[...].T.reshape(8, 32, ROWS)


def finish(order, parts):
    out = pl.pallas_call(
        functools.partial(finish_kernel, order),
        out_shape=jax.ShapeDtypeStruct((8, 32, ROWS), F32),
        in_specs=[spec(pltpu.VMEM)] * 4,
        out_specs=spec(pltpu.VMEM),
        scratch_shapes=[pltpu.VMEM((2, 64, 128), F32), pltpu.VMEM((ROWS, 256), F32)],
        compiler_params=params(6),
        name="finish",
    )(*parts)
    return jnp.transpose(out, (2, 0, 1))


FAST, SLOW, HOLD = 0, 8, 16


def shards(cholesky, amplitudes, mirror):
    chunks, outgoing = cut_to_send(cholesky, amplitudes)
    quarters = {k: over_y(chunks[k], k) for k in (2, 1, 3)}
    tiles = twist_tiles(mirror, amplitudes, to_sibling(outgoing))
    mine = order_rows((chunks[0], quarters[2], quarters[1], quarters[3]), tiles[1])
    own = (mine, to_sibling(mine))

    c0, c1, c4, c5 = ((g, g) for g in (0, 1, 4, 5))
    c26, c62, c37, c73 = (2, 6), (6, 2), (3, 7), (7, 3)
    x1a, z0 = over_x(mine, 1, 3), over_z(mine)
    x0m, x0o = stage1(halves(c0), own, tiles)
    again = join((mine,), x0o)
    x1b = over_x(again, 3, 1).reshape(1024, 128)
    xs = stage1(halves(c1, c26, c62, c4), own, tiles, (again,))
    (x1a,) = relay((x1a,), (xs[2],))
    x2 = over_x(x1a, 3, 1)
    x1 = join((x1a, x1b), xs[2])
    near_blocks = join((x1a, x1b, z0), xs[2])
    zx1 = over_z(x1)
    other_blocks = to_sibling(near_blocks)
    x37, self0 = mixed(halves(c37, c73), own, tiles, (x0m, x0o), x1)
    (x2,) = relay((x2,), (self0,), HOLD)
    zx2 = over_z(x2)
    x2_other = to_sibling(x2)
    near = stage2(
        "near",
        xs[0:6],
        (((0, 2), (1, 2)), ((0, 0), (1, 1)), ((0, 1), (1, 0))),
        (near_blocks, other_blocks),
        (self0,),
        (x2,),
        SLOW,
    )
    (zx1,) = relay((zx1,), (near,))
    zx1_other = to_sibling(zx1)
    x5 = stage1(halves(c5), own, tiles, (zx1,))
    (zx2,) = relay((zx2,), (x5[0],))
    zx2_other = to_sibling(zx2)
    far = stage2("far", xs[6:8], (((0, None), (1, None)),), (x2, x2_other), (near,), (zx2,))
    last = stage2(
        "last",
        (*x37, *x5),
        (((0, 0), (1, 1)), ((0, 1), (1, 0)), ((2, None), (3, None))),
        (zx1, zx1_other, zx2, zx2_other),
        (far,),
    )
    parts = {k: over_y(last[k], k) for k in (2, 1, 3)}
    return finish((c0, c1, c26, c62, c4, c37, c73, c5), (last, parts[2], parts[1], parts[3]))


def solution(mesh):
    placed = (P(None, "vir", None), P("occ", None, None, None), P("occ"))
    return jax.shard_map(
        shards, mesh=mesh, in_specs=placed, out_specs=P("occ", "vir", None), check_vma=False
    )
```
